128 devices in a mesh: seq: 16 (over x, z), head: 8 (over y, core).
Axes of the slice: x: 4, y: 4, z: 4, core: 2. Of those that a mesh axis runs over, the one named last changes fastest.
Arguments:
- conv_input: bfloat16 [16384, 8, 1280], P(('seq', 'head')), may hold values from -6 to 6
- gate_input: bfloat16 [16384, 8192], P(('seq', 'head')), may hold values from -40 to 40
- step_size: bfloat16 [16384, 128], P(('seq', 'head')), may hold values from 0.0015 to 0.18
- decay_log: bfloat16 [16384, 128], P(('seq', 'head')), may hold values from -0.6 to 0
- conv_weight: float32 [4, 8, 1280], P(None, 'head'), may hold values from -3 to 3
- conv_bias: float32 [8, 1280], P('head'), may hold values from -3 to 3
- skip_gain: float32 [128], replicated, may hold values from 0.5 to 1.5
- norm_gain: float32 [8192], replicated, may hold values from 0.5 to 1.5
- seg_length: int32 [16], P('seq'), may hold values from 64 to 1024, as said below
- seg_first: int32 [16], P('seq'), may hold values from 0 to 1, as said below
Outputs:
- normed: bfloat16 [16384, 8192], P(('seq', 'head'))
The draws below stay inside these ranges and needn't reach their ends.
Inputs may be any that keep to these rules, and one draw needn't show every extreme that they name: The first seg_length[s] slots of segment s hold tokens, the rest are padding; in every draw one segment is full (1024). 1 where segment s begins a new request, 0 where it continues the request of segment s - 1; seg_first[0] = 1 and seg_first[15] = 0.
All inputs are finite; a program needn't handle non-finite values.
Results may differ from the reference program's by a relative error of at most 0.012.
Values may be sent and summed in bfloat16 or wider, within the bound.
No kernel may reach another device: no remote copies, remote signals or barrier semaphores. Data moves between devices by JAX's collectives and lax.ppermute only.
A program may use at most 128 MiB of HBM per device.

```python
import math
import jax
import jax.numpy as jnp
from jax import lax

SCAN_CHANNELS = 128
HEAD_DIM = 64
STATE = 128
GROUPS = 8
KERNEL = 4
BLOCK = 256
SEG = 1024
SEGMENTS = 16
PLACE_CAPACITY = 16384
INNER = 8192
GROUP_WIDTH = 1280


def head_rates(key, fast_share):
    key = jax.random.fold_in(key, 5)
    child_seeds = jax.random.split(key, 3)
    is_fast = jax.random.uniform(child_seeds[0], (SCAN_CHANNELS,)) < fast_share
    fast_rate = jax.random.uniform(child_seeds[1], (SCAN_CHANNELS,), minval=1.0 / 50.0, maxval=1.0 / 30.0)
    slow_rate = jnp.exp(jax.random.uniform(child_seeds[2], (SCAN_CHANNELS,), minval=math.log(2e-05), maxval=math.log(0.003)))
    return jnp.where(is_fast, fast_rate, slow_rate)


def draw_gate_input(key, part):
    key = jax.random.fold_in(key, 23)
    stochastic_child_seeds = jax.random.split(key, 3)
    baseline = jnp.clip(jax.random.normal(stochastic_child_seeds[0], (PLACE_CAPACITY, INNER)), -4.0, 4.0)
    log_high = 1.15
    row_scale = jnp.exp(jax.random.uniform(stochastic_child_seeds[1], (PLACE_CAPACITY, 1), minval=-log_high, maxval=log_high))
    col_scale = jnp.exp(jax.random.uniform(stochastic_child_seeds[2], (1, INNER), minval=-log_high, maxval=log_high))
    return (baseline * row_scale * col_scale).astype(jnp.bfloat16)


def draw_step_size(key, part):
    fast_share = 0.5
    rates = head_rates(key, fast_share)
    key = jax.random.fold_in(key, 41)
    tok_factor = jnp.exp(jax.random.uniform(key, (PLACE_CAPACITY, SCAN_CHANNELS), minval=-0.5, maxval=0.5))
    base_step = 0.1 * jnp.sqrt(rates / 0.03)
    return (base_step[None, :] * tok_factor).astype(jnp.bfloat16)


def draw_decay_log(key, part):
    fast_share = 0.5
    rates = head_rates(key, fast_share)
    key = jax.random.fold_in(key, 11)
    stochastic_child_seeds = jax.random.split(key, 4)
    seg_factor = jnp.exp(jax.random.uniform(stochastic_child_seeds[0], (SEGMENTS, SCAN_CHANNELS), minval=-0.7, maxval=0.7))
    tok_factor = jnp.exp(jax.random.uniform(stochastic_child_seeds[1], (PLACE_CAPACITY, SCAN_CHANNELS), minval=-0.7, maxval=0.7))
    forgetting_speeds = rates[None, :] * jnp.repeat(seg_factor, SEG, axis=0) * tok_factor
    spike_position = jax.random.randint(stochastic_child_seeds[2], (3,), 0, PLACE_CAPACITY)
    spike_detected = jnp.any(jnp.arange(PLACE_CAPACITY)[:, None] == spike_position[None, :], axis=1)
    spike_ledger = jnp.log(jax.random.uniform(stochastic_child_seeds[3], (PLACE_CAPACITY, SCAN_CHANNELS), minval=0.55, maxval=0.8))
    return jnp.where(spike_detected[:, None], spike_ledger, -forgetting_speeds).astype(jnp.bfloat16)


def draw_seg_length(key, part):
    key = jax.random.fold_in(key, 31)
    stochastic_child_seeds = jax.random.split(key, 2)
    lowest = max(KERNEL - 1, SEG // 16)
    lengths = jax.random.randint(stochastic_child_seeds[0], (SEGMENTS,), lowest, SEG // 2 + 1)
    full_index = jax.random.randint(stochastic_child_seeds[1], (), 0, SEGMENTS)
    return jnp.where(jnp.arange(SEGMENTS) == full_index, SEG, lengths).astype(jnp.int32)


def draw_seg_first(key, part):
    key = jax.random.fold_in(key, 37)
    new_flags = (jax.random.randint(key, (SEGMENTS,), 0, 4) == 0).astype(jnp.int32)
    positions = jnp.arange(SEGMENTS)
    flags = jnp.where(positions == SEGMENTS - 1, 0, new_flags)
    return jnp.where(positions == 0, 1, flags).astype(jnp.int32)


def block_levels(stream_key, extent, shards, smallest, largest):
    def one(axis_at, shards_of):
        draws = jax.random.uniform(jax.random.fold_in(jax.random.fold_in(stream_key, 6), axis_at), (shards_of,), jnp.float32, smallest / len(shards), largest / len(shards))
        return jnp.repeat(jnp.exp(draws), extent[axis_at] // shards_of).reshape((-1,) + (1,) * (len(extent) - axis_at - 1))

    loudness = one(*shards[0])
    for cut in shards[1:]:
        loudness = loudness * one(*cut)
    return loudness


def normal_values(own_key, shape, scale, limit, cuts=(), dtype=jnp.bfloat16):
    loudness = block_levels(own_key, shape, cuts, -0.22, 0.18) if cuts else 1.0
    array = jax.random.normal(own_key, shape, jnp.float32) * scale * loudness
    return jnp.minimum(jnp.maximum(array, -limit), limit).astype(dtype)


def setup_inputs(seed: int = 0) -> dict:
    seeds = jax.random.split(jax.random.key(seed), 11)
    conv_input = normal_values(seeds[0], (PLACE_CAPACITY, GROUPS, GROUP_WIDTH), 1.0, 6.0, ((0, 128),))
    gate_input = draw_gate_input(jax.random.fold_in(seeds[10], 71), 0)
    step_size = draw_step_size(jax.random.fold_in(seeds[10], 71), 0)
    decay_log = draw_decay_log(jax.random.fold_in(seeds[10], 71), 0)
    conv_weight = normal_values(seeds[4], (KERNEL, GROUPS, GROUP_WIDTH), KERNEL ** -0.5, 3.0, ((1, 8),), jnp.float32)
    conv_bias = normal_values(seeds[5], (GROUPS, GROUP_WIDTH), 0.5, 3.0, ((0, 8),), jnp.float32)
    skip_gain = jnp.clip(jax.random.uniform(seeds[6], (SCAN_CHANNELS,), jnp.float32, 0.5, 1.5), 0.5, 1.5)
    norm_gain = jnp.clip(1.0 + 0.1 * jax.random.normal(seeds[7], (INNER,), jnp.float32), 0.5, 1.5)
    seg_length = draw_seg_length(jax.random.fold_in(seeds[10], 71), 0)
    seg_first = draw_seg_first(jax.random.fold_in(seeds[10], 71), 0)
    return {"conv_input": conv_input, "gate_input": gate_input, "step_size": step_size, "decay_log": decay_log, "conv_weight": conv_weight, "conv_bias": conv_bias, "skip_gain": skip_gain, "norm_gain": norm_gain, "seg_length": seg_length, "seg_first": seg_first}


EPSILON = 1e-05

def block_terms(state_pair, x_heads, b_rows, c_rows, log_rate, input_gain):
    h_prev, offset = state_pair
    block_len = log_rate.shape[0]
    head_count = log_rate.shape[1]
    groups = b_rows.shape[1]
    per_group = head_count // groups
    head_dim = x_heads.shape[2]
    state_dim = b_rows.shape[2]
    running = jnp.cumsum(log_rate, axis=0)
    running_t = running.T
    spread = running_t[:, :, None] - running_t[:, None, :]
    causal = (jnp.arange(block_len)[:, None] >= jnp.arange(block_len)[None, :])[None]
    decay_mat = jnp.where(causal, jnp.exp(jnp.where(causal, spread, 0.0)), 0.0)
    scores = jnp.einsum('tgn,ugn->gtu', c_rows.astype(jnp.float32), b_rows.astype(jnp.float32))
    weights = scores[:, None] * decay_mat.reshape(groups, per_group, block_len, block_len) * input_gain.T.reshape(groups, per_group, 1, block_len)
    weights = weights.astype(jnp.bfloat16).reshape(head_count, block_len, block_len)
    y_in = jnp.einsum('htu,uhp->thp', weights.astype(jnp.float32), x_heads.astype(jnp.float32))
    state_four = h_prev.reshape(groups, per_group, head_dim, state_dim)
    readout = jnp.einsum('tgn,gkpn->tgkp', c_rows.astype(jnp.float32), state_four, precision=lax.Precision.HIGHEST)
    y_off = jnp.exp(running)[:, :, None] * readout.reshape(block_len, head_count, head_dim)
    final_log = running[-1]
    to_final = jnp.exp(final_log[None, :] - running)
    weighted = ((to_final * input_gain)[:, :, None] * x_heads.astype(jnp.float32)).astype(jnp.bfloat16)
    update = jnp.einsum('ugkp,ugn->gkpn', weighted.astype(jnp.float32).reshape(block_len, groups, per_group, head_dim), b_rows.astype(jnp.float32))
    h_next = jnp.exp(final_log)[:, None, None] * h_prev + update.reshape(head_count, head_dim, state_dim)
    return ((h_next, offset + final_log), (y_in + y_off, offset[None, :] + running))

def gate_norm(values, gates, gains):
    gated = values.astype(jnp.float32) * jax.nn.silu(gates.astype(jnp.float32))
    mean_square = lax.optimization_barrier(jnp.mean(gated * gated, axis=-1, keepdims=True))
    return gated * lax.rsqrt(mean_square + EPSILON) * gains[None]

def reference(conv_input, gate_input, step_size, decay_log, conv_weight, conv_bias, skip_gain, norm_gain, seg_length, seg_first):
    per_group = SCAN_CHANNELS // GROUPS
    xwidth = per_group * HEAD_DIM
    nblocks = SEG // BLOCK
    segments_in = conv_input.reshape(SEGMENTS, SEG, GROUPS, GROUP_WIDTH)

    def take_tail(segment, length):
        return lax.dynamic_slice_in_dim(segment, (length - (KERNEL - 1)).astype(jnp.int32), KERNEL - 1, 0)
    tail_rows = jax.vmap(take_tail)(segments_in, seg_length)
    keep_flag = (1 - seg_first).astype(jnp.float32)
    previous = jnp.concatenate([jnp.zeros_like(tail_rows[:1]), tail_rows[:-1]], axis=0)
    previous = previous * keep_flag[:, None, None, None].astype(jnp.bfloat16)

    def one_segment(carried, inputs):
        segment, tail_here, gate_rows, step_rows, decay_rows, length, keep_one = inputs
        padded = jnp.concatenate([tail_here, segment], axis=0)
        mixed = conv_bias[None]
        for tap_index in range(KERNEL):
            mixed = mixed + conv_weight[tap_index][None] * padded[tap_index:tap_index + SEG].astype(jnp.float32)
        activated = jax.nn.silu(mixed).astype(jnp.bfloat16)
        x_heads = activated[:, :, :xwidth].reshape(SEG, SCAN_CHANNELS, HEAD_DIM)
        b_rows = activated[:, :, xwidth:xwidth + STATE]
        c_rows = activated[:, :, xwidth + STATE:]
        is_live = jnp.arange(SEG) < length
        log_rate = jnp.where(is_live[:, None], decay_rows.astype(jnp.float32), 0.0)
        input_gain = jnp.where(is_live[:, None], step_rows.astype(jnp.float32), 0.0)
        operands = (x_heads, b_rows, c_rows, log_rate, input_gain)
        blocked = tuple((operand.reshape((nblocks, BLOCK) + operand.shape[1:]) for operand in operands))
        start_state = (jnp.zeros((SCAN_CHANNELS, HEAD_DIM, STATE), jnp.float32), jnp.zeros((SCAN_CHANNELS,), jnp.float32))
        (local_state, total_log), (y_local, running) = lax.scan(lambda state_pair, block_data: block_terms(state_pair, *block_data), start_state, blocked)
        y_local = y_local.reshape(SEG, SCAN_CHANNELS, HEAD_DIM)
        running = running.reshape(SEG, SCAN_CHANNELS)
        incoming = keep_one * carried
        readout = jnp.einsum('tgn,gkpn->tgkp', c_rows.astype(jnp.float32), incoming.reshape(GROUPS, per_group, HEAD_DIM, STATE), precision=lax.Precision.HIGHEST)
        readout = readout.reshape(SEG, SCAN_CHANNELS, HEAD_DIM)
        output_y = (y_local + jnp.exp(running)[:, :, None] * readout + skip_gain[None, :, None] * x_heads.astype(jnp.float32)).astype(jnp.bfloat16)
        result = gate_norm(output_y.reshape(SEG, GROUPS, xwidth), gate_rows.reshape(SEG, GROUPS, xwidth), norm_gain.reshape(GROUPS, xwidth))
        result = jnp.where(is_live[:, None], result.reshape(SEG, INNER), 0.0).astype(jnp.bfloat16)
        final_state = jnp.exp(total_log)[:, None, None] * incoming + local_state
        return (final_state, result)
    inputs = (segments_in, previous, gate_input.reshape(SEGMENTS, SEG, INNER), step_size.reshape(SEGMENTS, SEG, SCAN_CHANNELS), decay_log.reshape(SEGMENTS, SEG, SCAN_CHANNELS), seg_length, keep_flag)
    unused_state, outputs = lax.scan(one_segment, jnp.zeros((SCAN_CHANNELS, HEAD_DIM, STATE), jnp.float32), inputs)
    return outputs.reshape(PLACE_CAPACITY, INNER)
```

```python
import functools

import jax
import jax.numpy as jnp
from jax import lax
from jax.experimental import pallas as pl
from jax.experimental.pallas import tpu as pltpu
from jax.sharding import Mesh, PartitionSpec as P

HEAD_DIM = 64
KERNEL = 4
EPSILON = 1e-05
TOK = 128
GROUPS = 8
XW = 1024
GW = 1280
LANE = 128
LW = 256
CHUNKS = 64
ROWS = 80
AXES = ("seq", "y", "core")
CHIPS = ("seq", "y")
F32 = jnp.float32
BF16 = jnp.bfloat16
VMEM_LIMIT = 56 * 1024 * 1024


def iota(shape, dim):
    return lax.broadcasted_iota(jnp.int32, shape, dim)


def split3(v):
    hi = v.astype(BF16).astype(F32)
    mid = (v - hi).astype(BF16).astype(F32)
    return hi, mid, v - hi - mid


def widen(table, first):
    rows = table.shape[0]
    low = iota((rows, LANE), 1) < HEAD_DIM
    cols = [jnp.broadcast_to(table[:, first + q : first + q + 1], (rows, LANE)) for q in range(4)]
    return jnp.concatenate([jnp.where(low, cols[0], cols[1]), jnp.where(low, cols[2], cols[3])], axis=1)


def head_place():
    return lax.axis_index("y") * 2 + lax.axis_index("core")


def prep_kernel(len_ref, decay_ref, step_ref, conv_ref, tab_ref, dt_ref, cand_ref, rows_ref, sems):
    first_row = len_ref[0] - head_place() * TOK
    copies = []
    for k in range(KERNEL - 1):
        row = jnp.clip(first_row - (KERNEL - 1) + k, 0, TOK - 1)
        copy = pltpu.make_async_copy(conv_ref.at[pl.ds(row, 1)], rows_ref.at[pl.ds(k, 1)], sems.at[k])
        copy.start()
        copies.append(copy)
    to = iota((LANE, LANE), 1)
    head = ((to % 32) // 4) * 16 + (to // 32) * 4 + to % 4
    order = jnp.where(iota((LANE, LANE), 0) == head, 1.0, 0.0).astype(BF16)
    live = iota((TOK, LANE), 0) < first_row
    log_rate = jnp.where(live, jnp.dot(decay_ref[...], order, preferred_element_type=F32), 0.0)
    gain = jnp.where(live, jnp.dot(step_ref[...], order, preferred_element_type=F32), 0.0)
    upto = jnp.where(iota((TOK, TOK), 0) >= iota((TOK, TOK), 1), 1.0, 0.0).astype(BF16)
    running = jnp.dot(upto, log_rate.astype(BF16), preferred_element_type=F32)
    middle = running[TOK // 2 - 1 : TOK // 2]
    total = running[TOK - 1 : TOK]
    tab_ref[0] = jnp.exp(total - running) * gain
    tab_ref[1] = jnp.exp(middle - running) * gain
    tab_ref[2] = jnp.exp(running - middle)
    tab_ref[3] = jnp.exp(running)
    dt_ref[...] = jnp.broadcast_to(jnp.exp(total), (8, LANE))
    for k in range(KERNEL - 1):
        copies[k].wait()
        row = first_row - (KERNEL - 1) + k
        inside = jnp.where((row >= 0) & (row < TOK), 1.0, 0.0)
        cand_ref[k] = (rows_ref[k].astype(F32) * inside).astype(BF16)


def prep(seg_length, decay_log, step_size, conv_input):
    return pl.pallas_call(
        prep_kernel,
        in_specs=[
            pl.BlockSpec(memory_space=pltpu.SMEM),
            pl.BlockSpec(memory_space=pltpu.VMEM),
            pl.BlockSpec(memory_space=pltpu.VMEM),
            pl.BlockSpec(memory_space=pl.ANY),
        ],
        out_specs=[pl.BlockSpec(memory_space=pltpu.VMEM)] * 3,
        out_shape=[
            jax.ShapeDtypeStruct((4, TOK, LANE), F32),
            jax.ShapeDtypeStruct((8, LANE), F32),
            jax.ShapeDtypeStruct((KERNEL - 1, GROUPS, GW), BF16),
        ],
        scratch_shapes=[pltpu.VMEM((KERNEL - 1, GROUPS, GW), BF16), pltpu.SemaphoreType.DMA((KERNEL - 1,))],
        compiler_params=pltpu.CompilerParams(vmem_limit_bytes=VMEM_LIMIT),
        name="prep",
    )(seg_length, decay_log, step_size, conv_input)


def conv_kernel(core_ref, conv_ref, halo_ref, w_ref, decay_ref, x_ref, bc_ref, own_ref, oth_ref, act_ref, bt_ref):
    step = pl.program_id(0)
    core = core_ref[0]
    taps = [w_ref[k] * 0.5 for k in range(KERNEL)]
    bias = w_ref[KERNEL] * 0.5

    def activate(window, at):
        half = bias[None] + taps[0][None] * window[0:8]
        for k in range(1, KERNEL):
            half = half + taps[k][None] * window[k : k + 8]
        half = half + half * jnp.tanh(half)
        for tile in range(2):
            act_ref[tile, pl.ds(at, 64), :] = half[:, :, tile * LANE : (tile + 1) * LANE].reshape(64, LANE)

    def of_group(g):
        return jnp.concatenate([act_ref[tile, pl.ds(g, TOK, stride=GROUPS), :] for tile in range(2)], axis=1)

    activate(jnp.concatenate([halo_ref[...].astype(F32), conv_ref[0:8].astype(F32)], axis=0), 0)

    def tokens(i, carry):
        activate(conv_ref[pl.ds(i * 8 - (KERNEL - 1), 8 + KERNEL - 1)].astype(F32), pl.multiple_of(i * 64, 64))
        return carry

    lax.fori_loop(1, TOK // 8, tokens, 0, unroll=3)

    @pl.when(step == 0)
    def _():
        for g in range(GROUPS):
            both = of_group(g)
            bc_ref[g] = both.astype(BF16)
            bt_ref[g] = both[:, :LANE].T.astype(BF16)

    @pl.when(step > 0)
    def _():
        decay = pltpu.roll(decay_ref[...], (LANE - 32 * (step - 1)) % LANE, 1)
        for g in range(GROUPS):
            x = of_group(g)
            x_ref[g] = x.astype(BF16)
            carried = (x * widen(decay, g * 4)).astype(BF16)
            state = jnp.dot(bt_ref[g], carried, preferred_element_type=F32).astype(BF16)

            def put(ref):
                for tile in range(2):
                    for part in range(2):
                        ref[g % 4, 0, tile * 2 + part] = state[part * 64 : part * 64 + 64, tile * LANE : (tile + 1) * LANE]

            pl.when(core == g // 4)(functools.partial(put, own_ref))
            pl.when(core != g // 4)(functools.partial(put, oth_ref))


def conv_states(core, conv_input, halo, weights, decay):
    lanes = lambda j, s: (0, 0, (j + 4) % 5)
    later = lambda j: jnp.maximum(j - 1, 0)
    half = jax.ShapeDtypeStruct((4, 4, 4, 64, LANE), BF16)
    half_spec = pl.BlockSpec((4, 1, 4, 64, LANE), lambda j, s: (0, later(j), 0, 0, 0))
    return pl.pallas_call(
        conv_kernel,
        grid_spec=pltpu.PrefetchScalarGridSpec(
            num_scalar_prefetch=1,
            grid=(5,),
            in_specs=[
                pl.BlockSpec((TOK, GROUPS, LW), lanes),
                pl.BlockSpec((KERNEL - 1, GROUPS, LW), lanes),
                pl.BlockSpec((KERNEL + 1, GROUPS, LW), lanes),
                pl.BlockSpec((TOK, LANE), lambda j, s: (0, 0)),
            ],
            out_specs=[
                pl.BlockSpec((GROUPS, TOK, LW), lambda j, s: (0, 0, later(j))),
                pl.BlockSpec((GROUPS, TOK, LW), lambda j, s: (0, 0, 0)),
                half_spec,
                half_spec,
            ],
            scratch_shapes=[pltpu.VMEM((2, TOK * GROUPS, LANE), F32), pltpu.VMEM((GROUPS, LANE, TOK), BF16)],
        ),
        out_shape=[
            jax.ShapeDtypeStruct((GROUPS, TOK, XW), BF16),
            jax.ShapeDtypeStruct((GROUPS, TOK, LW), BF16),
            half,
            half,
        ],
        compiler_params=pltpu.CompilerParams(vmem_limit_bytes=VMEM_LIMIT),
        name="conv_states",
    )(core, conv_input, halo, weights, decay)


def combine_kernel(core_ref, first_ref, own_ref, sib_ref, dto_ref, dts_ref, out_ref):
    core = core_ref[0]
    keep = jnp.where(lax.axis_index("y") == 0, 1 - first_ref[0], 1).astype(F32)
    shift = (2 * LANE - 16 * core - 4 * pl.program_id(0)) % LANE
    d_own = pltpu.roll(dto_ref[...], shift, 1)
    d_sib = pltpu.roll(dts_ref[...], shift, 1)
    on_own = jnp.where(core == 0, d_sib, 1.0)
    on_sib = jnp.where(core == 1, d_own, 1.0)
    row = iota((16, LANE), 0)
    for j in range(4):
        a, b, d = (widen(v, 32 * j)[0:1] for v in (on_own, on_sib, d_own * d_sib))
        hi, mid, low = split3(d)
        for tile in range(2):
            at = slice(tile * LANE, (tile + 1) * LANE)
            extra = jnp.where(row == 0, hi[:, at], jnp.where(row == 1, mid[:, at], jnp.where(row == 2, low[:, at], keep)))
            for part in range(2):
                state = own_ref[0, j, tile * 2 + part].astype(F32) * a[:, at]
                state = state + sib_ref[0, j, tile * 2 + part].astype(F32) * b[:, at]
                piece = (j * 2 + tile) * 2 + part
                out_ref[piece, 0:64] = state.astype(BF16)
                out_ref[piece, 64:ROWS] = extra.astype(BF16)


def combine(core, seg_first, own, sib, d_own, d_sib):
    half_spec = pl.BlockSpec((1, 4, 4, 64, LANE), lambda i, s: (i, 0, 0, 0, 0))
    row_spec = pl.BlockSpec((8, LANE), lambda i, s: (0, 0))
    return pl.pallas_call(
        combine_kernel,
        grid_spec=pltpu.PrefetchScalarGridSpec(
            num_scalar_prefetch=1,
            grid=(4,),
            in_specs=[pl.BlockSpec(memory_space=pltpu.SMEM), half_spec, half_spec, row_spec, row_spec],
            out_specs=pl.BlockSpec((16, ROWS, LANE), lambda i, s: (i, 0, 0)),
        ),
        out_shape=jax.ShapeDtypeStruct((CHUNKS, ROWS, LANE), BF16),
        compiler_params=pltpu.CompilerParams(vmem_limit_bytes=VMEM_LIMIT),
        name="combine",
    )(core, seg_first, own, sib, d_own, d_sib)


def scan_kernel(chips, in_ref, out_ref):
    each = in_ref.shape[0] // chips

    def chip(c, states):
        after = []
        for i, state in enumerate(states):
            at = c * each + i
            extra = in_ref[at, 64:ROWS].astype(F32)
            state = extra[3:4] * state
            out_ref[at] = state.astype(BF16)
            decay = extra[0:1] + extra[1:2] + extra[2:3]
            after.append(decay * state + in_ref[at, 0:64].astype(F32))
        return tuple(after)

    lax.fori_loop(0, chips, chip, tuple(jnp.zeros((64, LANE), F32) for _ in range(each)), unroll=4)


def scan(chips, pieces):
    return pl.pallas_call(
        functools.partial(scan_kernel, chips),
        in_specs=[pl.BlockSpec(memory_space=pltpu.VMEM)],
        out_specs=pl.BlockSpec(memory_space=pltpu.VMEM),
        out_shape=jax.ShapeDtypeStruct((CHUNKS, 64, LANE), BF16),
        compiler_params=pltpu.CompilerParams(vmem_limit_bytes=VMEM_LIMIT),
        name="scan",
    )(pieces)


def local_kernel(other, core_ref, len_ref, x_ref, bc_ref, tab_ref, before_ref, dts_ref, gate_ref, skip_ref, p_ref, q_ref):
    core = core_ref[0]
    group = ((core + other) % 2) * 4 + pl.program_id(0)
    shift = (LANE - 4 * group) % LANE
    inner, after, since = (pltpu.roll(tab_ref[k], shift, 1) for k in (1, 2, 3))
    d_before = jnp.where(core == 1, pltpu.roll(dts_ref[...], shift, 1), 1.0)
    b = bc_ref[0, :, :LANE]
    c = bc_ref[0, :, LANE:]
    scores = lax.dot_general(c, b, (((1,), (1,)), ((), ())), preferred_element_type=F32)
    causal = iota((TOK, TOK), 0) >= iota((TOK, TOK), 1)
    scores = jnp.where(causal, scores, 0.0).astype(BF16)
    live = iota((TOK, LW), 0) < len_ref[0] - head_place() * TOK
    for j in range(4):
        at = slice(j * LW, (j + 1) * LW)
        x = x_ref[0, :, at].astype(F32)
        scaled = (x * widen(inner, 32 * j)).astype(BF16)
        y = widen(after, 32 * j) * jnp.dot(scores, scaled, preferred_element_type=F32)
        before = jnp.concatenate(
            [jnp.concatenate([before_ref[0, j, tile * 2], before_ref[0, j, tile * 2 + 1]], axis=0) for tile in range(2)],
            axis=1,
        )
        grown = widen(since, 32 * j)
        y = y + grown * (core.astype(F32) * jnp.dot(c, before, preferred_element_type=F32))
        y = y + skip_ref[:, at] * x
        half = gate_ref[:, at].astype(F32) * 0.5
        silu = half + half * jnp.tanh(half)
        p_ref[0, :, at] = jnp.where(live, y * silu, 0.0).astype(BF16)
        q_ref[0, :, at] = jnp.where(live, grown * widen(d_before, 32 * j)[0:1] * silu, 0.0).astype(BF16)


def local(other, core, seg_length, x, bc, tables, before, d_sib, gate_input, skip):
    group = lambda i, s: ((s[0] + other) % 2) * 4 + i
    out = jax.ShapeDtypeStruct((4, TOK, XW), BF16)
    out_spec = pl.BlockSpec((1, TOK, XW), lambda i, s: (i, 0, 0))
    return pl.pallas_call(
        functools.partial(local_kernel, other),
        grid_spec=pltpu.PrefetchScalarGridSpec(
            num_scalar_prefetch=1,
            grid=(4,),
            in_specs=[
                pl.BlockSpec(memory_space=pltpu.SMEM),
                pl.BlockSpec((1, TOK, XW), lambda i, s: (group(i, s), 0, 0)),
                pl.BlockSpec((1, TOK, LW), lambda i, s: (group(i, s), 0, 0)),
                pl.BlockSpec((4, TOK, LANE), lambda i, s: (0, 0, 0)),
                pl.BlockSpec((1, 4, 4, 64, LANE), lambda i, s: (i, 0, 0, 0, 0)),
                pl.BlockSpec((8, LANE), lambda i, s: (0, 0)),
                pl.BlockSpec((TOK, XW), lambda i, s: (0, group(i, s))),
                pl.BlockSpec((1, XW), lambda i, s: (0, group(i, s))),
            ],
            out_specs=[out_spec, out_spec],
        ),
        out_shape=[out, out],
        compiler_params=pltpu.CompilerParams(vmem_limit_bytes=VMEM_LIMIT),
        cost_estimate=pl.CostEstimate(flops=400_000_000, bytes_accessed=8_000_000, transcendentals=600_000),
        name="local",
    )(core, seg_length, x, bc, tables, before, d_sib, gate_input, skip)


def finish_kernel(core_ref, p_ref, q_ref, c_ref, state_ref, gain_ref, *rest):
    out_ref = rest[-1]
    c = c_ref[0]
    gated = []
    for tile in range(0, 8, 2):
        state = jnp.concatenate(
            [jnp.concatenate([state_ref[(tile + k) * 2], state_ref[(tile + k) * 2 + 1]], axis=0) for k in range(2)],
            axis=1,
        )
        at = slice(tile * LANE, (tile + 2) * LANE)
        read = jnp.dot(c, state, preferred_element_type=F32)
        gated.append(p_ref[0, :, at].astype(F32) + read * q_ref[0, :, at].astype(F32))
    total = sum(jnp.sum(v * v, axis=1, keepdims=True) for v in gated)
    scale = lax.rsqrt(total / XW + EPSILON)
    for j, v in enumerate(gated):
        at = slice(j * LW, (j + 1) * LW)
        out_ref[:, at] = (v * scale * gain_ref[:, at]).astype(BF16)


def finish(other, core, p, q, bc, states, gain, out=None):
    group = lambda i, s: ((s[0] + other) % 2) * 4 + i
    operands = [core, p, q, bc, states, gain]
    in_specs = [
        pl.BlockSpec((1, TOK, XW), lambda i, s: (i, 0, 0)),
        pl.BlockSpec((1, TOK, XW), lambda i, s: (i, 0, 0)),
        pl.BlockSpec((1, TOK, LANE), lambda i, s: (group(i, s), 0, 1)),
        pl.BlockSpec((16, 64, LANE), lambda i, s: (i, 0, 0)),
        pl.BlockSpec((1, XW), lambda i, s: (0, group(i, s))),
    ]
    aliases = {}
    if out is not None:
        operands.append(out)
        in_specs.append(pl.BlockSpec(memory_space=pl.ANY))
        aliases = {6: 0}
    return pl.pallas_call(
        finish_kernel,
        grid_spec=pltpu.PrefetchScalarGridSpec(
            num_scalar_prefetch=1,
            grid=(4,),
            in_specs=in_specs,
            out_specs=pl.BlockSpec((TOK, XW), lambda i, s: (0, group(i, s))),
        ),
        out_shape=jax.ShapeDtypeStruct((TOK, GROUPS * XW), BF16),
        input_output_aliases=aliases,
        compiler_params=pltpu.CompilerParams(vmem_limit_bytes=VMEM_LIMIT),
        cost_estimate=pl.CostEstimate(flops=200_000_000, bytes_accessed=4_000_000, transcendentals=1000),
        name="finish",
    )(*operands)


def body(
    conv_input,
    gate_input,
    step_size,
    decay_log,
    conv_weight,
    conv_bias,
    skip_gain,
    norm_gain,
    seg_length,
    seg_first,
):
    segments = lax.axis_size("seq")
    in_segment = lax.axis_size("y") * lax.axis_size("core")
    count = segments * in_segment
    chips = count // 2
    core = lax.axis_index("core").astype(jnp.int32).reshape(1)
    swap = [(0, 1), (1, 0)]

    last = lax.ppermute(
        conv_input[TOK - (KERNEL - 1) :], AXES, [(i, i + 1) for i in range(count) if (i + 1) % in_segment]
    )
    tables, d_own, cand = prep(seg_length, decay_log, step_size, conv_input)
    tails = [
        lax.ppermute(cand, AXES, [(s * in_segment + h, (s + 1) * in_segment) for s in range(segments - 1)])
        for h in range(in_segment)
    ]
    d_sib = lax.ppermute(d_own, "core", swap)
    weights = jnp.concatenate([conv_weight[:, 0], conv_bias], axis=0)
    weights = jnp.broadcast_to(weights[None], (GROUPS,) + weights.shape)
    weights = lax.all_to_all(weights, ("y", "core"), 0, 0, tiled=True).transpose(1, 0, 2)
    keep = (1 - seg_first[0]).astype(BF16)
    halo = last + keep * functools.reduce(jnp.add, tails)

    x, bc, own, oth = conv_states(core, conv_input, halo, weights, tables[0])
    sib_own = lax.ppermute(oth, "core", swap)
    pieces = combine(core, seg_first, own, sib_own, d_own, d_sib)
    pieces = lax.all_to_all(pieces, CHIPS, 0, 0, tiled=True)
    sib_oth = lax.ppermute(own, "core", swap[:1])

    skip = jnp.repeat(skip_gain, HEAD_DIM)[None]
    p_own, q_own = local(0, core, seg_length, x, bc, tables, sib_own, d_sib, gate_input, skip)
    p_oth, q_oth = local(1, core, seg_length, x, bc, tables, sib_oth, d_sib, gate_input, skip)

    states = lax.all_to_all(scan(chips, pieces), CHIPS, 0, 0, tiled=True)
    states_oth = lax.ppermute(states, "core", swap)
    gain = norm_gain[None]
    out = finish(0, core, p_own, q_own, bc, states, gain)
    return finish(1, core, p_oth, q_oth, bc, states_oth, gain, out)


def solution(mesh):
    segments, in_segment = mesh.devices.shape
    fine = Mesh(mesh.devices.reshape(segments, in_segment // 2, 2), AXES)
    tokens = P(AXES, None)
    return jax.shard_map(
        body,
        mesh=fine,
        in_specs=(
            P(AXES, None, None),
            tokens,
            tokens,
            tokens,
            P(None, ("y", "core"), None),
            P(("y", "core"), None),
            P(),
            P(),
            P("seq"),
            P("seq"),
        ),
        out_specs=tokens,
        check_vma=False,
    )
```

```python
import functools

import jax
import jax.numpy as jnp
from jax import lax
from jax.experimental import pallas as pl
from jax.experimental.pallas import tpu as pltpu
from jax.sharding import Mesh, PartitionSpec as P

HEAD_DIM = 64
KERNEL = 4
EPSILON = 1e-05
TOK = 128
GROUPS = 8
XW = 1024
GW = 1280
LANE = 128
LW = 256
CHUNKS = 64
ENDS = KERNEL - 1
PACK = 24
ROWS = 72
AXES = ("seq", "y", "core")
CHIPS = ("seq", "y")
F32 = jnp.float32
BF16 = jnp.bfloat16


def iota(shape, dim):
    return lax.broadcasted_iota(jnp.int32, shape, dim)


def split3(v):
    hi = v.astype(BF16).astype(F32)
    mid = (v - hi).astype(BF16).astype(F32)
    return hi, mid, v - hi - mid


def widen(table, first):
    lane = iota(table.shape, 1) // HEAD_DIM + first
    return jnp.take_along_axis(table, lane, axis=1, mode="promise_in_bounds")


def head_place():
    return lax.axis_index("y") * 2 + lax.axis_index("core")


def in_vmem(count):
    return [pl.BlockSpec(memory_space=pltpu.VMEM)] * count


def in_hbm(count):
    return [pl.BlockSpec(memory_space=pltpu.HBM)] * count


def in_smem(count):
    return [pl.BlockSpec(memory_space=pltpu.SMEM)] * count


def hbm(shape):
    return pltpu.HBM(shape, BF16)


def from_hbm(value):
    return pltpu.with_memory_space_constraint(value, pltpu.HBM)


def params(mib=16):
    return pltpu.CompilerParams(vmem_limit_bytes=mib * 1024 * 1024)


def start_kernel(
    len_ref, decay_hbm, step_hbm, conv_hbm, tab_ref, et_ref, tail_ref, decay_ref, step_ref, rows_ref, sems
):
    first_row = len_ref[0] - head_place() * TOK
    copies = [
        pltpu.make_async_copy(decay_hbm, decay_ref, sems.at[0]),
        pltpu.make_async_copy(step_hbm, step_ref, sems.at[1]),
    ]
    for k in range(ENDS):
        row = jnp.clip(first_row - ENDS + k, 0, TOK - 1)
        copies.append(pltpu.make_async_copy(conv_hbm.at[pl.ds(row, 1)], rows_ref.at[pl.ds(k, 1)], sems.at[2 + k]))
    for copy in copies:
        copy.start()
    for copy in copies:
        copy.wait()
    for k in range(ENDS):
        row = first_row - ENDS + k
        inside = jnp.where((row >= 0) & (row < TOK), 1.0, 0.0)
        tail_ref[k] = (rows_ref[k].astype(F32) * inside).astype(BF16)
    live = iota((TOK, LANE), 0) < first_row
    log_rate = jnp.where(live, decay_ref[...].astype(F32), 0.0)
    gain = jnp.where(live, step_ref[...].astype(F32), 0.0)
    upto = jnp.where(iota((TOK, TOK), 0) >= iota((TOK, TOK), 1), 1.0, 0.0).astype(BF16)
    running = jnp.dot(upto, log_rate.astype(BF16), preferred_element_type=F32)
    middle = running[TOK // 2 - 1 : TOK // 2]
    total = running[TOK - 1 : TOK]
    tab_ref[0] = jnp.exp(middle - running) * gain
    tab_ref[1] = jnp.exp(running - middle)
    tab_ref[2] = jnp.exp(running)
    et_ref[0:TOK] = jnp.exp(total - running) * gain
    et_ref[TOK:] = jnp.broadcast_to(jnp.exp(total), (8, LANE))


def start(seg_length, decay_log, step_size, conv_input):
    return pl.pallas_call(
        start_kernel,
        in_specs=in_smem(1) + in_hbm(3),
        out_specs=in_vmem(3),
        out_shape=[
            jax.ShapeDtypeStruct((3, TOK, LANE), F32),
            jax.ShapeDtypeStruct((TOK + 8, LANE), F32),
            jax.ShapeDtypeStruct((ENDS, GROUPS, GW), BF16),
        ],
        scratch_shapes=[
            pltpu.VMEM((TOK, LANE), BF16),
            pltpu.VMEM((TOK, LANE), BF16),
            pltpu.VMEM((ENDS, GROUPS, GW), BF16),
            pltpu.SemaphoreType.DMA((2 + ENDS,)),
        ],
        compiler_params=params(),
        name="start",
    )(seg_length, from_hbm(decay_log), from_hbm(step_size), from_hbm(conv_input))


def weight_row(m):
    return m // 4 * 8 + 4 + m % 4


def pack_kernel(first_ref, conv_hbm, tail_ref, weight_ref, bias_ref, out_hbm, last_ref, out_ref, sem, sems):
    load = pltpu.make_async_copy(conv_hbm.at[pl.ds(TOK - ENDS, ENDS)], last_ref, sem)
    load.start()
    place, core = lax.axis_index("y"), lax.axis_index("core")
    keep = (1 - first_ref[0]).astype(F32)
    row = iota((GROUPS, LANE), 0)
    low = row < 4
    load.wait()
    for tile in range(GW // LANE):
        at = slice(tile * LANE, (tile + 1) * LANE)
        rows = [weight_ref[k, :, at] for k in range(KERNEL)] + [bias_ref[:, at]]
        rows = rows + [v - v.astype(BF16).astype(F32) for v in rows]
        for k in range(ENDS):
            fill = jnp.zeros((GROUPS, LANE), F32)
            for m in range(4 * k, min(4 * k + 4, len(rows))):
                fill = jnp.where(row == 4 + m % 4, rows[m], fill)
            tail = tail_ref[k, :, at].astype(F32) * keep
            last = last_ref[k, :, at].astype(F32)
            for y in range(4):
                if y == 0:
                    value = tail
                else:
                    value = last * jnp.where((place == y - 1) & (core == 1), 1.0, 0.0)
                for c in range(2):
                    mine = value if c == 0 else pltpu.roll(value, 4, 0)
                    out_ref[y * 2 + c, k * 8 : k * 8 + 8, at] = jnp.where(low, mine, fill).astype(BF16)
    copies = [pltpu.make_async_copy(out_ref.at[pl.ds(4 * k, 4)], out_hbm.at[pl.ds(4 * k, 4)], sems.at[k]) for k in range(2)]
    for copy in copies:
        copy.start()
    for copy in copies:
        copy.wait()


def pack(seg_first, conv_input, tail, weight, bias):
    shape = (GROUPS, PACK, GW)
    return pl.pallas_call(
        pack_kernel,
        in_specs=in_smem(1) + in_hbm(1) + in_vmem(3),
        out_specs=in_hbm(1)[0],
        out_shape=hbm(shape),
        scratch_shapes=[
            pltpu.VMEM((ENDS, GROUPS, GW), BF16),
            pltpu.VMEM(shape, BF16),
            pltpu.SemaphoreType.DMA,
            pltpu.SemaphoreType.DMA((2,)),
        ],
        compiler_params=params(),
        name="pack",
    )(seg_first, from_hbm(conv_input), tail, weight, bias)


PART = 16


def convolve(window, taps):
    half = taps[KERNEL][None] + taps[0][None] * window[0:PART]
    for k in range(1, KERNEL):
        half = half + taps[k][None] * window[k : k + PART]
    half = half + half * jnp.tanh(half)
    return half.reshape(PART * GROUPS, LANE)


def load_lanes(refs, to_refs, sems):
    loads = []
    for i in range(GW // LW):
        at = pl.ds(i * LW, LW)
        loads.append(
            [pltpu.make_async_copy(ref.at[:, :, at], to.at[:, :, at], sems.at[k, i]) for k, (ref, to) in enumerate(zip(refs, to_refs))]
        )
        for load in loads[-1]:
            load.start()
    return loads


def states_kernel(
    core_ref, first_ref, own_hbm, sib_hbm, pack_ref, ets_ref, eto_ref, out_hbm, before_hbm, w_ref, halo_ref,
    own_ref, sib_ref, packed_ref, act_ref, pieces_ref, before_ref, sems, load_sems,
):
    core = core_ref[0]
    loads = load_lanes((own_hbm, sib_hbm), (own_ref, sib_ref), load_sems)
    low = iota((1, GROUPS, LANE), 1) < 4
    kept = low == (core == 0)
    swap = lambda v: pltpu.roll(v, 4, v.ndim - 2)
    for tile in range(GW // LANE):
        at = slice(tile * LANE, (tile + 1) * LANE)
        packed_ref[...] = pack_ref[:, :, at].astype(F32).reshape(GROUPS * PACK, LANE)
        before = [sum(packed_ref[d * PACK + k * 8 : d * PACK + k * 8 + 8] for d in range(GROUPS)) for k in range(ENDS)]
        before = jnp.stack([jnp.where(low[0], v, 0.0) for v in before])
        halo_ref[:, :, at] = before.astype(BF16)
        halves = [packed_ref[pl.ds(weight_row(m), GROUPS, stride=PACK), :] * 0.5 for m in range(2 * KERNEL + 2)]
        taps = [halves[k] + halves[k + KERNEL + 1] for k in range(KERNEL + 1)]
        for k, v in enumerate(taps):
            w_ref[k, :, at] = v
        taps = [jnp.where(kept[0], v, swap(v)) for v in taps]
        if tile % 2 == 0:
            for load in loads[tile // 2]:
                load.wait()

        def merged(rows, at=at):
            return jnp.where(kept, own_ref[rows, :, at].astype(F32), swap(sib_ref[rows, :, at].astype(F32)))

        def tokens(i, carry, tile=tile, taps=taps, merged=merged):
            window = merged(pl.ds(i * PART - (KERNEL - 1), PART + KERNEL - 1))
            act_ref[tile, pl.ds(pl.multiple_of(i * PART * GROUPS, PART * GROUPS), PART * GROUPS), :] = convolve(window, taps)
            return carry

        last = slice(TOK - (KERNEL - 1), TOK)
        between = jnp.where(core == 0, swap(own_ref[last, :, at].astype(F32)), sib_ref[last, :, at].astype(F32))
        window = jnp.concatenate([jnp.where(low, before, between), merged(slice(0, PART))], axis=0)
        act_ref[tile, 0 : PART * GROUPS, :] = convolve(window, taps)
        lax.fori_loop(1, TOK // PART, tokens, 0, unroll=True)

    own, sib = eto_ref[...], ets_ref[...]
    decay = [jnp.where(core == 0, own, sib), jnp.where(core == 0, sib, own)]
    d_last = decay[1][TOK:]
    d_chip = decay[0][TOK:] * d_last
    keep = jnp.where(lax.axis_index("y") == 0, 1 - first_ref[0], 1).astype(F32)
    row = iota((8, LANE), 0)
    copies = []
    for i in range(4):
        of_group = lambda half, tile: act_ref[tile, pl.ds(half * 4 + i, TOK, stride=GROUPS), :]
        b_t = [of_group(half, 8).T.astype(BF16) for half in range(2)]
        for j in range(4):
            states = []
            for half in range(2):
                carried = [
                    (of_group(half, tile) * widen(decay[half][:TOK], core * 64 + i * 16 + tile * 2)).astype(BF16)
                    for tile in (2 * j, 2 * j + 1)
                ]
                states.append(jnp.dot(b_t[half], jnp.concatenate(carried, axis=1), preferred_element_type=F32))
            for tile in range(2):
                lanes = slice(tile * LANE, (tile + 1) * LANE)
                head = core * 64 + i * 16 + (2 * j + tile) * 2
                hi, mid, bottom = split3(widen(d_chip, head))
                extra = jnp.where(row == 0, hi, jnp.where(row == 1, mid, jnp.where(row == 2, bottom, keep)))
                first = states[0][:, lanes]
                both = (first * widen(d_last, head)[0:1] + states[1][:, lanes]).astype(BF16)
                first = first.astype(BF16)
                for rows in range(2):
                    piece = (i * 8 + 2 * j + tile) * 2 + rows
                    before_ref[i, j, tile * 2 + rows] = first[rows * 64 : rows * 64 + 64]
                    pieces_ref[piece, 0:64] = both[rows * 64 : rows * 64 + 64]
                    pieces_ref[piece, 64:ROWS] = extra.astype(BF16)
        group = pl.ds(i * 16, 16)
        copies.append(pltpu.make_async_copy(pieces_ref.at[group], out_hbm.at[group], sems.at[0, i]))
        copies.append(pltpu.make_async_copy(before_ref.at[i], before_hbm.at[i], sems.at[1, i]))
        copies[-2].start()
        copies[-1].start()
    for copy in copies:
        copy.wait()


def chip_states(core, seg_first, own, sib, packs, et_sib, et_own):
    pieces = (CHUNKS, ROWS, LANE)
    before = (4, 4, 4, 64, LANE)
    return pl.pallas_call(
        states_kernel,
        in_specs=in_smem(2) + in_hbm(2) + in_vmem(3),
        out_specs=in_hbm(2) + in_vmem(2),
        out_shape=[
            hbm(pieces),
            hbm(before),
            jax.ShapeDtypeStruct((KERNEL + 1, GROUPS, GW), F32),
            jax.ShapeDtypeStruct((ENDS, GROUPS, GW), BF16),
        ],
        scratch_shapes=[
            pltpu.VMEM((TOK, GROUPS, GW), BF16),
            pltpu.VMEM((TOK, GROUPS, GW), BF16),
            pltpu.VMEM((GROUPS * PACK, LANE), F32),
            pltpu.VMEM((GW // LANE, TOK * GROUPS, LANE), F32),
            pltpu.VMEM(pieces, BF16),
            pltpu.VMEM(before, BF16),
            pltpu.SemaphoreType.DMA((2, 4)),
            pltpu.SemaphoreType.DMA((2, GW // LW)),
        ],
        compiler_params=params(20),
        name="chip_states",
    )(core, seg_first, from_hbm(own), from_hbm(sib), packs, et_sib, et_own)


def act_kernel(
    core_ref, conv_hbm, sib_hbm, own_halo_ref, sib_halo_ref, w_ref, x_hbm, bc_hbm,
    conv_ref, last_ref, act_ref, x_ref, bc_ref, sems, load_sems,
):
    core = core_ref[0]
    last = pltpu.make_async_copy(sib_hbm.at[pl.ds(TOK - ENDS, ENDS)], last_ref, load_sems.at[1, 0])
    last.start()
    loads = load_lanes((conv_hbm,), (conv_ref,), load_sems)
    last.wait()
    low = iota((1, GROUPS, LANE), 1) < 4
    for tile in range(GW // LANE):
        at = slice(tile * LANE, (tile + 1) * LANE)
        taps = [w_ref[k, :, at] for k in range(KERNEL + 1)]
        if tile % 2 == 0:
            loads[tile // 2][0].wait()

        def tokens(i, carry, at=at, tile=tile, taps=taps):
            window = conv_ref[pl.ds(i * PART - (KERNEL - 1), PART + KERNEL - 1), :, at].astype(F32)
            act_ref[tile, pl.ds(pl.multiple_of(i * PART * GROUPS, PART * GROUPS), PART * GROUPS), :] = convolve(window, taps)
            return carry

        halo = pltpu.roll(sib_halo_ref[:, :, at].astype(F32), 4, 1)
        halo = jnp.where(low, own_halo_ref[:, :, at].astype(F32), halo)
        halo = jnp.where(core == 0, halo, last_ref[:, :, at].astype(F32))
        window = jnp.concatenate([halo, conv_ref[0:PART, :, at].astype(F32)], axis=0)
        act_ref[tile, 0 : PART * GROUPS, :] = convolve(window, taps)
        lax.fori_loop(1, TOK // PART, tokens, 0, unroll=True)
    copies = []
    for g in range(GROUPS):
        for tile in range(GW // LANE):
            values = act_ref[tile, pl.ds(g, TOK, stride=GROUPS), :].astype(BF16)
            if tile < XW // LANE:
                x_ref[g, :, tile * LANE : (tile + 1) * LANE] = values
            else:
                bc_ref[g, :, tile * LANE - XW : (tile + 1) * LANE - XW] = values
        copies.append(pltpu.make_async_copy(x_ref.at[g], x_hbm.at[g], sems.at[0, g]))
        copies.append(pltpu.make_async_copy(bc_ref.at[g], bc_hbm.at[g], sems.at[1, g]))
        copies[-2].start()
        copies[-1].start()
    for copy in copies:
        copy.wait()


def activate(core, conv_input, sib, own_halo, sib_halo, weights):
    x, bc = (GROUPS, TOK, XW), (GROUPS, TOK, LW)
    return pl.pallas_call(
        act_kernel,
        in_specs=in_smem(1) + in_hbm(2) + in_vmem(3),
        out_specs=in_hbm(2),
        out_shape=[hbm(x), hbm(bc)],
        scratch_shapes=[
            pltpu.VMEM((TOK, GROUPS, GW), BF16),
            pltpu.VMEM((ENDS, GROUPS, GW), BF16),
            pltpu.VMEM((GW // LANE, TOK * GROUPS, LANE), F32),
            pltpu.VMEM(x, BF16),
            pltpu.VMEM(bc, BF16),
            pltpu.SemaphoreType.DMA((2, GROUPS)),
            pltpu.SemaphoreType.DMA((2, GW // LW)),
        ],
        compiler_params=params(18),
        cost_estimate=pl.CostEstimate(flops=20_000_000, bytes_accessed=8_000_000, transcendentals=1_400_000),
        name="activate",
    )(core, from_hbm(conv_input), from_hbm(sib), own_halo, sib_halo, weights)


def scan_kernel(chips, in_ref, out_hbm, out_ref, sems):
    each = CHUNKS // chips
    parts = 4
    size = CHUNKS // parts
    states = [jnp.zeros((64, LANE), F32) for _ in range(each)]
    stores = []
    for k in range(parts):
        for at in range(k * size, (k + 1) * size):
            i = at % each
            extra = in_ref[at, 64:ROWS].astype(F32)
            state = extra[3:4] * states[i]
            out_ref[at] = state.astype(BF16)
            states[i] = (extra[0:1] + extra[1:2] + extra[2:3]) * state + in_ref[at, 0:64].astype(F32)
        span = pl.ds(k * size, size)
        stores.append(pltpu.make_async_copy(out_ref.at[span], out_hbm.at[span], sems.at[k]))
        stores[-1].start()
    for store in stores:
        store.wait()


def scan(chips, pieces):
    return pl.pallas_call(
        functools.partial(scan_kernel, chips),
        in_specs=in_vmem(1),
        out_specs=in_hbm(1)[0],
        out_shape=hbm((CHUNKS, 64, LANE)),
        scratch_shapes=[pltpu.VMEM((CHUNKS, 64, LANE), BF16), pltpu.SemaphoreType.DMA((4,))],
        compiler_params=params(),
        name="scan",
    )(pieces)


def local_kernel(other, core_ref, len_ref, x_ref, bc_ref, tab_ref, before_ref, dts_ref, gate_ref, skip_ref, p_ref, q_ref):
    core = core_ref[0]
    group = ((core + other) % 2) * 4 + pl.program_id(0)
    inner, after, since = (tab_ref[k] for k in range(3))
    d_before = jnp.where(core == 1, dts_ref[TOK:], 1.0)
    spread = lambda table, j: jnp.concatenate([widen(table, group * 16 + j * 4 + 2 * k) for k in range(2)], axis=1)
    b = bc_ref[0, :, :LANE]
    c = bc_ref[0, :, LANE:]
    scores = lax.dot_general(c, b, (((1,), (1,)), ((), ())), preferred_element_type=F32)
    causal = iota((TOK, TOK), 0) >= iota((TOK, TOK), 1)
    scores = jnp.where(causal, scores, 0.0).astype(BF16)
    live = iota((TOK, LW), 0) < len_ref[0] - head_place() * TOK
    for j in range(4):
        at = slice(j * LW, (j + 1) * LW)
        x = x_ref[0, :, at].astype(F32)
        scaled = (x * spread(inner, j)).astype(BF16)
        y = spread(after, j) * jnp.dot(scores, scaled, preferred_element_type=F32)
        before = jnp.concatenate(
            [jnp.concatenate([before_ref[0, j, tile * 2], before_ref[0, j, tile * 2 + 1]], axis=0) for tile in range(2)],
            axis=1,
        )
        grown = spread(since, j)
        y = y + grown * (core.astype(F32) * jnp.dot(c, before, preferred_element_type=F32))
        y = y + skip_ref[:, at] * x
        half = gate_ref[:, at].astype(F32) * 0.5
        silu = half + half * jnp.tanh(half)
        p_ref[0, :, at] = jnp.where(live, y * silu, 0.0).astype(BF16)
        q_ref[0, :, at] = jnp.where(live, grown * spread(d_before, j)[0:1] * silu, 0.0).astype(BF16)


def local(other, core, seg_length, x, bc, tables, before, d_sib, gate_input, skip):
    group = lambda i, s: ((s[0] + other) % 2) * 4 + i
    out = hbm((4, TOK, XW))
    out_spec = pl.BlockSpec((1, TOK, XW), lambda i, s: (i, 0, 0))
    return pl.pallas_call(
        functools.partial(local_kernel, other),
        grid_spec=pltpu.PrefetchScalarGridSpec(
            num_scalar_prefetch=1,
            grid=(4,),
            in_specs=[
                pl.BlockSpec(memory_space=pltpu.SMEM),
                pl.BlockSpec((1, TOK, XW), lambda i, s: (group(i, s), 0, 0)),
                pl.BlockSpec((1, TOK, LW), lambda i, s: (group(i, s), 0, 0)),
                pl.BlockSpec((3, TOK, LANE), lambda i, s: (0, 0, 0)),
                pl.BlockSpec((1, 4, 4, 64, LANE), lambda i, s: (i, 0, 0, 0, 0)),
                pl.BlockSpec((TOK + 8, LANE), lambda i, s: (0, 0)),
                pl.BlockSpec((TOK, XW), lambda i, s: (0, group(i, s))),
                pl.BlockSpec((1, XW), lambda i, s: (0, group(i, s))),
            ],
            out_specs=[out_spec, out_spec],
        ),
        out_shape=[out, out],
        compiler_params=params(),
        cost_estimate=pl.CostEstimate(flops=400_000_000, bytes_accessed=8_000_000, transcendentals=600_000),
        name="local",
    )(core, seg_length, x, bc, tables, before, d_sib, gate_input, skip)


def finish_kernel(other, core_ref, p_ref, q_ref, bc_ref, state_ref, gain_ref, *rest):
    first = ((core_ref[0] + other) % 2) * 4
    if other:
        _, out_ref, rows_ref, sems = rest
    else:
        out_ref, rows_ref, sems, p_to, q_to, state_to, load_sems = rest
        loads = []
        for i in range(4):
            group = pl.ds(i * 16, 16)
            loads.append(pltpu.make_async_copy(state_ref.at[group], state_to.at[group], load_sems.at[0, i]))
            loads.append(pltpu.make_async_copy(p_ref.at[i], p_to.at[i], load_sems.at[1, i]))
            loads.append(pltpu.make_async_copy(q_ref.at[i], q_to.at[i], load_sems.at[2, i]))
        for load in loads:
            load.start()
        p_ref, q_ref, state_ref = p_to, q_to, state_to
    copies = []
    for i in range(4):
        if not other and i % 2 == 0:
            for load in loads[3 * i : 3 * i + 6]:
                load.wait()
        c = bc_ref[first + i, :, LANE:]
        gated = []
        for tile in range(0, 8, 2):
            state = jnp.concatenate(
                [
                    jnp.concatenate([state_ref[i * 16 + (tile + k) * 2], state_ref[i * 16 + (tile + k) * 2 + 1]], axis=0)
                    for k in range(2)
                ],
                axis=1,
            )
            at = slice(tile * LANE, (tile + 2) * LANE)
            read = jnp.dot(c, state, preferred_element_type=F32)
            gated.append(p_ref[i, :, at].astype(F32) + read * q_ref[i, :, at].astype(F32))
        total = sum(jnp.sum(v * v, axis=1, keepdims=True) for v in gated)
        scale = lax.rsqrt(total / XW + EPSILON)
        for j, v in enumerate(gated):
            at = slice(j * LW, (j + 1) * LW)
            rows_ref[i, :, at] = (v * scale * gain_ref[first + i, :, at]).astype(BF16)
        to = out_ref.at[:, pl.ds(pl.multiple_of((first + i) * XW, XW), XW)]
        copies.append(pltpu.make_async_copy(rows_ref.at[i], to, sems.at[i]))
        copies[-1].start()
    for copy in copies:
        copy.wait()


def finish(other, core, p, q, bc, states, gain, out=None):
    if other:
        operands = [core, p, q, bc, states, gain, out]
        in_specs = in_smem(1) + in_vmem(5) + [pl.BlockSpec(memory_space=pl.ANY)]
        loaded = []
    else:
        operands = [core, from_hbm(p), from_hbm(q), bc, from_hbm(states), gain]
        in_specs = in_smem(1) + in_hbm(2) + in_vmem(1) + in_hbm(1) + in_vmem(1)
        loaded = [
            pltpu.VMEM((4, TOK, XW), BF16),
            pltpu.VMEM((4, TOK, XW), BF16),
            pltpu.VMEM((CHUNKS, 64, LANE), BF16),
            pltpu.SemaphoreType.DMA((3, 4)),
        ]
    return pl.pallas_call(
        functools.partial(finish_kernel, other),
        in_specs=in_specs,
        out_specs=pl.BlockSpec(memory_space=pl.ANY),
        scratch_shapes=[pltpu.VMEM((4, TOK, XW), BF16), pltpu.SemaphoreType.DMA((4,))] + loaded,
        out_shape=jax.ShapeDtypeStruct((TOK, GROUPS * XW), BF16),
        input_output_aliases={6: 0} if other else {},
        compiler_params=params(),
        cost_estimate=pl.CostEstimate(flops=200_000_000, bytes_accessed=4_000_000, transcendentals=1000),
        name="finish",
    )(*operands)


def body(
    conv_input,
    gate_input,
    step_size,
    decay_log,
    conv_weight,
    conv_bias,
    skip_gain,
    norm_gain,
    seg_length,
    seg_first,
):
    segments = lax.axis_size("seq")
    in_segment = lax.axis_size("y") * lax.axis_size("core")
    chips = segments * in_segment // 2
    core = lax.axis_index("core").astype(jnp.int32).reshape(1)
    swap = [(0, 1), (1, 0)]

    sib = lax.ppermute(conv_input, "core", swap)
    tables, et_own, tail = start(seg_length, decay_log, step_size, conv_input)
    tail = lax.ppermute(tail, "seq", [(k, (k + 1) % segments) for k in range(segments)])
    et_sib = lax.ppermute(et_own, "core", swap)
    packs = pack(seg_first, conv_input, tail, conv_weight, conv_bias)
    packs = lax.all_to_all(packs, ("y", "core"), 0, 0, tiled=True)

    pieces, before_own, weights, halo = chip_states(core, seg_first, conv_input, sib, packs, et_sib, et_own)
    pieces = lax.all_to_all(pieces, CHIPS, 0, 0, tiled=True)
    before_oth = lax.ppermute(before_own, "core", swap[:1])
    halo_sib = lax.ppermute(halo, "core", swap)
    x, bc = activate(core, conv_input, sib, halo, halo_sib, weights)

    skip = jnp.repeat(skip_gain, HEAD_DIM)[None]
    pieces, x, bc = lax.optimization_barrier((pieces, x, bc))
    p_own, q_own = local(0, core, seg_length, x, bc, tables, before_own, et_sib, gate_input, skip)
    p_oth, q_oth = local(1, core, seg_length, x, bc, tables, before_oth, et_sib, gate_input, skip)
    states = lax.all_to_all(scan(chips, pieces), CHIPS, 0, 0, tiled=True)
    states, p_own, q_own, p_oth, q_oth = lax.optimization_barrier((states, p_own, q_own, p_oth, q_oth))
    states_oth = lax.ppermute(states, "core", swap)
    gain = norm_gain.reshape(GROUPS, 1, XW)
    out = finish(0, core, p_own, q_own, bc, states, gain)
    return finish(1, core, p_oth, q_oth, bc, states_oth, gain, out)


def solution(mesh):
    segments, in_segment = mesh.devices.shape
    fine = Mesh(mesh.devices.reshape(segments, in_segment // 2, 2), AXES)
    tokens = P(AXES, None)
    return jax.shard_map(
        body,
        mesh=fine,
        in_specs=(
            P(AXES, None, None),
            tokens,
            tokens,
            tokens,
            P(None, ("y", "core"), None),
            P(("y", "core"), None),
            P(),
            P(),
            P("seq"),
            P("seq"),
        ),
        out_specs=tokens,
        check_vma=False,
    )
```

```python
import functools

import jax
import jax.numpy as jnp
from jax import lax
from jax.experimental import pallas as pl
from jax.experimental.pallas import tpu as pltpu
from jax.sharding import Mesh, PartitionSpec as P

HEAD_DIM = 64
KERNEL = 4
EPSILON = 1e-05
TOK = 128
GROUPS = 8
XW = 1024
GW = 1280
LANE = 128
LW = 256
CHUNKS = 64
ENDS = KERNEL - 1
PACK = 24
ROWS = 72
AXES = ("seq", "y", "core")
CHIPS = ("seq", "y")
F32 = jnp.float32
BF16 = jnp.bfloat16
DONE = jax.ShapeDtypeStruct((8, LANE), F32)


def iota(shape, dim):
    return lax.broadcasted_iota(jnp.int32, shape, dim)


def split3(v):
    hi = v.astype(BF16).astype(F32)
    mid = (v - hi).astype(BF16).astype(F32)
    return hi, mid, v - hi - mid


def widen(table, first):
    lane = iota(table.shape, 1) // HEAD_DIM + first
    return jnp.take_along_axis(table, lane, axis=1, mode="promise_in_bounds")


def head_place():
    return lax.axis_index("y") * 2 + lax.axis_index("core")


def in_vmem(count):
    return [pl.BlockSpec(memory_space=pltpu.VMEM)] * count


def in_hbm(count):
    return [pl.BlockSpec(memory_space=pltpu.HBM)] * count


def in_smem(count):
    return [pl.BlockSpec(memory_space=pltpu.SMEM)] * count


def hbm(shape):
    return pltpu.HBM(shape, BF16)


def from_hbm(value):
    return pltpu.with_memory_space_constraint(value, pltpu.HBM)


def params(mib=16):
    return pltpu.CompilerParams(vmem_limit_bytes=mib * 1024 * 1024)


def start_kernel(
    len_ref, decay_hbm, step_hbm, conv_hbm, tab_ref, et_ref, ends_ref, decay_ref, step_ref, rows_ref, sems
):
    first_row = len_ref[0] - head_place() * TOK
    copies = [
        pltpu.make_async_copy(decay_hbm, decay_ref, sems.at[0]),
        pltpu.make_async_copy(step_hbm, step_ref, sems.at[1]),
    ]
    for k in range(ENDS):
        row = jnp.clip(first_row - ENDS + k, 0, TOK - 1)
        copies.append(pltpu.make_async_copy(conv_hbm.at[pl.ds(row, 1)], rows_ref.at[pl.ds(k, 1)], sems.at[2 + k]))
    copies.append(pltpu.make_async_copy(conv_hbm.at[pl.ds(TOK - ENDS, ENDS)], rows_ref.at[pl.ds(ENDS, ENDS)], sems.at[2 + ENDS]))
    for copy in copies:
        copy.start()
    for copy in copies:
        copy.wait()
    for k in range(ENDS):
        row = first_row - ENDS + k
        inside = jnp.where((row >= 0) & (row < TOK), 1.0, 0.0)
        ends_ref[k] = (rows_ref[k].astype(F32) * inside).astype(BF16)
        ends_ref[ENDS + k] = rows_ref[ENDS + k]
    live = iota((TOK, LANE), 0) < first_row
    log_rate = jnp.where(live, decay_ref[...].astype(F32), 0.0)
    gain = jnp.where(live, step_ref[...].astype(F32), 0.0)
    upto = jnp.where(iota((TOK, TOK), 0) >= iota((TOK, TOK), 1), 1.0, 0.0).astype(BF16)
    running = jnp.dot(upto, log_rate.astype(BF16), preferred_element_type=F32)
    middle = running[TOK // 2 - 1 : TOK // 2]
    total = running[TOK - 1 : TOK]
    tab_ref[0] = jnp.exp(middle - running) * gain
    tab_ref[1] = jnp.exp(running - middle)
    tab_ref[2] = jnp.exp(running)
    et_ref[0:TOK] = jnp.exp(total - running) * gain
    et_ref[TOK:] = jnp.broadcast_to(jnp.exp(total), (8, LANE))


def start(seg_length, decay_log, step_size, conv_input):
    return pl.pallas_call(
        start_kernel,
        in_specs=in_smem(1) + in_hbm(3),
        out_specs=in_vmem(3),
        out_shape=[
            jax.ShapeDtypeStruct((3, TOK, LANE), F32),
            jax.ShapeDtypeStruct((TOK + 8, LANE), F32),
            jax.ShapeDtypeStruct((2 * ENDS, GROUPS, GW), BF16),
        ],
        scratch_shapes=[
            pltpu.VMEM((TOK, LANE), BF16),
            pltpu.VMEM((TOK, LANE), BF16),
            pltpu.VMEM((2 * ENDS, GROUPS, GW), BF16),
            pltpu.SemaphoreType.DMA((3 + ENDS,)),
        ],
        compiler_params=params(),
        name="start",
    )(seg_length, from_hbm(decay_log), from_hbm(step_size), from_hbm(conv_input))


def weight_row(m):
    return m // 4 * 8 + m % 4 * 2 + 1


def pack_kernel(own_ref, sib_ref, weight_ref, bias_ref, on_ref, tail_ref):
    place, core = lax.axis_index("y"), lax.axis_index("core")
    row = iota((GROUPS, LANE), 0)
    even = row % 2 == 0
    for tile in range(GW // LANE):
        at = slice(tile * LANE, (tile + 1) * LANE)
        rows = [weight_ref[k, :, at] for k in range(KERNEL)] + [bias_ref[:, at]]
        rows = rows + [v - v.astype(BF16).astype(F32) for v in rows]
        for k in range(ENDS):
            fill = jnp.zeros((GROUPS, LANE), F32)
            for m in range(4 * k, min(4 * k + 4, len(rows))):
                fill = jnp.where(row == weight_row(m % 4), rows[m], fill)
            tail = own_ref[k, :, at].astype(F32) + sib_ref[k, :, at].astype(F32)
            last = jnp.where(core == 0, sib_ref[ENDS + k, :, at].astype(F32), own_ref[ENDS + k, :, at].astype(F32))
            onward = jnp.where(place == lax.axis_size("y") - 1, tail, last)
            for value, ref in ((onward, on_ref), (tail, tail_ref)):
                value = jnp.where(core == 0, value, pltpu.roll(value, GROUPS - 1, 0))
                ref[k * 8 : k * 8 + 8, at] = jnp.where(even, value, fill).astype(BF16)


def pack(own, sib, weight, bias):
    shape = jax.ShapeDtypeStruct((PACK, GW), BF16)
    return pl.pallas_call(
        pack_kernel,
        in_specs=in_vmem(4),
        out_specs=in_vmem(2),
        out_shape=[shape, shape],
        compiler_params=params(),
        name="pack",
    )(own, sib, weight, bias)


PART = 16


def convolve(window, taps):
    half = taps[KERNEL][None] + taps[0][None] * window[0:PART]
    for k in range(1, KERNEL):
        half = half + taps[k][None] * window[k : k + PART]
    half = half + half * jnp.tanh(half)
    return half.reshape(PART * GROUPS, LANE)


def load_lanes(refs, to_refs, sems):
    loads = []
    for i in range(GW // LW):
        at = pl.ds(i * LW, LW)
        loads.append(
            [pltpu.make_async_copy(ref.at[:, :, at], to.at[:, :, at], sems.at[k, i]) for k, (ref, to) in enumerate(zip(refs, to_refs))]
        )
        for load in loads[-1]:
            load.start()
    return loads


def states_kernel(
    core_ref, first_ref, own_hbm, sib_hbm, p0, p1, p2, p3, p4, ets_ref, eto_ref, out_hbm, before_hbm, w_ref, halo_ref,
    own_ref, sib_ref, packed_ref, act_ref, pieces_ref, before_ref, sems, load_sems,
):
    core = core_ref[0]
    place = lax.axis_index("y")
    loads = load_lanes((own_hbm, sib_hbm), (own_ref, sib_ref), load_sems)
    keep = jnp.where(place == 0, 1 - first_ref[0], 1).astype(F32)
    low = iota((1, GROUPS, LANE), 1) % 2 == 0
    kept = iota((1, GROUPS, LANE), 1) % 2 == core
    swap = lambda v: pltpu.roll(v, 1 + 6 * core, v.ndim - 2)
    for tile in range(GW // LANE):
        at = slice(tile * LANE, (tile + 1) * LANE)
        packs = [ref[:, at].astype(F32) for ref in (p0, p1, p2, p3)]
        for k, pack in enumerate(packs):
            source = lax.rem(place - k + 4, 4)
            for double in range(2):
                packed_ref[pl.ds(pl.multiple_of((source * 2 + double) * PACK, 8), PACK), :] = pack
        halves = [packed_ref[pl.ds(weight_row(m), GROUPS, stride=PACK), :] * 0.5 for m in range(2 * KERNEL + 2)]
        taps = [halves[k] + halves[k + KERNEL + 1] for k in range(KERNEL + 1)]
        for k, v in enumerate(taps):
            w_ref[k, :, at] = v
        before = packs[1] + jnp.where(place == 0, packs[2] + packs[3] + p4[:, at].astype(F32), 0.0)
        before = jnp.where(low, before.reshape(ENDS, GROUPS, LANE) * keep, 0.0)
        halo_ref[:, :, at] = before.astype(BF16)
        if tile % 2 == 0:
            for load in loads[tile // 2]:
                load.wait()

        def merged(rows, at=at):
            return jnp.where(kept, own_ref[rows, :, at].astype(F32), swap(sib_ref[rows, :, at].astype(F32)))

        def tokens(i, carry, tile=tile, taps=taps, merged=merged):
            window = merged(pl.ds(i * PART - (KERNEL - 1), PART + KERNEL - 1))
            act_ref[tile, pl.ds(pl.multiple_of(i * PART * GROUPS, PART * GROUPS), PART * GROUPS), :] = convolve(window, taps)
            return carry

        last = slice(TOK - (KERNEL - 1), TOK)
        between = jnp.where(core == 0, swap(own_ref[last, :, at].astype(F32)), sib_ref[last, :, at].astype(F32))
        window = jnp.concatenate([jnp.where(low, before, between), merged(slice(0, PART))], axis=0)
        act_ref[tile, 0 : PART * GROUPS, :] = convolve(window, taps)
        lax.fori_loop(1, TOK // PART, tokens, 0, unroll=True)

    own, sib = eto_ref[...], ets_ref[...]
    decay = [jnp.where(core == 0, own, sib), jnp.where(core == 0, sib, own)]
    d_last = decay[1][TOK:]
    d_chip = decay[0][TOK:] * d_last
    row = iota((8, LANE), 0)
    copies = []
    for i in range(4):
        of_group = lambda half, tile: act_ref[tile, pl.ds(2 * i + half, TOK, stride=GROUPS), :]
        b_t = [of_group(half, 8).T.astype(BF16) for half in range(2)]
        for j in range(4):
            states = []
            for half in range(2):
                carried = [
                    (of_group(half, tile) * widen(decay[half][:TOK], core * 16 + i * 32 + tile * 2)).astype(BF16)
                    for tile in (2 * j, 2 * j + 1)
                ]
                states.append(jnp.dot(b_t[half], jnp.concatenate(carried, axis=1), preferred_element_type=F32))
            for tile in range(2):
                lanes = slice(tile * LANE, (tile + 1) * LANE)
                head = core * 16 + i * 32 + (2 * j + tile) * 2
                hi, mid, bottom = split3(widen(d_chip, head))
                extra = jnp.where(row == 0, hi, jnp.where(row == 1, mid, jnp.where(row == 2, bottom, keep)))
                first = states[0][:, lanes]
                both = (first * widen(d_last, head)[0:1] + states[1][:, lanes]).astype(BF16)
                first = first.astype(BF16)
                for rows in range(2):
                    piece = (i * 8 + 2 * j + tile) * 2 + rows
                    before_ref[i, j, tile * 2 + rows] = first[rows * 64 : rows * 64 + 64]
                    pieces_ref[piece, 0:64] = both[rows * 64 : rows * 64 + 64]
                    pieces_ref[piece, 64:ROWS] = extra.astype(BF16)
        group = pl.ds(i * 16, 16)
        copies.append(pltpu.make_async_copy(pieces_ref.at[group], out_hbm.at[group], sems.at[0, i]))
        copies.append(pltpu.make_async_copy(before_ref.at[i], before_hbm.at[i], sems.at[1, i]))
        copies[-2].start()
        copies[-1].start()
    for copy in copies:
        copy.wait()


def chip_states(core, seg_first, own, sib, packs, et_sib, et_own):
    pieces = (CHUNKS, ROWS, LANE)
    before = (4, 4, 4, 64, LANE)
    return pl.pallas_call(
        states_kernel,
        in_specs=in_smem(2) + in_hbm(2) + in_vmem(7),
        out_specs=in_hbm(2) + in_vmem(2),
        out_shape=[
            hbm(pieces),
            hbm(before),
            jax.ShapeDtypeStruct((KERNEL + 1, GROUPS, GW), F32),
            jax.ShapeDtypeStruct((ENDS, GROUPS, GW), BF16),
        ],
        scratch_shapes=[
            pltpu.VMEM((TOK, GROUPS, GW), BF16),
            pltpu.VMEM((TOK, GROUPS, GW), BF16),
            pltpu.VMEM((GROUPS * PACK, LANE), F32),
            pltpu.VMEM((GW // LANE, TOK * GROUPS, LANE), F32),
            pltpu.VMEM(pieces, BF16),
            pltpu.VMEM(before, BF16),
            pltpu.SemaphoreType.DMA((2, 4)),
            pltpu.SemaphoreType.DMA((2, GW // LW)),
        ],
        compiler_params=params(20),
        name="chip_states",
    )(core, seg_first, from_hbm(own), from_hbm(sib), *packs, et_sib, et_own)


def act_kernel(
    core_ref, conv_hbm, sib_hbm, own_halo_ref, sib_halo_ref, own_w_ref, sib_w_ref, x_hbm, bc_hbm, done_ref,
    conv_ref, last_ref, act_ref, x_ref, bc_ref, sems, load_sems,
):
    done_ref[...] = jnp.zeros_like(done_ref)
    core = core_ref[0]
    last = pltpu.make_async_copy(sib_hbm.at[pl.ds(TOK - ENDS, ENDS)], last_ref, load_sems.at[1, 0])
    last.start()
    loads = load_lanes((conv_hbm,), (conv_ref,), load_sems)
    last.wait()
    low = iota((1, GROUPS, LANE), 1) % 2 == 0
    kept = iota((GROUPS, LANE), 0) % 2 == core
    for tile in range(GW // LANE):
        at = slice(tile * LANE, (tile + 1) * LANE)
        taps = [jnp.where(kept, own_w_ref[k, :, at], sib_w_ref[k, :, at]) for k in range(KERNEL + 1)]
        if tile % 2 == 0:
            loads[tile // 2][0].wait()

        def tokens(i, carry, at=at, tile=tile, taps=taps):
            window = conv_ref[pl.ds(i * PART - (KERNEL - 1), PART + KERNEL - 1), :, at].astype(F32)
            act_ref[tile, pl.ds(pl.multiple_of(i * PART * GROUPS, PART * GROUPS), PART * GROUPS), :] = convolve(window, taps)
            return carry

        halo = pltpu.roll(sib_halo_ref[:, :, at].astype(F32), 1, 1)
        halo = jnp.where(low, own_halo_ref[:, :, at].astype(F32), halo)
        halo = jnp.where(core == 0, halo, last_ref[:, :, at].astype(F32))
        window = jnp.concatenate([halo, conv_ref[0:PART, :, at].astype(F32)], axis=0)
        act_ref[tile, 0 : PART * GROUPS, :] = convolve(window, taps)
        lax.fori_loop(1, TOK // PART, tokens, 0, unroll=True)
    copies = []
    for g in range(GROUPS):
        for tile in range(GW // LANE):
            values = act_ref[tile, pl.ds(g, TOK, stride=GROUPS), :].astype(BF16)
            if tile < XW // LANE:
                x_ref[g, :, tile * LANE : (tile + 1) * LANE] = values
            else:
                bc_ref[g, :, tile * LANE - XW : (tile + 1) * LANE - XW] = values
        copies.append(pltpu.make_async_copy(x_ref.at[g], x_hbm.at[g], sems.at[0, g]))
        copies.append(pltpu.make_async_copy(bc_ref.at[g], bc_hbm.at[g], sems.at[1, g]))
        copies[-2].start()
        copies[-1].start()
    for copy in copies:
        copy.wait()


def activate(core, conv_input, sib, own_halo, sib_halo, own_weights, sib_weights):
    x, bc = (GROUPS, TOK, XW), (GROUPS, TOK, LW)
    return pl.pallas_call(
        act_kernel,
        in_specs=in_smem(1) + in_hbm(2) + in_vmem(4),
        out_specs=in_hbm(2) + in_vmem(1),
        out_shape=[hbm(x), hbm(bc), DONE],
        scratch_shapes=[
            pltpu.VMEM((TOK, GROUPS, GW), BF16),
            pltpu.VMEM((ENDS, GROUPS, GW), BF16),
            pltpu.VMEM((GW // LANE, TOK * GROUPS, LANE), F32),
            pltpu.VMEM(x, BF16),
            pltpu.VMEM(bc, BF16),
            pltpu.SemaphoreType.DMA((2, GROUPS)),
            pltpu.SemaphoreType.DMA((2, GW // LW)),
        ],
        compiler_params=params(18),
        cost_estimate=pl.CostEstimate(flops=20_000_000, bytes_accessed=8_000_000, transcendentals=1_400_000),
        name="activate",
    )(core, from_hbm(conv_input), from_hbm(sib), own_halo, sib_halo, own_weights, sib_weights)


def scan_kernel(chips, in_hbm, done_ref, out_hbm, in_ref, out_ref, sems):
    each = CHUNKS // chips
    parts = 4
    size = CHUNKS // parts
    spans = [pl.ds(k * size, size) for k in range(parts)]
    loads = [pltpu.make_async_copy(in_hbm.at[at], in_ref.at[at], sems.at[0, k]) for k, at in enumerate(spans)]
    stores = [pltpu.make_async_copy(out_ref.at[at], out_hbm.at[at], sems.at[1, k]) for k, at in enumerate(spans)]
    for load in loads:
        load.start()
    states = [jnp.zeros((64, LANE), F32) for _ in range(each)]
    for k in range(parts):
        loads[k].wait()
        for at in range(k * size, (k + 1) * size):
            i = at % each
            extra = in_ref[at, 64:ROWS].astype(F32)
            state = extra[3:4] * states[i]
            out_ref[at] = state.astype(BF16)
            states[i] = (extra[0:1] + extra[1:2] + extra[2:3]) * state + in_ref[at, 0:64].astype(F32)
        stores[k].start()
    for store in stores:
        store.wait()


def scan(chips, pieces, done):
    return pl.pallas_call(
        functools.partial(scan_kernel, chips),
        in_specs=in_hbm(1) + [pl.BlockSpec(memory_space=pl.ANY)],
        out_specs=in_hbm(1)[0],
        out_shape=hbm((CHUNKS, 64, LANE)),
        scratch_shapes=[
            pltpu.VMEM((CHUNKS, ROWS, LANE), BF16),
            pltpu.VMEM((CHUNKS, 64, LANE), BF16),
            pltpu.SemaphoreType.DMA((2, 4)),
        ],
        compiler_params=params(),
        name="scan",
    )(from_hbm(pieces), done)


def local_kernel(other, core_ref, len_ref, x_ref, bc_ref, tab_ref, before_ref, dts_ref, gate_ref, skip_ref, p_ref, q_ref, done_ref):
    core = core_ref[0]
    done_ref[...] = jnp.zeros_like(done_ref)
    group = (core + other) % 2 + 2 * pl.program_id(0)
    inner, after, since = (tab_ref[k] for k in range(3))
    d_before = jnp.where(core == 1, dts_ref[TOK:], 1.0)
    spread = lambda table, j: jnp.concatenate([widen(table, group * 16 + j * 4 + 2 * k) for k in range(2)], axis=1)
    b = bc_ref[0, :, :LANE]
    c = bc_ref[0, :, LANE:]
    scores = lax.dot_general(c, b, (((1,), (1,)), ((), ())), preferred_element_type=F32)
    causal = iota((TOK, TOK), 0) >= iota((TOK, TOK), 1)
    scores = jnp.where(causal, scores, 0.0).astype(BF16)
    live = iota((TOK, LW), 0) < len_ref[0] - head_place() * TOK
    for j in range(4):
        at = slice(j * LW, (j + 1) * LW)
        x = x_ref[0, :, at].astype(F32)
        scaled = (x * spread(inner, j)).astype(BF16)
        y = spread(after, j) * jnp.dot(scores, scaled, preferred_element_type=F32)
        before = jnp.concatenate(
            [jnp.concatenate([before_ref[0, j, tile * 2], before_ref[0, j, tile * 2 + 1]], axis=0) for tile in range(2)],
            axis=1,
        )
        grown = spread(since, j)
        y = y + grown * (core.astype(F32) * jnp.dot(c, before, preferred_element_type=F32))
        y = y + skip_ref[:, at] * x
        half = gate_ref[:, at].astype(F32) * 0.5
        silu = half + half * jnp.tanh(half)
        p_ref[0, :, at] = jnp.where(live, y * silu, 0.0).astype(BF16)
        q_ref[0, :, at] = jnp.where(live, grown * spread(d_before, j)[0:1] * silu, 0.0).astype(BF16)


def local(other, core, seg_length, x, bc, tables, before, d_sib, gate_input, skip):
    group = lambda i, s: (s[0] + other) % 2 + 2 * i
    out = hbm((4, TOK, XW))
    out_spec = pl.BlockSpec((1, TOK, XW), lambda i, s: (i, 0, 0))
    return pl.pallas_call(
        functools.partial(local_kernel, other),
        grid_spec=pltpu.PrefetchScalarGridSpec(
            num_scalar_prefetch=1,
            grid=(4,),
            in_specs=[
                pl.BlockSpec(memory_space=pltpu.SMEM),
                pl.BlockSpec((1, TOK, XW), lambda i, s: (group(i, s), 0, 0)),
                pl.BlockSpec((1, TOK, LW), lambda i, s: (group(i, s), 0, 0)),
                pl.BlockSpec((3, TOK, LANE), lambda i, s: (0, 0, 0)),
                pl.BlockSpec((1, 4, 4, 64, LANE), lambda i, s: (i, 0, 0, 0, 0)),
                pl.BlockSpec((TOK + 8, LANE), lambda i, s: (0, 0)),
                pl.BlockSpec((TOK, XW), lambda i, s: (0, group(i, s))),
                pl.BlockSpec((1, XW), lambda i, s: (0, group(i, s))),
            ],
            out_specs=[out_spec, out_spec, pl.BlockSpec((8, LANE), lambda i, s: (0, 0))],
        ),
        out_shape=[out, out, DONE],
        compiler_params=params(),
        cost_estimate=pl.CostEstimate(flops=400_000_000, bytes_accessed=8_000_000, transcendentals=600_000),
        name="local",
    )(core, seg_length, x, bc, tables, before, d_sib, gate_input, skip)


def finish_kernel(other, core_ref, p_ref, q_ref, bc_ref, state_ref, gain_ref, *rest):
    first = (core_ref[0] + other) % 2
    if other:
        _, out_ref, rows_ref, sems = rest
    else:
        _, out_ref, rows_ref, sems, p_to, q_to, state_to, load_sems = rest
        loads = []
        for i in range(4):
            group = pl.ds(i * 16, 16)
            loads.append(pltpu.make_async_copy(state_ref.at[group], state_to.at[group], load_sems.at[0, i]))
            loads.append(pltpu.make_async_copy(p_ref.at[i], p_to.at[i], load_sems.at[1, i]))
            loads.append(pltpu.make_async_copy(q_ref.at[i], q_to.at[i], load_sems.at[2, i]))
        for load in loads:
            load.start()
        p_ref, q_ref, state_ref = p_to, q_to, state_to
    copies = []
    for i in range(4):
        if not other and i % 2 == 0:
            for load in loads[3 * i : 3 * i + 6]:
                load.wait()
        c = bc_ref[first + 2 * i, :, LANE:]
        gated = []
        for tile in range(0, 8, 2):
            state = jnp.concatenate(
                [
                    jnp.concatenate([state_ref[i * 16 + (tile + k) * 2], state_ref[i * 16 + (tile + k) * 2 + 1]], axis=0)
                    for k in range(2)
                ],
                axis=1,
            )
            at = slice(tile * LANE, (tile + 2) * LANE)
            read = jnp.dot(c, state, preferred_element_type=F32)
            gated.append(p_ref[i, :, at].astype(F32) + read * q_ref[i, :, at].astype(F32))
        total = sum(jnp.sum(v * v, axis=1, keepdims=True) for v in gated)
        scale = lax.rsqrt(total / XW + EPSILON)
        for j, v in enumerate(gated):
            at = slice(j * LW, (j + 1) * LW)
            rows_ref[i, :, at] = (v * scale * gain_ref[first + 2 * i, :, at]).astype(BF16)
        to = out_ref.at[:, pl.ds(pl.multiple_of((first + 2 * i) * XW, XW), XW)]
        copies.append(pltpu.make_async_copy(rows_ref.at[i], to, sems.at[i]))
        copies[-1].start()
    for copy in copies:
        copy.wait()


def finish(other, core, p, q, bc, states, gain, out):
    if other:
        operands = [core, p, q, bc, states, gain, out]
        in_specs = in_smem(1) + in_vmem(5) + [pl.BlockSpec(memory_space=pl.ANY)]
        loaded = []
    else:
        operands = [core, from_hbm(p), from_hbm(q), bc, from_hbm(states), gain, out]
        in_specs = in_smem(1) + in_hbm(2) + in_vmem(1) + in_hbm(1) + in_vmem(1) + [pl.BlockSpec(memory_space=pl.ANY)]
        loaded = [
            pltpu.VMEM((4, TOK, XW), BF16),
            pltpu.VMEM((4, TOK, XW), BF16),
            pltpu.VMEM((CHUNKS, 64, LANE), BF16),
            pltpu.SemaphoreType.DMA((3, 4)),
        ]
    return pl.pallas_call(
        functools.partial(finish_kernel, other),
        in_specs=in_specs,
        out_specs=pl.BlockSpec(memory_space=pl.ANY),
        scratch_shapes=[pltpu.VMEM((4, TOK, XW), BF16), pltpu.SemaphoreType.DMA((4,))] + loaded,
        out_shape=jax.ShapeDtypeStruct((TOK, GROUPS * XW), BF16),
        input_output_aliases={6: 0} if other else {},
        compiler_params=params(),
        cost_estimate=pl.CostEstimate(flops=200_000_000, bytes_accessed=4_000_000, transcendentals=1000),
        name="finish",
    )(*operands)


def body(
    conv_input,
    gate_input,
    step_size,
    decay_log,
    conv_weight,
    conv_bias,
    skip_gain,
    norm_gain,
    seg_length,
    seg_first,
):
    segments = lax.axis_size("seq")
    in_segment = lax.axis_size("y") * lax.axis_size("core")
    chips = segments * in_segment // 2
    core = lax.axis_index("core").astype(jnp.int32).reshape(1)
    swap = [(0, 1), (1, 0)]

    sib = lax.ppermute(conv_input, "core", swap)
    tables, et_own, ends = start(seg_length, decay_log, step_size, conv_input)
    onward, tail = pack(ends, lax.ppermute(ends, "core", swap), conv_weight, conv_bias)
    packs = [
        lax.ppermute(tail if k > 1 else onward, CHIPS, [(c, (c + k) % chips) for c in range(chips)]) for k in range(1, 5)
    ]
    et_sib = lax.ppermute(et_own, "core", swap)

    pieces, before_own, weights, halo = chip_states(
        core, seg_first, conv_input, sib, [tail] + packs, et_sib, et_own
    )
    pieces = lax.all_to_all(pieces, CHIPS, 0, 0, tiled=True)
    before_oth = lax.ppermute(before_own, "core", swap[:1])
    halo_sib = lax.ppermute(halo, "core", swap)
    weights_sib = lax.ppermute(weights, "core", swap)
    x, bc, done = activate(core, conv_input, sib, halo, halo_sib, weights, weights_sib)

    skip = jnp.repeat(skip_gain, HEAD_DIM)[None]
    p_own, q_own, done_own = local(0, core, seg_length, x, bc, tables, before_own, et_sib, gate_input, skip)
    p_oth, q_oth, done_oth = local(1, core, seg_length, x, bc, tables, before_oth, et_sib, gate_input, skip)
    pieces, done = lax.optimization_barrier((pieces, done))
    states = lax.all_to_all(scan(chips, pieces, done), CHIPS, 0, 0, tiled=True)
    states, done = lax.optimization_barrier((states, done_own + done_oth))
    states_oth = lax.ppermute(states, "core", swap)
    gain = norm_gain.reshape(GROUPS, 1, XW)
    out = finish(0, core, p_own, q_own, bc, states, gain, done)
    return finish(1, core, p_oth, q_oth, bc, states_oth, gain, out)


def solution(mesh):
    segments, in_segment = mesh.devices.shape
    fine = Mesh(mesh.devices.reshape(segments, in_segment // 2, 2), AXES)
    tokens = P(AXES, None)
    return jax.shard_map(
        body,
        mesh=fine,
        in_specs=(
            P(AXES, None, None),
            tokens,
            tokens,
            tokens,
            P(None, ("y", "core"), None),
            P(("y", "core"), None),
            P(),
            P(),
            P("seq"),
            P("seq"),
        ),
        out_specs=tokens,
        check_vma=False,
    )
```

```python
import functools

import jax
import jax.numpy as jnp
from jax import lax
from jax.experimental import pallas as pl
from jax.experimental.pallas import tpu as pltpu
from jax.sharding import Mesh, PartitionSpec as P

HEAD_DIM = 64
KERNEL = 4
EPSILON = 1e-05
TOK = 128
GROUPS = 8
XW = 1024
GW = 1280
LANE = 128
LW = 256
CHUNKS = 64
ENDS = KERNEL - 1
PACK = 24
ROWS = 72
AXES = ("seq", "y", "core")
CHIPS = ("seq", "y")
F32 = jnp.float32
BF16 = jnp.bfloat16
DONE = jax.ShapeDtypeStruct((8, LANE), F32)


def iota(shape, dim):
    return lax.broadcasted_iota(jnp.int32, shape, dim)


def split3(v):
    hi = v.astype(BF16).astype(F32)
    mid = (v - hi).astype(BF16).astype(F32)
    return hi, mid, v - hi - mid


def widen(table, first):
    lane = iota(table.shape, 1) // HEAD_DIM + first
    return jnp.take_along_axis(table, lane, axis=1, mode="promise_in_bounds")


def head_place():
    return lax.axis_index("y") * 2 + lax.axis_index("core")


def in_vmem(count):
    return [pl.BlockSpec(memory_space=pltpu.VMEM)] * count


def in_hbm(count):
    return [pl.BlockSpec(memory_space=pltpu.HBM)] * count


def in_smem(count):
    return [pl.BlockSpec(memory_space=pltpu.SMEM)] * count


def hbm(shape):
    return pltpu.HBM(shape, BF16)


def from_hbm(value):
    return pltpu.with_memory_space_constraint(value, pltpu.HBM)


def params(mib=16):
    return pltpu.CompilerParams(vmem_limit_bytes=mib * 1024 * 1024)


def start_kernel(
    len_ref, decay_hbm, step_hbm, conv_hbm, tab_ref, et_ref, ends_ref, decay_ref, step_ref, rows_ref, sems
):
    first_row = len_ref[0] - head_place() * TOK
    copies = [
        pltpu.make_async_copy(decay_hbm, decay_ref, sems.at[0]),
        pltpu.make_async_copy(step_hbm, step_ref, sems.at[1]),
    ]
    for k in range(ENDS):
        row = jnp.clip(first_row - ENDS + k, 0, TOK - 1)
        copies.append(pltpu.make_async_copy(conv_hbm.at[pl.ds(row, 1)], rows_ref.at[pl.ds(k, 1)], sems.at[2 + k]))
    copies.append(pltpu.make_async_copy(conv_hbm.at[pl.ds(TOK - ENDS, ENDS)], rows_ref.at[pl.ds(ENDS, ENDS)], sems.at[2 + ENDS]))
    for copy in copies:
        copy.start()
    for copy in copies:
        copy.wait()
    for k in range(ENDS):
        row = first_row - ENDS + k
        inside = jnp.where((row >= 0) & (row < TOK), 1.0, 0.0)
        ends_ref[k] = (rows_ref[k].astype(F32) * inside).astype(BF16)
        ends_ref[ENDS + k] = rows_ref[ENDS + k]
    live = iota((TOK, LANE), 0) < first_row
    log_rate = jnp.where(live, decay_ref[...].astype(F32), 0.0)
    gain = jnp.where(live, step_ref[...].astype(F32), 0.0)
    upto = jnp.where(iota((TOK, TOK), 0) >= iota((TOK, TOK), 1), 1.0, 0.0).astype(BF16)
    running = jnp.dot(upto, log_rate.astype(BF16), preferred_element_type=F32)
    middle = running[TOK // 2 - 1 : TOK // 2]
    total = running[TOK - 1 : TOK]
    tab_ref[0] = jnp.exp(middle - running) * gain
    tab_ref[1] = jnp.exp(running - middle)
    tab_ref[2] = jnp.exp(running)
    et_ref[0:TOK] = jnp.exp(total - running) * gain
    et_ref[TOK:] = jnp.broadcast_to(jnp.exp(total), (8, LANE))


def start(seg_length, decay_log, step_size, conv_input):
    return pl.pallas_call(
        start_kernel,
        in_specs=in_smem(1) + in_hbm(3),
        out_specs=in_vmem(3),
        out_shape=[
            jax.ShapeDtypeStruct((3, TOK, LANE), F32),
            jax.ShapeDtypeStruct((TOK + 8, LANE), F32),
            jax.ShapeDtypeStruct((2 * ENDS, GROUPS, GW), BF16),
        ],
        scratch_shapes=[
            pltpu.VMEM((TOK, LANE), BF16),
            pltpu.VMEM((TOK, LANE), BF16),
            pltpu.VMEM((2 * ENDS, GROUPS, GW), BF16),
            pltpu.SemaphoreType.DMA((3 + ENDS,)),
        ],
        compiler_params=params(),
        name="start",
    )(seg_length, from_hbm(decay_log), from_hbm(step_size), from_hbm(conv_input))


def weight_row(m):
    return m // 4 * 8 + m % 4 * 2 + 1


def pack_kernel(own_ref, sib_ref, weight_ref, bias_ref, on_ref, tail_ref):
    place, core = lax.axis_index("y"), lax.axis_index("core")
    row = iota((GROUPS, LANE), 0)
    even = row % 2 == 0
    for tile in range(GW // LANE):
        at = slice(tile * LANE, (tile + 1) * LANE)
        rows = [weight_ref[k, :, at] for k in range(KERNEL)] + [bias_ref[:, at]]
        rows = rows + [v - v.astype(BF16).astype(F32) for v in rows]
        for k in range(ENDS):
            fill = jnp.zeros((GROUPS, LANE), F32)
            for m in range(4 * k, min(4 * k + 4, len(rows))):
                fill = jnp.where(row == weight_row(m % 4), rows[m], fill)
            tail = own_ref[k, :, at].astype(F32) + sib_ref[k, :, at].astype(F32)
            last = jnp.where(core == 0, sib_ref[ENDS + k, :, at].astype(F32), own_ref[ENDS + k, :, at].astype(F32))
            onward = jnp.where(place == lax.axis_size("y") - 1, tail, last)
            for value, ref in ((onward, on_ref), (tail, tail_ref)):
                value = jnp.where(core == 0, value, pltpu.roll(value, GROUPS - 1, 0))
                ref[k * 8 : k * 8 + 8, at] = jnp.where(even, value, fill).astype(BF16)


def pack(own, sib, weight, bias):
    shape = jax.ShapeDtypeStruct((PACK, GW), BF16)
    return pl.pallas_call(
        pack_kernel,
        in_specs=in_vmem(4),
        out_specs=in_vmem(2),
        out_shape=[shape, shape],
        compiler_params=params(),
        name="pack",
    )(own, sib, weight, bias)


PART = 16


def convolve(window, taps):
    half = taps[KERNEL][None] + taps[0][None] * window[0:PART]
    for k in range(1, KERNEL):
        half = half + taps[k][None] * window[k : k + PART]
    half = half + half * jnp.tanh(half)
    return half.reshape(PART * GROUPS, LANE)


def load_lanes(refs, to_refs, sems):
    loads = []
    for i in range(GW // LW):
        at = pl.ds(i * LW, LW)
        loads.append(
            [pltpu.make_async_copy(ref.at[:, :, at], to.at[:, :, at], sems.at[k, i]) for k, (ref, to) in enumerate(zip(refs, to_refs))]
        )
        for load in loads[-1]:
            load.start()
    return loads


def states_kernel(
    core_ref, first_ref, own_hbm, sib_hbm, p0, p1, p2, p3, p4, ets_ref, eto_ref, out_hbm, before_hbm, w_ref, halo_ref,
    own_ref, sib_ref, packed_ref, act_ref, pieces_ref, before_ref, sems, load_sems,
):
    core = core_ref[0]
    place = lax.axis_index("y")
    loads = load_lanes((own_hbm, sib_hbm), (own_ref, sib_ref), load_sems)
    keep = jnp.where(place == 0, 1 - first_ref[0], 1).astype(F32)
    low = iota((1, GROUPS, LANE), 1) % 2 == 0
    kept = iota((1, GROUPS, LANE), 1) % 2 == core
    swap = lambda v: pltpu.roll(v, 1 + 6 * core, v.ndim - 2)
    for tile in range(GW // LANE):
        at = slice(tile * LANE, (tile + 1) * LANE)
        packs = [ref[:, at].astype(F32) for ref in (p0, p1, p2, p3)]
        for k, pack in enumerate(packs):
            source = lax.rem(place - k + 4, 4)
            for double in range(2):
                packed_ref[pl.ds(pl.multiple_of((source * 2 + double) * PACK, 8), PACK), :] = pack
        halves = [packed_ref[pl.ds(weight_row(m), GROUPS, stride=PACK), :] * 0.5 for m in range(2 * KERNEL + 2)]
        taps = [halves[k] + halves[k + KERNEL + 1] for k in range(KERNEL + 1)]
        for k, v in enumerate(taps):
            w_ref[k, :, at] = v
        before = packs[1] + jnp.where(place == 0, packs[2] + packs[3] + p4[:, at].astype(F32), 0.0)
        before = jnp.where(low, before.reshape(ENDS, GROUPS, LANE) * keep, 0.0)
        halo_ref[:, :, at] = before.astype(BF16)
        if tile % 2 == 0:
            for load in loads[tile // 2]:
                load.wait()

        def merged(rows, at=at):
            return jnp.where(kept, own_ref[rows, :, at].astype(F32), swap(sib_ref[rows, :, at].astype(F32)))

        def tokens(i, carry, tile=tile, taps=taps, merged=merged):
            window = merged(pl.ds(i * PART - (KERNEL - 1), PART + KERNEL - 1))
            act_ref[tile, pl.ds(pl.multiple_of(i * PART * GROUPS, PART * GROUPS), PART * GROUPS), :] = convolve(window, taps)
            return carry

        last = slice(TOK - (KERNEL - 1), TOK)
        between = jnp.where(core == 0, swap(own_ref[last, :, at].astype(F32)), sib_ref[last, :, at].astype(F32))
        window = jnp.concatenate([jnp.where(low, before, between), merged(slice(0, PART))], axis=0)
        act_ref[tile, 0 : PART * GROUPS, :] = convolve(window, taps)
        lax.fori_loop(1, TOK // PART, tokens, 0, unroll=True)

    own, sib = eto_ref[...], ets_ref[...]
    decay = [jnp.where(core == 0, own, sib), jnp.where(core == 0, sib, own)]
    d_last = decay[1][TOK:]
    d_chip = decay[0][TOK:] * d_last
    row = iota((8, LANE), 0)
    copies = []
    for i in range(4):
        of_group = lambda half, tile: act_ref[tile, pl.ds(2 * i + half, TOK, stride=GROUPS), :]
        b_t = [of_group(half, 8).T.astype(BF16) for half in range(2)]
        for j in range(4):
            states = []
            for half in range(2):
                carried = [
                    (of_group(half, tile) * widen(decay[half][:TOK], core * 16 + i * 32 + tile * 2)).astype(BF16)
                    for tile in (2 * j, 2 * j + 1)
                ]
                states.append(jnp.dot(b_t[half], jnp.concatenate(carried, axis=1), preferred_element_type=F32))
            for tile in range(2):
                lanes = slice(tile * LANE, (tile + 1) * LANE)
                head = core * 16 + i * 32 + (2 * j + tile) * 2
                hi, mid, bottom = split3(widen(d_chip, head))
                extra = jnp.where(row == 0, hi, jnp.where(row == 1, mid, jnp.where(row == 2, bottom, keep)))
                first = states[0][:, lanes]
                both = (first * widen(d_last, head)[0:1] + states[1][:, lanes]).astype(BF16)
                first = first.astype(BF16)
                for rows in range(2):
                    piece = (i * 8 + 2 * j + tile) * 2 + rows
                    before_ref[i, j, tile * 2 + rows] = first[rows * 64 : rows * 64 + 64]
                    pieces_ref[piece, 0:64] = both[rows * 64 : rows * 64 + 64]
                    pieces_ref[piece, 64:ROWS] = extra.astype(BF16)
        group = pl.ds(i * 16, 16)
        copies.append(pltpu.make_async_copy(pieces_ref.at[group], out_hbm.at[group], sems.at[0, i]))
        copies.append(pltpu.make_async_copy(before_ref.at[i], before_hbm.at[i], sems.at[1, i]))
        copies[-2].start()
        copies[-1].start()
    for copy in copies:
        copy.wait()


def chip_states(core, seg_first, own, sib, packs, et_sib, et_own):
    pieces = (CHUNKS, ROWS, LANE)
    before = (4, 4, 4, 64, LANE)
    return pl.pallas_call(
        states_kernel,
        in_specs=in_smem(2) + in_hbm(2) + in_vmem(7),
        out_specs=in_hbm(2) + in_vmem(2),
        out_shape=[
            hbm(pieces),
            hbm(before),
            jax.ShapeDtypeStruct((KERNEL + 1, GROUPS, GW), F32),
            jax.ShapeDtypeStruct((ENDS, GROUPS, GW), BF16),
        ],
        scratch_shapes=[
            pltpu.VMEM((TOK, GROUPS, GW), BF16),
            pltpu.VMEM((TOK, GROUPS, GW), BF16),
            pltpu.VMEM((GROUPS * PACK, LANE), F32),
            pltpu.VMEM((GW // LANE, TOK * GROUPS, LANE), F32),
            pltpu.VMEM(pieces, BF16),
            pltpu.VMEM(before, BF16),
            pltpu.SemaphoreType.DMA((2, 4)),
            pltpu.SemaphoreType.DMA((2, GW // LW)),
        ],
        compiler_params=params(20),
        name="chip_states",
    )(core, seg_first, from_hbm(own), from_hbm(sib), *packs, et_sib, et_own)


def act_kernel(
    core_ref, conv_hbm, sib_hbm, own_halo_ref, sib_halo_ref, own_w_ref, sib_w_ref, x_hbm, bc_hbm, done_ref,
    conv_ref, last_ref, act_ref, x_ref, bc_ref, sems, load_sems,
):
    done_ref[...] = jnp.zeros_like(done_ref)
    core = core_ref[0]
    last = pltpu.make_async_copy(sib_hbm.at[pl.ds(TOK - ENDS, ENDS)], last_ref, load_sems.at[1, 0])
    last.start()
    loads = load_lanes((conv_hbm,), (conv_ref,), load_sems)
    last.wait()
    low = iota((1, GROUPS, LANE), 1) % 2 == 0
    kept = iota((GROUPS, LANE), 0) % 2 == core
    for tile in range(GW // LANE):
        at = slice(tile * LANE, (tile + 1) * LANE)
        taps = [jnp.where(kept, own_w_ref[k, :, at], sib_w_ref[k, :, at]) for k in range(KERNEL + 1)]
        if tile % 2 == 0:
            loads[tile // 2][0].wait()

        def tokens(i, carry, at=at, tile=tile, taps=taps):
            window = conv_ref[pl.ds(i * PART - (KERNEL - 1), PART + KERNEL - 1), :, at].astype(F32)
            act_ref[tile, pl.ds(pl.multiple_of(i * PART * GROUPS, PART * GROUPS), PART * GROUPS), :] = convolve(window, taps)
            return carry

        halo = pltpu.roll(sib_halo_ref[:, :, at].astype(F32), 1, 1)
        halo = jnp.where(low, own_halo_ref[:, :, at].astype(F32), halo)
        halo = jnp.where(core == 0, halo, last_ref[:, :, at].astype(F32))
        window = jnp.concatenate([halo, conv_ref[0:PART, :, at].astype(F32)], axis=0)
        act_ref[tile, 0 : PART * GROUPS, :] = convolve(window, taps)
        lax.fori_loop(1, TOK // PART, tokens, 0, unroll=True)
    copies = []
    for g in range(GROUPS):
        for tile in range(GW // LANE):
            values = act_ref[tile, pl.ds(g, TOK, stride=GROUPS), :].astype(BF16)
            if tile < XW // LANE:
                x_ref[g, :, tile * LANE : (tile + 1) * LANE] = values
            else:
                bc_ref[g, :, tile * LANE - XW : (tile + 1) * LANE - XW] = values
        copies.append(pltpu.make_async_copy(x_ref.at[g], x_hbm.at[g], sems.at[0, g]))
        copies.append(pltpu.make_async_copy(bc_ref.at[g], bc_hbm.at[g], sems.at[1, g]))
        copies[-2].start()
        copies[-1].start()
    for copy in copies:
        copy.wait()


def activate(core, conv_input, sib, own_halo, sib_halo, own_weights, sib_weights):
    x, bc = (GROUPS, TOK, XW), (GROUPS, TOK, LW)
    return pl.pallas_call(
        act_kernel,
        in_specs=in_smem(1) + in_hbm(2) + in_vmem(4),
        out_specs=in_hbm(2) + in_vmem(1),
        out_shape=[hbm(x), hbm(bc), DONE],
        scratch_shapes=[
            pltpu.VMEM((TOK, GROUPS, GW), BF16),
            pltpu.VMEM((ENDS, GROUPS, GW), BF16),
            pltpu.VMEM((GW // LANE, TOK * GROUPS, LANE), F32),
            pltpu.VMEM(x, BF16),
            pltpu.VMEM(bc, BF16),
            pltpu.SemaphoreType.DMA((2, GROUPS)),
            pltpu.SemaphoreType.DMA((2, GW // LW)),
        ],
        compiler_params=params(18),
        cost_estimate=pl.CostEstimate(flops=20_000_000, bytes_accessed=8_000_000, transcendentals=1_400_000),
        name="activate",
    )(core, from_hbm(conv_input), from_hbm(sib), own_halo, sib_halo, own_weights, sib_weights)


def scan_kernel(chips, in_ref, done_ref, out_hbm, out_ref, sems):
    each = CHUNKS // chips
    parts = 4
    size = CHUNKS // parts
    states = [jnp.zeros((64, LANE), F32) for _ in range(each)]
    stores = []
    for k in range(parts):
        for at in range(k * size, (k + 1) * size):
            i = at % each
            extra = in_ref[at, 64:ROWS].astype(F32)
            state = extra[3:4] * states[i]
            out_ref[at] = state.astype(BF16)
            states[i] = (extra[0:1] + extra[1:2] + extra[2:3]) * state + in_ref[at, 0:64].astype(F32)
        span = pl.ds(k * size, size)
        stores.append(pltpu.make_async_copy(out_ref.at[span], out_hbm.at[span], sems.at[k]))
        stores[-1].start()
    for store in stores:
        store.wait()


def scan(chips, pieces, done):
    return pl.pallas_call(
        functools.partial(scan_kernel, chips),
        in_specs=in_vmem(1) + [pl.BlockSpec(memory_space=pl.ANY)],
        out_specs=in_hbm(1)[0],
        out_shape=hbm((CHUNKS, 64, LANE)),
        scratch_shapes=[pltpu.VMEM((CHUNKS, 64, LANE), BF16), pltpu.SemaphoreType.DMA((4,))],
        compiler_params=params(4),
        name="scan",
    )(pieces, done)


def local_kernel(other, core_ref, len_ref, x_ref, bc_ref, tab_ref, before_ref, dts_ref, gate_ref, skip_ref, p_ref, q_ref, done_ref):
    core = core_ref[0]
    done_ref[...] = jnp.zeros_like(done_ref)
    group = (core + other) % 2 + 2 * pl.program_id(0)
    inner, after, since = (tab_ref[k] for k in range(3))
    since = since * jnp.where(core == 1, dts_ref[TOK : TOK + 1], 1.0)
    rise = jnp.where(core == 1, tab_ref[2, TOK // 2 - 1 : TOK // 2], 0.0)
    rise = jnp.broadcast_to(rise, (8, LANE))
    spread = lambda table, j: jnp.concatenate([widen(table, group * 16 + j * 4 + 2 * k) for k in range(2)], axis=1)
    b = bc_ref[0, :, :LANE]
    c = bc_ref[0, :, LANE:]
    scores = lax.dot_general(c, b, (((1,), (1,)), ((), ())), preferred_element_type=F32)
    causal = iota((TOK, TOK), 0) >= iota((TOK, TOK), 1)
    scores = jnp.where(causal, scores, 0.0).astype(BF16)
    live = iota((TOK, LW), 0) < len_ref[0] - head_place() * TOK
    for j in range(4):
        at = slice(j * LW, (j + 1) * LW)
        x = x_ref[0, :, at].astype(F32)
        scaled = (x * spread(inner, j)).astype(BF16)
        before = jnp.concatenate(
            [jnp.concatenate([before_ref[0, j, tile * 2], before_ref[0, j, tile * 2 + 1]], axis=0) for tile in range(2)],
            axis=1,
        )
        read = jnp.dot(scores, scaled, preferred_element_type=F32)
        read = read + spread(rise, j)[0:1] * jnp.dot(c, before, preferred_element_type=F32)
        y = spread(after, j) * read + skip_ref[:, at] * x
        half = gate_ref[:, at].astype(F32) * 0.5
        silu = half + half * jnp.tanh(half)
        p_ref[0, :, at] = jnp.where(live, y * silu, 0.0).astype(BF16)
        q_ref[0, :, at] = jnp.where(live, spread(since, j) * silu, 0.0).astype(BF16)


def local(other, core, seg_length, x, bc, tables, before, d_sib, gate_input, skip):
    group = lambda i, s: (s[0] + other) % 2 + 2 * i
    out = hbm((4, TOK, XW))
    out_spec = pl.BlockSpec((1, TOK, XW), lambda i, s: (i, 0, 0))
    return pl.pallas_call(
        functools.partial(local_kernel, other),
        grid_spec=pltpu.PrefetchScalarGridSpec(
            num_scalar_prefetch=1,
            grid=(4,),
            in_specs=[
                pl.BlockSpec(memory_space=pltpu.SMEM),
                pl.BlockSpec((1, TOK, XW), lambda i, s: (group(i, s), 0, 0)),
                pl.BlockSpec((1, TOK, LW), lambda i, s: (group(i, s), 0, 0)),
                pl.BlockSpec((3, TOK, LANE), lambda i, s: (0, 0, 0)),
                pl.BlockSpec((1, 4, 4, 64, LANE), lambda i, s: (i, 0, 0, 0, 0)),
                pl.BlockSpec((TOK + 8, LANE), lambda i, s: (0, 0)),
                pl.BlockSpec((TOK, XW), lambda i, s: (0, group(i, s))),
                pl.BlockSpec((1, XW), lambda i, s: (0, group(i, s))),
            ],
            out_specs=[out_spec, out_spec, pl.BlockSpec((8, LANE), lambda i, s: (0, 0))],
        ),
        out_shape=[out, out, DONE],
        compiler_params=params(),
        cost_estimate=pl.CostEstimate(flops=400_000_000, bytes_accessed=8_000_000, transcendentals=600_000),
        name="local",
    )(core, seg_length, from_hbm(x), from_hbm(bc), tables, from_hbm(before), d_sib, from_hbm(gate_input), skip)


def finish_kernel(other, core_ref, p_ref, q_ref, bc_ref, state_ref, gain_ref, *rest):
    first = (core_ref[0] + other) % 2
    if other:
        _, out_ref, rows_ref, sems = rest
    else:
        _, out_ref, rows_ref, sems, p_to, q_to, state_to, load_sems = rest
        loads = []
        for i in range(4):
            group = pl.ds(i * 16, 16)
            loads.append(pltpu.make_async_copy(state_ref.at[group], state_to.at[group], load_sems.at[0, i]))
            loads.append(pltpu.make_async_copy(p_ref.at[i], p_to.at[i], load_sems.at[1, i]))
            loads.append(pltpu.make_async_copy(q_ref.at[i], q_to.at[i], load_sems.at[2, i]))
        for load in loads:
            load.start()
        p_ref, q_ref, state_ref = p_to, q_to, state_to
    copies = []
    for i in range(4):
        if not other and i % 2 == 0:
            for load in loads[3 * i : 3 * i + 6]:
                load.wait()
        c = bc_ref[first + 2 * i, :, LANE:]
        gated = []
        for tile in range(0, 8, 2):
            state = jnp.concatenate(
                [
                    jnp.concatenate([state_ref[i * 16 + (tile + k) * 2], state_ref[i * 16 + (tile + k) * 2 + 1]], axis=0)
                    for k in range(2)
                ],
                axis=1,
            )
            at = slice(tile * LANE, (tile + 2) * LANE)
            read = jnp.dot(c, state, preferred_element_type=F32)
            gated.append(p_ref[i, :, at].astype(F32) + read * q_ref[i, :, at].astype(F32))
        total = sum(jnp.sum(v * v, axis=1, keepdims=True) for v in gated)
        scale = lax.rsqrt(total / XW + EPSILON)
        for j, v in enumerate(gated):
            at = slice(j * LW, (j + 1) * LW)
            rows_ref[i, :, at] = (v * scale * gain_ref[first + 2 * i, :, at]).astype(BF16)
        to = out_ref.at[:, pl.ds(pl.multiple_of((first + 2 * i) * XW, XW), XW)]
        copies.append(pltpu.make_async_copy(rows_ref.at[i], to, sems.at[i]))
        copies[-1].start()
    for copy in copies:
        copy.wait()


def finish(other, core, p, q, bc, states, gain, out):
    if other:
        operands = [core, p, q, bc, states, gain, out]
        in_specs = in_smem(1) + in_vmem(5) + [pl.BlockSpec(memory_space=pl.ANY)]
        loaded = []
    else:
        operands = [core, from_hbm(p), from_hbm(q), bc, from_hbm(states), gain, out]
        in_specs = in_smem(1) + in_hbm(2) + in_vmem(1) + in_hbm(1) + in_vmem(1) + [pl.BlockSpec(memory_space=pl.ANY)]
        loaded = [
            pltpu.VMEM((4, TOK, XW), BF16),
            pltpu.VMEM((4, TOK, XW), BF16),
            pltpu.VMEM((CHUNKS, 64, LANE), BF16),
            pltpu.SemaphoreType.DMA((3, 4)),
        ]
    return pl.pallas_call(
        functools.partial(finish_kernel, other),
        in_specs=in_specs,
        out_specs=pl.BlockSpec(memory_space=pl.ANY),
        scratch_shapes=[pltpu.VMEM((4, TOK, XW), BF16), pltpu.SemaphoreType.DMA((4,))] + loaded,
        out_shape=jax.ShapeDtypeStruct((TOK, GROUPS * XW), BF16),
        input_output_aliases={6: 0} if other else {},
        compiler_params=params(),
        cost_estimate=pl.CostEstimate(flops=200_000_000, bytes_accessed=4_000_000, transcendentals=1000),
        name="finish",
    )(*operands)


def body(
    conv_input,
    gate_input,
    step_size,
    decay_log,
    conv_weight,
    conv_bias,
    skip_gain,
    norm_gain,
    seg_length,
    seg_first,
):
    segments = lax.axis_size("seq")
    in_segment = lax.axis_size("y") * lax.axis_size("core")
    chips = segments * in_segment // 2
    core = lax.axis_index("core").astype(jnp.int32).reshape(1)
    swap = [(0, 1), (1, 0)]

    sib = lax.ppermute(conv_input, "core", swap)
    tables, et_own, ends = start(seg_length, decay_log, step_size, conv_input)
    onward, tail = pack(ends, lax.ppermute(ends, "core", swap), conv_weight, conv_bias)
    packs = [
        lax.ppermute(tail if k > 1 else onward, CHIPS, [(c, (c + k) % chips) for c in range(chips)]) for k in range(1, 5)
    ]
    et_sib = lax.ppermute(et_own, "core", swap)

    pieces, before_own, weights, halo = chip_states(
        core, seg_first, conv_input, sib, [tail] + packs, et_sib, et_own
    )
    pieces = lax.all_to_all(pieces, CHIPS, 0, 0, tiled=True)
    before_oth = lax.ppermute(before_own, "core", swap[:1])
    halo_sib = lax.ppermute(halo, "core", swap)
    weights_sib = lax.ppermute(weights, "core", swap)
    x, bc, done = activate(core, conv_input, sib, halo, halo_sib, weights, weights_sib)

    skip = jnp.repeat(skip_gain, HEAD_DIM)[None]
    p_own, q_own, done_own = local(0, core, seg_length, x, bc, tables, before_own, et_sib, gate_input, skip)
    p_oth, q_oth, done_oth = local(1, core, seg_length, x, bc, tables, before_oth, et_sib, gate_input, skip)
    states = lax.all_to_all(scan(chips, pieces, done), CHIPS, 0, 0, tiled=True)
    states, done = lax.optimization_barrier((states, done_own + done_oth))
    states_oth = lax.ppermute(states, "core", swap)
    gain = norm_gain.reshape(GROUPS, 1, XW)
    out = finish(0, core, p_own, q_own, bc, states, gain, done)
    return finish(1, core, p_oth, q_oth, bc, states_oth, gain, out)


def solution(mesh):
    segments, in_segment = mesh.devices.shape
    fine = Mesh(mesh.devices.reshape(segments, in_segment // 2, 2), AXES)
    tokens = P(AXES, None)
    return jax.shard_map(
        body,
        mesh=fine,
        in_specs=(
            P(AXES, None, None),
            tokens,
            tokens,
            tokens,
            P(None, ("y", "core"), None),
            P(("y", "core"), None),
            P(),
            P(),
            P("seq"),
            P("seq"),
        ),
        out_specs=tokens,
        check_vma=False,
    )
```

```python
import functools

import jax
import jax.numpy as jnp
from jax import lax
from jax.experimental import pallas as pl
from jax.experimental.pallas import tpu as pltpu
from jax.sharding import Mesh, PartitionSpec as P

HEAD_DIM = 64
KERNEL = 4
EPSILON = 1e-05
TOK = 128
GROUPS = 8
XW = 1024
GW = 1280
LANE = 128
LW = 256
CHUNKS = 64
ENDS = KERNEL - 1
PACK = 24
ROWS = 72
AXES = ("seq", "y", "core")
CHIPS = ("seq", "y")
F32 = jnp.float32
BF16 = jnp.bfloat16
DONE = jax.ShapeDtypeStruct((8, LANE), F32)


def iota(shape, dim):
    return lax.broadcasted_iota(jnp.int32, shape, dim)


def split3(v):
    hi = v.astype(BF16).astype(F32)
    mid = (v - hi).astype(BF16).astype(F32)
    return hi, mid, v - hi - mid


def widen(table, first):
    lane = iota(table.shape, 1) // HEAD_DIM + first
    return jnp.take_along_axis(table, lane, axis=1, mode="promise_in_bounds")


def head_place():
    return lax.axis_index("y") * 2 + lax.axis_index("core")


def in_vmem(count):
    return [pl.BlockSpec(memory_space=pltpu.VMEM)] * count


def in_hbm(count):
    return [pl.BlockSpec(memory_space=pltpu.HBM)] * count


def in_smem(count):
    return [pl.BlockSpec(memory_space=pltpu.SMEM)] * count


def hbm(shape):
    return pltpu.HBM(shape, BF16)


def from_hbm(value):
    return pltpu.with_memory_space_constraint(value, pltpu.HBM)


def params(mib=16):
    return pltpu.CompilerParams(vmem_limit_bytes=mib * 1024 * 1024)


def start_kernel(
    len_ref, decay_hbm, step_hbm, conv_hbm, tab_ref, et_ref, ends_ref, decay_ref, step_ref, rows_ref, sems
):
    first_row = len_ref[0] - head_place() * TOK
    copies = [
        pltpu.make_async_copy(decay_hbm, decay_ref, sems.at[0]),
        pltpu.make_async_copy(step_hbm, step_ref, sems.at[1]),
    ]
    for k in range(ENDS):
        row = jnp.clip(first_row - ENDS + k, 0, TOK - 1)
        copies.append(pltpu.make_async_copy(conv_hbm.at[pl.ds(row, 1)], rows_ref.at[pl.ds(k, 1)], sems.at[2 + k]))
    copies.append(pltpu.make_async_copy(conv_hbm.at[pl.ds(TOK - ENDS, ENDS)], rows_ref.at[pl.ds(ENDS, ENDS)], sems.at[2 + ENDS]))
    for copy in copies:
        copy.start()
    for copy in copies:
        copy.wait()
    for k in range(ENDS):
        row = first_row - ENDS + k
        inside = jnp.where((row >= 0) & (row < TOK), 1.0, 0.0)
        ends_ref[k] = (rows_ref[k].astype(F32) * inside).astype(BF16)
        ends_ref[ENDS + k] = rows_ref[ENDS + k]
    live = iota((TOK, LANE), 0) < first_row
    log_rate = jnp.where(live, decay_ref[...].astype(F32), 0.0)
    gain = jnp.where(live, step_ref[...].astype(F32), 0.0)
    upto = jnp.where(iota((TOK, TOK), 0) >= iota((TOK, TOK), 1), 1.0, 0.0).astype(BF16)
    running = jnp.dot(upto, log_rate.astype(BF16), preferred_element_type=F32)
    middle = running[TOK // 2 - 1 : TOK // 2]
    total = running[TOK - 1 : TOK]
    tab_ref[0] = jnp.exp(middle - running) * gain
    tab_ref[1] = jnp.exp(running - middle)
    tab_ref[2] = jnp.exp(running)
    et_ref[0:TOK] = jnp.exp(total - running) * gain
    et_ref[TOK:] = jnp.broadcast_to(jnp.exp(total), (8, LANE))


def start(seg_length, decay_log, step_size, conv_input):
    return pl.pallas_call(
        start_kernel,
        in_specs=in_smem(1) + in_hbm(3),
        out_specs=in_vmem(3),
        out_shape=[
            jax.ShapeDtypeStruct((3, TOK, LANE), F32),
            jax.ShapeDtypeStruct((TOK + 8, LANE), F32),
            jax.ShapeDtypeStruct((2 * ENDS, GROUPS, GW), BF16),
        ],
        scratch_shapes=[
            pltpu.VMEM((TOK, LANE), BF16),
            pltpu.VMEM((TOK, LANE), BF16),
            pltpu.VMEM((2 * ENDS, GROUPS, GW), BF16),
            pltpu.SemaphoreType.DMA((3 + ENDS,)),
        ],
        compiler_params=params(),
        name="start",
    )(seg_length, from_hbm(decay_log), from_hbm(step_size), from_hbm(conv_input))


def weight_row(m):
    return m // 4 * 8 + m % 4 * 2 + 1


def pack_kernel(own_ref, sib_ref, weight_ref, bias_ref, on_ref, tail_ref):
    place, core = lax.axis_index("y"), lax.axis_index("core")
    row = iota((GROUPS, LANE), 0)
    even = row % 2 == 0
    for tile in range(GW // LANE):
        at = slice(tile * LANE, (tile + 1) * LANE)
        rows = [weight_ref[k, :, at] for k in range(KERNEL)] + [bias_ref[:, at]]
        rows = rows + [v - v.astype(BF16).astype(F32) for v in rows]
        for k in range(ENDS):
            fill = jnp.zeros((GROUPS, LANE), F32)
            for m in range(4 * k, min(4 * k + 4, len(rows))):
                fill = jnp.where(row == weight_row(m % 4), rows[m], fill)
            tail = own_ref[k, :, at].astype(F32) + sib_ref[k, :, at].astype(F32)
            last = jnp.where(core == 0, sib_ref[ENDS + k, :, at].astype(F32), own_ref[ENDS + k, :, at].astype(F32))
            onward = jnp.where(place == lax.axis_size("y") - 1, tail, last)
            for value, ref in ((onward, on_ref), (tail, tail_ref)):
                value = jnp.where(core == 0, value, pltpu.roll(value, GROUPS - 1, 0))
                ref[k * 8 : k * 8 + 8, at] = jnp.where(even, value, fill).astype(BF16)


def pack(own, sib, weight, bias):
    shape = jax.ShapeDtypeStruct((PACK, GW), BF16)
    return pl.pallas_call(
        pack_kernel,
        in_specs=in_vmem(4),
        out_specs=in_vmem(2),
        out_shape=[shape, shape],
        compiler_params=params(),
        name="pack",
    )(own, sib, weight, bias)


PART = 16


def convolve(window, taps):
    half = taps[KERNEL][None] + taps[0][None] * window[0:PART]
    for k in range(1, KERNEL):
        half = half + taps[k][None] * window[k : k + PART]
    half = half + half * jnp.tanh(half)
    return half.reshape(PART * GROUPS, LANE)


def load_lanes(refs, to_refs, sems):
    loads = []
    for i in range(GW // LW):
        at = pl.ds(i * LW, LW)
        loads.append(
            [pltpu.make_async_copy(ref.at[:, :, at], to.at[:, :, at], sems.at[k, i]) for k, (ref, to) in enumerate(zip(refs, to_refs))]
        )
        for load in loads[-1]:
            load.start()
    return loads


def states_kernel(
    core_ref, first_ref, own_hbm, sib_hbm, p0, p1, p2, p3, p4, ets_ref, eto_ref, out_hbm, before_hbm, w_ref, halo_ref,
    own_ref, sib_ref, packed_ref, act_ref, pieces_ref, before_ref, sems, load_sems,
):
    core = core_ref[0]
    place = lax.axis_index("y")
    loads = load_lanes((own_hbm, sib_hbm), (own_ref, sib_ref), load_sems)
    keep = jnp.where(place == 0, 1 - first_ref[0], 1).astype(F32)
    low = iota((1, GROUPS, LANE), 1) % 2 == 0
    kept = iota((1, GROUPS, LANE), 1) % 2 == core
    swap = lambda v: pltpu.roll(v, 1 + 6 * core, v.ndim - 2)
    for tile in range(GW // LANE):
        at = slice(tile * LANE, (tile + 1) * LANE)
        packs = [ref[:, at].astype(F32) for ref in (p0, p1, p2, p3)]
        for k, pack in enumerate(packs):
            source = lax.rem(place - k + 4, 4)
            for double in range(2):
                packed_ref[pl.ds(pl.multiple_of((source * 2 + double) * PACK, 8), PACK), :] = pack
        halves = [packed_ref[pl.ds(weight_row(m), GROUPS, stride=PACK), :] * 0.5 for m in range(2 * KERNEL + 2)]
        taps = [halves[k] + halves[k + KERNEL + 1] for k in range(KERNEL + 1)]
        for k, v in enumerate(taps):
            w_ref[k, :, at] = v
        before = packs[1] + jnp.where(place == 0, packs[2] + packs[3] + p4[:, at].astype(F32), 0.0)
        before = jnp.where(low, before.reshape(ENDS, GROUPS, LANE) * keep, 0.0)
        halo_ref[:, :, at] = before.astype(BF16)
        if tile % 2 == 0:
            for load in loads[tile // 2]:
                load.wait()

        def merged(rows, at=at):
            return jnp.where(kept, own_ref[rows, :, at].astype(F32), swap(sib_ref[rows, :, at].astype(F32)))

        def tokens(i, carry, tile=tile, taps=taps, merged=merged):
            window = merged(pl.ds(i * PART - (KERNEL - 1), PART + KERNEL - 1))
            act_ref[tile, pl.ds(pl.multiple_of(i * PART * GROUPS, PART * GROUPS), PART * GROUPS), :] = convolve(window, taps)
            return carry

        last = slice(TOK - (KERNEL - 1), TOK)
        between = jnp.where(core == 0, swap(own_ref[last, :, at].astype(F32)), sib_ref[last, :, at].astype(F32))
        window = jnp.concatenate([jnp.where(low, before, between), merged(slice(0, PART))], axis=0)
        act_ref[tile, 0 : PART * GROUPS, :] = convolve(window, taps)
        lax.fori_loop(1, TOK // PART, tokens, 0, unroll=True)

    own, sib = eto_ref[...], ets_ref[...]
    decay = [jnp.where(core == 0, own, sib), jnp.where(core == 0, sib, own)]
    d_last = decay[1][TOK:]
    d_chip = decay[0][TOK:] * d_last
    row = iota((8, LANE), 0)
    copies = []
    for i in range(4):
        of_group = lambda half, tile: act_ref[tile, pl.ds(2 * i + half, TOK, stride=GROUPS), :]
        b_t = [of_group(half, 8).T.astype(BF16) for half in range(2)]
        for j in range(4):
            states = []
            for half in range(2):
                carried = [
                    (of_group(half, tile) * widen(decay[half][:TOK], core * 16 + i * 32 + tile * 2)).astype(BF16)
                    for tile in (2 * j, 2 * j + 1)
                ]
                states.append(jnp.dot(b_t[half], jnp.concatenate(carried, axis=1), preferred_element_type=F32))
            for tile in range(2):
                lanes = slice(tile * LANE, (tile + 1) * LANE)
                head = core * 16 + i * 32 + (2 * j + tile) * 2
                hi, mid, bottom = split3(widen(d_chip, head))
                extra = jnp.where(row == 0, hi, jnp.where(row == 1, mid, jnp.where(row == 2, bottom, keep)))
                first = states[0][:, lanes]
                both = (first * widen(d_last, head)[0:1] + states[1][:, lanes]).astype(BF16)
                first = first.astype(BF16)
                for rows in range(2):
                    piece = (i * 8 + 2 * j + tile) * 2 + rows
                    before_ref[i, j, tile * 2 + rows] = first[rows * 64 : rows * 64 + 64]
                    pieces_ref[piece, 0:64] = both[rows * 64 : rows * 64 + 64]
                    pieces_ref[piece, 64:ROWS] = extra.astype(BF16)
        group = pl.ds(i * 16, 16)
        copies.append(pltpu.make_async_copy(pieces_ref.at[group], out_hbm.at[group], sems.at[0, i]))
        copies.append(pltpu.make_async_copy(before_ref.at[i], before_hbm.at[i], sems.at[1, i]))
        copies[-2].start()
        copies[-1].start()
    for copy in copies:
        copy.wait()


def chip_states(core, seg_first, own, sib, packs, et_sib, et_own):
    pieces = (CHUNKS, ROWS, LANE)
    before = (4, 4, 4, 64, LANE)
    return pl.pallas_call(
        states_kernel,
        in_specs=in_smem(2) + in_hbm(2) + in_vmem(7),
        out_specs=in_hbm(2) + in_vmem(2),
        out_shape=[
            hbm(pieces),
            hbm(before),
            jax.ShapeDtypeStruct((KERNEL + 1, GROUPS, GW), F32),
            jax.ShapeDtypeStruct((ENDS, GROUPS, GW), BF16),
        ],
        scratch_shapes=[
            pltpu.VMEM((TOK, GROUPS, GW), BF16),
            pltpu.VMEM((TOK, GROUPS, GW), BF16),
            pltpu.VMEM((GROUPS * PACK, LANE), F32),
            pltpu.VMEM((GW // LANE, TOK * GROUPS, LANE), F32),
            pltpu.VMEM(pieces, BF16),
            pltpu.VMEM(before, BF16),
            pltpu.SemaphoreType.DMA((2, 4)),
            pltpu.SemaphoreType.DMA((2, GW // LW)),
        ],
        compiler_params=params(20),
        name="chip_states",
    )(core, seg_first, from_hbm(own), from_hbm(sib), *packs, et_sib, et_own)


def act_kernel(
    core_ref, conv_hbm, sib_hbm, own_halo_ref, sib_halo_ref, own_w_ref, sib_w_ref, x_hbm, bc_hbm, done_ref,
    conv_ref, last_ref, act_ref, x_ref, bc_ref, sems, load_sems,
):
    done_ref[...] = jnp.zeros_like(done_ref)
    core = core_ref[0]
    last = pltpu.make_async_copy(sib_hbm.at[pl.ds(TOK - ENDS, ENDS)], last_ref, load_sems.at[1, 0])
    last.start()
    loads = load_lanes((conv_hbm,), (conv_ref,), load_sems)
    last.wait()
    low = iota((1, GROUPS, LANE), 1) % 2 == 0
    kept = iota((GROUPS, LANE), 0) % 2 == core
    for tile in range(GW // LANE):
        at = slice(tile * LANE, (tile + 1) * LANE)
        taps = [jnp.where(kept, own_w_ref[k, :, at], sib_w_ref[k, :, at]) for k in range(KERNEL + 1)]
        if tile % 2 == 0:
            loads[tile // 2][0].wait()

        def tokens(i, carry, at=at, tile=tile, taps=taps):
            window = conv_ref[pl.ds(i * PART - (KERNEL - 1), PART + KERNEL - 1), :, at].astype(F32)
            act_ref[tile, pl.ds(pl.multiple_of(i * PART * GROUPS, PART * GROUPS), PART * GROUPS), :] = convolve(window, taps)
            return carry

        halo = pltpu.roll(sib_halo_ref[:, :, at].astype(F32), 1, 1)
        halo = jnp.where(low, own_halo_ref[:, :, at].astype(F32), halo)
        halo = jnp.where(core == 0, halo, last_ref[:, :, at].astype(F32))
        window = jnp.concatenate([halo, conv_ref[0:PART, :, at].astype(F32)], axis=0)
        act_ref[tile, 0 : PART * GROUPS, :] = convolve(window, taps)
        lax.fori_loop(1, TOK // PART, tokens, 0, unroll=True)
    copies = []
    for g in range(GROUPS):
        for tile in range(GW // LANE):
            values = act_ref[tile, pl.ds(g, TOK, stride=GROUPS), :].astype(BF16)
            if tile < XW // LANE:
                x_ref[g, :, tile * LANE : (tile + 1) * LANE] = values
            else:
                bc_ref[g, :, tile * LANE - XW : (tile + 1) * LANE - XW] = values
        copies.append(pltpu.make_async_copy(x_ref.at[g], x_hbm.at[g], sems.at[0, g]))
        copies.append(pltpu.make_async_copy(bc_ref.at[g], bc_hbm.at[g], sems.at[1, g]))
        copies[-2].start()
        copies[-1].start()
    for copy in copies:
        copy.wait()


def activate(core, conv_input, sib, own_halo, sib_halo, own_weights, sib_weights):
    x, bc = (GROUPS, TOK, XW), (GROUPS, TOK, LW)
    return pl.pallas_call(
        act_kernel,
        in_specs=in_smem(1) + in_hbm(2) + in_vmem(4),
        out_specs=in_hbm(2) + in_vmem(1),
        out_shape=[hbm(x), hbm(bc), DONE],
        scratch_shapes=[
            pltpu.VMEM((TOK, GROUPS, GW), BF16),
            pltpu.VMEM((ENDS, GROUPS, GW), BF16),
            pltpu.VMEM((GW // LANE, TOK * GROUPS, LANE), F32),
            pltpu.VMEM(x, BF16),
            pltpu.VMEM(bc, BF16),
            pltpu.SemaphoreType.DMA((2, GROUPS)),
            pltpu.SemaphoreType.DMA((2, GW // LW)),
        ],
        compiler_params=params(18),
        cost_estimate=pl.CostEstimate(flops=20_000_000, bytes_accessed=8_000_000, transcendentals=1_400_000),
        name="activate",
    )(core, from_hbm(conv_input), from_hbm(sib), own_halo, sib_halo, own_weights, sib_weights)


def scan_kernel(chips, in_ref, done_ref, out_hbm, out_ref, sems):
    each = CHUNKS // chips
    parts = 4
    size = CHUNKS // parts
    states = [jnp.zeros((64, LANE), F32) for _ in range(each)]
    stores = []
    for k in range(parts):
        for at in range(k * size, (k + 1) * size):
            i = at % each
            extra = in_ref[at, 64:ROWS].astype(F32)
            state = extra[3:4] * states[i]
            out_ref[at] = state.astype(BF16)
            states[i] = (extra[0:1] + extra[1:2] + extra[2:3]) * state + in_ref[at, 0:64].astype(F32)
        span = pl.ds(k * size, size)
        stores.append(pltpu.make_async_copy(out_ref.at[span], out_hbm.at[span], sems.at[k]))
        stores[-1].start()
    for store in stores:
        store.wait()


def scan(chips, pieces, done):
    return pl.pallas_call(
        functools.partial(scan_kernel, chips),
        in_specs=in_vmem(1) + [pl.BlockSpec(memory_space=pl.ANY)],
        out_specs=in_hbm(1)[0],
        out_shape=hbm((CHUNKS, 64, LANE)),
        scratch_shapes=[pltpu.VMEM((CHUNKS, 64, LANE), BF16), pltpu.SemaphoreType.DMA((4,))],
        compiler_params=params(4),
        name="scan",
    )(pieces, done)


def local_kernel(other, core_ref, len_ref, x_ref, bc_ref, tab_ref, before_ref, dts_ref, gate_ref, skip_ref, p_ref, q_ref, done_ref):
    core = core_ref[0]
    done_ref[...] = jnp.zeros_like(done_ref)
    group = (core + other) % 2 + 2 * pl.program_id(0)
    inner, after, since = (tab_ref[k] for k in range(3))
    since = since * jnp.where(core == 1, dts_ref[TOK : TOK + 1], 1.0)
    rise = jnp.where(core == 1, tab_ref[2, TOK // 2 - 1 : TOK // 2], 0.0)
    rise = jnp.broadcast_to(rise, (8, LANE))
    spread = lambda table, j: jnp.concatenate([widen(table, group * 16 + j * 4 + 2 * k) for k in range(2)], axis=1)
    b = bc_ref[0, :, :LANE]
    c = bc_ref[0, :, LANE:]
    scores = lax.dot_general(c, b, (((1,), (1,)), ((), ())), preferred_element_type=F32)
    causal = iota((TOK, TOK), 0) >= iota((TOK, TOK), 1)
    scores = jnp.where(causal, scores, 0.0).astype(BF16)
    live = iota((TOK, LW), 0) < len_ref[0] - head_place() * TOK
    for j in range(4):
        at = slice(j * LW, (j + 1) * LW)
        x = x_ref[0, :, at].astype(F32)
        scaled = (x * spread(inner, j)).astype(BF16)
        before = jnp.concatenate(
            [jnp.concatenate([before_ref[0, j, tile * 2], before_ref[0, j, tile * 2 + 1]], axis=0) for tile in range(2)],
            axis=1,
        )
        read = jnp.dot(scores, scaled, preferred_element_type=F32)
        read = read + spread(rise, j)[0:1] * jnp.dot(c, before, preferred_element_type=F32)
        y = spread(after, j) * read + skip_ref[:, at] * x
        half = gate_ref[:, at].astype(F32) * 0.5
        silu = half + half * jnp.tanh(half)
        p_ref[0, :, at] = jnp.where(live, y * silu, 0.0).astype(BF16)
        q_ref[0, :, at] = jnp.where(live, spread(since, j) * silu, 0.0).astype(BF16)


def local(other, core, seg_length, x, bc, tables, before, d_sib, gate_input, skip):
    group = lambda i, s: (s[0] + other) % 2 + 2 * i
    out = hbm((4, TOK, XW))
    out_spec = pl.BlockSpec((1, TOK, XW), lambda i, s: (i, 0, 0))
    return pl.pallas_call(
        functools.partial(local_kernel, other),
        grid_spec=pltpu.PrefetchScalarGridSpec(
            num_scalar_prefetch=1,
            grid=(4,),
            in_specs=[
                pl.BlockSpec(memory_space=pltpu.SMEM),
                pl.BlockSpec((1, TOK, XW), lambda i, s: (group(i, s), 0, 0)),
                pl.BlockSpec((1, TOK, LW), lambda i, s: (group(i, s), 0, 0)),
                pl.BlockSpec((3, TOK, LANE), lambda i, s: (0, 0, 0)),
                pl.BlockSpec((1, 4, 4, 64, LANE), lambda i, s: (i, 0, 0, 0, 0)),
                pl.BlockSpec((TOK + 8, LANE), lambda i, s: (0, 0)),
                pl.BlockSpec((TOK, XW), lambda i, s: (0, group(i, s))),
                pl.BlockSpec((1, XW), lambda i, s: (0, group(i, s))),
            ],
            out_specs=[out_spec, out_spec, pl.BlockSpec((8, LANE), lambda i, s: (0, 0))],
        ),
        out_shape=[out, out, DONE],
        compiler_params=params(),
        cost_estimate=pl.CostEstimate(flops=400_000_000, bytes_accessed=8_000_000, transcendentals=600_000),
        name="local",
    )(core, seg_length, from_hbm(x), from_hbm(bc), tables, from_hbm(before), d_sib, from_hbm(gate_input), skip)


def finish_kernel(other, core_ref, p_ref, q_ref, bc_ref, state_ref, gain_ref, *rest):
    first = (core_ref[0] + other) % 2
    copies = []

    def send(half, i, rows_ref, sems):
        group = (core_ref[0] + half) % 2 + 2 * i
        to = out_ref.at[:, pl.ds(pl.multiple_of(group * XW, XW), XW)]
        copies.append(pltpu.make_async_copy(rows_ref.at[i], to, sems.at[half, i]))
        copies[-1].start()

    if other:
        own_rows_ref, out_ref, rows_ref, sems = rest
        for i in range(4):
            send(0, i, own_rows_ref, sems)
    else:
        _, rows_ref, p_to, q_to, state_to, load_sems = rest
        loads = []
        for i in range(4):
            group = pl.ds(i * 16, 16)
            loads.append(pltpu.make_async_copy(state_ref.at[group], state_to.at[group], load_sems.at[0, i]))
            loads.append(pltpu.make_async_copy(p_ref.at[i], p_to.at[i], load_sems.at[1, i]))
            loads.append(pltpu.make_async_copy(q_ref.at[i], q_to.at[i], load_sems.at[2, i]))
        for load in loads:
            load.start()
        p_ref, q_ref, state_ref = p_to, q_to, state_to
    for i in range(4):
        if not other:
            for load in loads[3 * i : 3 * i + 6 if i % 2 == 0 else 3 * i]:
                load.wait()
        c = bc_ref[first + 2 * i, :, LANE:]
        gated = []
        for tile in range(0, 8, 2):
            state = jnp.concatenate(
                [
                    jnp.concatenate([state_ref[i * 16 + (tile + k) * 2], state_ref[i * 16 + (tile + k) * 2 + 1]], axis=0)
                    for k in range(2)
                ],
                axis=1,
            )
            at = slice(tile * LANE, (tile + 2) * LANE)
            read = jnp.dot(c, state, preferred_element_type=F32)
            gated.append(p_ref[i, :, at].astype(F32) + read * q_ref[i, :, at].astype(F32))
        total = sum(jnp.sum(v * v, axis=1, keepdims=True) for v in gated)
        scale = lax.rsqrt(total / XW + EPSILON)
        for j, v in enumerate(gated):
            at = slice(j * LW, (j + 1) * LW)
            rows_ref[i, :, at] = (v * scale * gain_ref[first + 2 * i, :, at]).astype(BF16)
        if other:
            send(1, i, rows_ref, sems)
    for copy in copies:
        copy.wait()


def finish(other, core, p, q, bc, states, gain, out):
    rows = pltpu.VMEM((4, TOK, XW), BF16)
    if other:
        operands = [core, p, q, bc, states, gain, out]
        in_specs = in_smem(1) + in_vmem(5) + [pl.BlockSpec(memory_space=pl.ANY)]
        out_shape = jax.ShapeDtypeStruct((TOK, GROUPS * XW), BF16)
        out_spec = pl.BlockSpec(memory_space=pl.ANY)
        scratch = [rows, pltpu.SemaphoreType.DMA((2, 4))]
    else:
        operands = [core, from_hbm(p), from_hbm(q), bc, from_hbm(states), gain, out]
        in_specs = in_smem(1) + in_hbm(2) + in_vmem(1) + in_hbm(1) + in_vmem(1) + [pl.BlockSpec(memory_space=pl.ANY)]
        out_shape = jax.ShapeDtypeStruct((4, TOK, XW), BF16)
        out_spec = in_vmem(1)[0]
        scratch = [rows, rows, pltpu.VMEM((CHUNKS, 64, LANE), BF16), pltpu.SemaphoreType.DMA((3, 4))]
    return pl.pallas_call(
        functools.partial(finish_kernel, other),
        in_specs=in_specs,
        out_specs=out_spec,
        scratch_shapes=scratch,
        out_shape=out_shape,
        compiler_params=params(),
        cost_estimate=pl.CostEstimate(flops=200_000_000, bytes_accessed=4_000_000, transcendentals=1000),
        name="finish",
    )(*operands)


def body(
    conv_input,
    gate_input,
    step_size,
    decay_log,
    conv_weight,
    conv_bias,
    skip_gain,
    norm_gain,
    seg_length,
    seg_first,
):
    segments = lax.axis_size("seq")
    in_segment = lax.axis_size("y") * lax.axis_size("core")
    chips = segments * in_segment // 2
    core = lax.axis_index("core").astype(jnp.int32).reshape(1)
    swap = [(0, 1), (1, 0)]

    sib = lax.ppermute(conv_input, "core", swap)
    tables, et_own, ends = start(seg_length, decay_log, step_size, conv_input)
    onward, tail = pack(ends, lax.ppermute(ends, "core", swap), conv_weight, conv_bias)
    packs = [
        lax.ppermute(tail if k > 1 else onward, CHIPS, [(c, (c + k) % chips) for c in range(chips)]) for k in range(1, 5)
    ]
    et_sib = lax.ppermute(et_own, "core", swap)

    pieces, before_own, weights, halo = chip_states(
        core, seg_first, conv_input, sib, [tail] + packs, et_sib, et_own
    )
    pieces = lax.all_to_all(pieces, CHIPS, 0, 0, tiled=True)
    before_oth = lax.ppermute(before_own, "core", swap[:1])
    halo_sib = lax.ppermute(halo, "core", swap)
    weights_sib = lax.ppermute(weights, "core", swap)
    x, bc, done = activate(core, conv_input, sib, halo, halo_sib, weights, weights_sib)

    skip = jnp.repeat(skip_gain, HEAD_DIM)[None]
    p_own, q_own, done_own = local(0, core, seg_length, x, bc, tables, before_own, et_sib, gate_input, skip)
    p_oth, q_oth, done_oth = local(1, core, seg_length, x, bc, tables, before_oth, et_sib, gate_input, skip)
    states = lax.all_to_all(scan(chips, pieces, done), CHIPS, 0, 0, tiled=True)
    states, done = lax.optimization_barrier((states, done_own + done_oth))
    states_oth = lax.ppermute(states, "core", swap)
    gain = norm_gain.reshape(GROUPS, 1, XW)
    out = finish(0, core, p_own, q_own, bc, states, gain, done)
    return finish(1, core, p_oth, q_oth, bc, states_oth, gain, out)


def solution(mesh):
    segments, in_segment = mesh.devices.shape
    fine = Mesh(mesh.devices.reshape(segments, in_segment // 2, 2), AXES)
    tokens = P(AXES, None)
    return jax.shard_map(
        body,
        mesh=fine,
        in_specs=(
            P(AXES, None, None),
            tokens,
            tokens,
            tokens,
            P(None, ("y", "core"), None),
            P(("y", "core"), None),
            P(),
            P(),
            P("seq"),
            P("seq"),
        ),
        out_specs=tokens,
        check_vma=False,
    )
```

```python
import functools

import jax
import jax.numpy as jnp
from jax import lax
from jax.experimental import pallas as pl
from jax.experimental.pallas import tpu as pltpu
from jax.sharding import Mesh, PartitionSpec as P

HEAD_DIM = 64
KERNEL = 4
EPSILON = 1e-05
TOK = 128
GROUPS = 8
XW = 1024
GW = 1280
LANE = 128
LW = 256
CHUNKS = 64
ENDS = KERNEL - 1
PACK = 24
ROWS = 72
AXES = ("seq", "y", "core")
CHIPS = ("seq", "y")
F32 = jnp.float32
BF16 = jnp.bfloat16
DONE = jax.ShapeDtypeStruct((8, LANE), F32)


def iota(shape, dim):
    return lax.broadcasted_iota(jnp.int32, shape, dim)


def split3(v):
    hi = v.astype(BF16).astype(F32)
    mid = (v - hi).astype(BF16).astype(F32)
    return hi, mid, v - hi - mid


def widen(table, first):
    lane = iota(table.shape, 1) // HEAD_DIM + first
    return jnp.take_along_axis(table, lane, axis=1, mode="promise_in_bounds")


def head_place():
    return lax.axis_index("y") * 2 + lax.axis_index("core")


def in_vmem(count):
    return [pl.BlockSpec(memory_space=pltpu.VMEM)] * count


def in_hbm(count):
    return [pl.BlockSpec(memory_space=pltpu.HBM)] * count


def in_smem(count):
    return [pl.BlockSpec(memory_space=pltpu.SMEM)] * count


def hbm(shape):
    return pltpu.HBM(shape, BF16)


def from_hbm(value):
    return pltpu.with_memory_space_constraint(value, pltpu.HBM)


def params(mib=16):
    return pltpu.CompilerParams(vmem_limit_bytes=mib * 1024 * 1024)


def start_kernel(
    len_ref, decay_hbm, step_hbm, conv_hbm, tab_ref, et_ref, ends_ref, decay_ref, step_ref, rows_ref, sems
):
    first_row = len_ref[0] - head_place() * TOK
    copies = [
        pltpu.make_async_copy(decay_hbm, decay_ref, sems.at[0]),
        pltpu.make_async_copy(step_hbm, step_ref, sems.at[1]),
    ]
    for k in range(ENDS):
        row = jnp.clip(first_row - ENDS + k, 0, TOK - 1)
        copies.append(pltpu.make_async_copy(conv_hbm.at[pl.ds(row, 1)], rows_ref.at[pl.ds(k, 1)], sems.at[2 + k]))
    copies.append(pltpu.make_async_copy(conv_hbm.at[pl.ds(TOK - ENDS, ENDS)], rows_ref.at[pl.ds(ENDS, ENDS)], sems.at[2 + ENDS]))
    for copy in copies:
        copy.start()
    for copy in copies:
        copy.wait()
    for k in range(ENDS):
        row = first_row - ENDS + k
        inside = jnp.where((row >= 0) & (row < TOK), 1.0, 0.0)
        ends_ref[k] = (rows_ref[k].astype(F32) * inside).astype(BF16)
        ends_ref[ENDS + k] = rows_ref[ENDS + k]
    live = iota((TOK, LANE), 0) < first_row
    log_rate = jnp.where(live, decay_ref[...].astype(F32), 0.0)
    gain = jnp.where(live, step_ref[...].astype(F32), 0.0)
    upto = jnp.where(iota((TOK, TOK), 0) >= iota((TOK, TOK), 1), 1.0, 0.0).astype(BF16)
    running = jnp.dot(upto, log_rate.astype(BF16), preferred_element_type=F32)
    middle = running[TOK // 2 - 1 : TOK // 2]
    total = running[TOK - 1 : TOK]
    tab_ref[0] = jnp.exp(middle - running) * gain
    tab_ref[1] = jnp.exp(running - middle)
    tab_ref[2] = jnp.exp(running)
    et_ref[0:TOK] = jnp.exp(total - running) * gain
    et_ref[TOK:] = jnp.broadcast_to(jnp.exp(total), (8, LANE))


def start(seg_length, decay_log, step_size, conv_input):
    return pl.pallas_call(
        start_kernel,
        in_specs=in_smem(1) + in_hbm(3),
        out_specs=in_vmem(3),
        out_shape=[
            jax.ShapeDtypeStruct((3, TOK, LANE), F32),
            jax.ShapeDtypeStruct((TOK + 8, LANE), F32),
            jax.ShapeDtypeStruct((2 * ENDS, GROUPS, GW), BF16),
        ],
        scratch_shapes=[
            pltpu.VMEM((TOK, LANE), BF16),
            pltpu.VMEM((TOK, LANE), BF16),
            pltpu.VMEM((2 * ENDS, GROUPS, GW), BF16),
            pltpu.SemaphoreType.DMA((3 + ENDS,)),
        ],
        compiler_params=params(),
        name="start",
    )(seg_length, from_hbm(decay_log), from_hbm(step_size), from_hbm(conv_input))


def weight_row(m):
    return m // 4 * 8 + m % 4 * 2 + 1


def pack_kernel(own_ref, sib_ref, weight_ref, bias_ref, on_ref, tail_ref):
    place, core = lax.axis_index("y"), lax.axis_index("core")
    row = iota((GROUPS, LANE), 0)
    even = row % 2 == 0
    for tile in range(GW // LANE):
        at = slice(tile * LANE, (tile + 1) * LANE)
        rows = [weight_ref[k, :, at] for k in range(KERNEL)] + [bias_ref[:, at]]
        rows = rows + [v - v.astype(BF16).astype(F32) for v in rows]
        for k in range(ENDS):
            fill = jnp.zeros((GROUPS, LANE), F32)
            for m in range(4 * k, min(4 * k + 4, len(rows))):
                fill = jnp.where(row == weight_row(m % 4), rows[m], fill)
            tail = own_ref[k, :, at].astype(F32) + sib_ref[k, :, at].astype(F32)
            last = jnp.where(core == 0, sib_ref[ENDS + k, :, at].astype(F32), own_ref[ENDS + k, :, at].astype(F32))
            onward = jnp.where(place == lax.axis_size("y") - 1, tail, last)
            for value, ref in ((onward, on_ref), (tail, tail_ref)):
                value = jnp.where(core == 0, value, pltpu.roll(value, GROUPS - 1, 0))
                ref[k * 8 : k * 8 + 8, at] = jnp.where(even, value, fill).astype(BF16)


def pack(own, sib, weight, bias):
    shape = jax.ShapeDtypeStruct((PACK, GW), BF16)
    return pl.pallas_call(
        pack_kernel,
        in_specs=in_vmem(4),
        out_specs=in_vmem(2),
        out_shape=[shape, shape],
        compiler_params=params(),
        name="pack",
    )(own, sib, weight, bias)


PART = 16


def convolve(window, taps):
    half = taps[KERNEL][None] + taps[0][None] * window[0:PART]
    for k in range(1, KERNEL):
        half = half + taps[k][None] * window[k : k + PART]
    half = half + half * jnp.tanh(half)
    return half.reshape(PART * GROUPS, LANE)


def load_lanes(refs, to_refs, sems):
    loads = []
    for i in range(GW // LW):
        at = pl.ds(i * LW, LW)
        loads.append(
            [pltpu.make_async_copy(ref.at[:, :, at], to.at[:, :, at], sems.at[k, i]) for k, (ref, to) in enumerate(zip(refs, to_refs))]
        )
        for load in loads[-1]:
            load.start()
    return loads


def states_kernel(
    core_ref, first_ref, own_hbm, sib_hbm, p0, p1, p2, p3, p4, ets_ref, eto_ref, out_hbm, before_hbm, w_ref, halo_ref,
    own_ref, sib_ref, packed_ref, act_ref, pieces_ref, before_ref, sems, load_sems,
):
    core = core_ref[0]
    place = lax.axis_index("y")
    loads = load_lanes((own_hbm, sib_hbm), (own_ref, sib_ref), load_sems)
    keep = jnp.where(place == 0, 1 - first_ref[0], 1).astype(F32)
    low = iota((1, GROUPS, LANE), 1) % 2 == 0
    kept = iota((1, GROUPS, LANE), 1) % 2 == core
    swap = lambda v: pltpu.roll(v, 1 + 6 * core, v.ndim - 2)
    for tile in range(GW // LANE):
        at = slice(tile * LANE, (tile + 1) * LANE)
        packs = [ref[:, at].astype(F32) for ref in (p0, p1, p2, p3)]
        for k, pack in enumerate(packs):
            source = lax.rem(place - k + 4, 4)
            for double in range(2):
                packed_ref[pl.ds(pl.multiple_of((source * 2 + double) * PACK, 8), PACK), :] = pack
        halves = [packed_ref[pl.ds(weight_row(m), GROUPS, stride=PACK), :] * 0.5 for m in range(2 * KERNEL + 2)]
        taps = [halves[k] + halves[k + KERNEL + 1] for k in range(KERNEL + 1)]
        for k, v in enumerate(taps):
            w_ref[k, :, at] = v
        before = packs[1] + jnp.where(place == 0, packs[2] + packs[3] + p4[:, at].astype(F32), 0.0)
        before = jnp.where(low, before.reshape(ENDS, GROUPS, LANE) * keep, 0.0)
        halo_ref[:, :, at] = before.astype(BF16)
        if tile % 2 == 0:
            for load in loads[tile // 2]:
                load.wait()

        def merged(rows, at=at):
            return jnp.where(kept, own_ref[rows, :, at].astype(F32), swap(sib_ref[rows, :, at].astype(F32)))

        def tokens(i, carry, tile=tile, taps=taps, merged=merged):
            window = merged(pl.ds(i * PART - (KERNEL - 1), PART + KERNEL - 1))
            act_ref[tile, pl.ds(pl.multiple_of(i * PART * GROUPS, PART * GROUPS), PART * GROUPS), :] = convolve(window, taps)
            return carry

        last = slice(TOK - (KERNEL - 1), TOK)
        between = jnp.where(core == 0, swap(own_ref[last, :, at].astype(F32)), sib_ref[last, :, at].astype(F32))
        window = jnp.concatenate([jnp.where(low, before, between), merged(slice(0, PART))], axis=0)
        act_ref[tile, 0 : PART * GROUPS, :] = convolve(window, taps)
        lax.fori_loop(1, TOK // PART, tokens, 0, unroll=True)

    own, sib = eto_ref[...], ets_ref[...]
    decay = [jnp.where(core == 0, own, sib), jnp.where(core == 0, sib, own)]
    d_last = decay[1][TOK:]
    d_chip = decay[0][TOK:] * d_last
    row = iota((8, LANE), 0)
    copies = []
    for i in range(4):
        of_group = lambda half, tile: act_ref[tile, pl.ds(2 * i + half, TOK, stride=GROUPS), :]
        b_t = [of_group(half, 8).T.astype(BF16) for half in range(2)]
        states = []
        for half in range(2):
            carried = [
                (of_group(half, tile) * widen(decay[half][:TOK], core * 16 + i * 32 + tile * 2)).astype(BF16)
                for tile in range(8)
            ]
            states.append(jnp.dot(b_t[half], jnp.concatenate(carried, axis=1), preferred_element_type=F32))
        for tile in range(8):
            lanes = slice(tile * LANE, (tile + 1) * LANE)
            head = core * 16 + i * 32 + tile * 2
            hi, mid, bottom = split3(widen(d_chip, head))
            extra = jnp.where(row == 0, hi, jnp.where(row == 1, mid, jnp.where(row == 2, bottom, keep)))
            first = states[0][:, lanes]
            both = (first * widen(d_last, head)[0:1] + states[1][:, lanes]).astype(BF16)
            first = first.astype(BF16)
            for rows in range(2):
                piece = (i * 8 + tile) * 2 + rows
                before_ref[i, tile // 2, tile % 2 * 2 + rows] = first[rows * 64 : rows * 64 + 64]
                pieces_ref[piece, 0:64] = both[rows * 64 : rows * 64 + 64]
                pieces_ref[piece, 64:ROWS] = extra.astype(BF16)
        group = pl.ds(i * 16, 16)
        copies.append(pltpu.make_async_copy(pieces_ref.at[group], out_hbm.at[group], sems.at[0, i]))
        copies.append(pltpu.make_async_copy(before_ref.at[i], before_hbm.at[i], sems.at[1, i]))
        copies[-2].start()
        copies[-1].start()
    for copy in copies:
        copy.wait()


def chip_states(core, seg_first, own, sib, packs, et_sib, et_own):
    pieces = (CHUNKS, ROWS, LANE)
    before = (4, 4, 4, 64, LANE)
    return pl.pallas_call(
        states_kernel,
        in_specs=in_smem(2) + in_hbm(2) + in_vmem(7),
        out_specs=in_hbm(2) + in_vmem(2),
        out_shape=[
            hbm(pieces),
            hbm(before),
            jax.ShapeDtypeStruct((KERNEL + 1, GROUPS, GW), F32),
            jax.ShapeDtypeStruct((ENDS, GROUPS, GW), BF16),
        ],
        scratch_shapes=[
            pltpu.VMEM((TOK, GROUPS, GW), BF16),
            pltpu.VMEM((TOK, GROUPS, GW), BF16),
            pltpu.VMEM((GROUPS * PACK, LANE), F32),
            pltpu.VMEM((GW // LANE, TOK * GROUPS, LANE), F32),
            pltpu.VMEM(pieces, BF16),
            pltpu.VMEM(before, BF16),
            pltpu.SemaphoreType.DMA((2, 4)),
            pltpu.SemaphoreType.DMA((2, GW // LW)),
        ],
        compiler_params=params(20),
        name="chip_states",
    )(core, seg_first, from_hbm(own), from_hbm(sib), *packs, et_sib, et_own)


def act_kernel(
    core_ref, conv_hbm, sib_hbm, own_halo_ref, sib_halo_ref, own_w_ref, sib_w_ref, x_hbm, bc_hbm, done_ref,
    conv_ref, last_ref, act_ref, x_ref, bc_ref, sems, load_sems,
):
    done_ref[...] = jnp.zeros_like(done_ref)
    core = core_ref[0]
    last = pltpu.make_async_copy(sib_hbm.at[pl.ds(TOK - ENDS, ENDS)], last_ref, load_sems.at[1, 0])
    last.start()
    loads = load_lanes((conv_hbm,), (conv_ref,), load_sems)
    last.wait()
    low = iota((1, GROUPS, LANE), 1) % 2 == 0
    kept = iota((GROUPS, LANE), 0) % 2 == core
    for tile in range(GW // LANE):
        at = slice(tile * LANE, (tile + 1) * LANE)
        taps = [jnp.where(kept, own_w_ref[k, :, at], sib_w_ref[k, :, at]) for k in range(KERNEL + 1)]
        if tile % 2 == 0:
            loads[tile // 2][0].wait()

        def tokens(i, carry, at=at, tile=tile, taps=taps):
            window = conv_ref[pl.ds(i * PART - (KERNEL - 1), PART + KERNEL - 1), :, at].astype(F32)
            act_ref[tile, pl.ds(pl.multiple_of(i * PART * GROUPS, PART * GROUPS), PART * GROUPS), :] = convolve(window, taps)
            return carry

        halo = pltpu.roll(sib_halo_ref[:, :, at].astype(F32), 1, 1)
        halo = jnp.where(low, own_halo_ref[:, :, at].astype(F32), halo)
        halo = jnp.where(core == 0, halo, last_ref[:, :, at].astype(F32))
        window = jnp.concatenate([halo, conv_ref[0:PART, :, at].astype(F32)], axis=0)
        act_ref[tile, 0 : PART * GROUPS, :] = convolve(window, taps)
        lax.fori_loop(1, TOK // PART, tokens, 0, unroll=True)
    copies = []
    for g in range(GROUPS):
        for tile in range(GW // LANE):
            values = act_ref[tile, pl.ds(g, TOK, stride=GROUPS), :].astype(BF16)
            if tile < XW // LANE:
                x_ref[g, :, tile * LANE : (tile + 1) * LANE] = values
            else:
                bc_ref[g, :, tile * LANE - XW : (tile + 1) * LANE - XW] = values
        copies.append(pltpu.make_async_copy(x_ref.at[g], x_hbm.at[g], sems.at[0, g]))
        copies.append(pltpu.make_async_copy(bc_ref.at[g], bc_hbm.at[g], sems.at[1, g]))
        copies[-2].start()
        copies[-1].start()
    for copy in copies:
        copy.wait()


def activate(core, conv_input, sib, own_halo, sib_halo, own_weights, sib_weights):
    x, bc = (GROUPS, TOK, XW), (GROUPS, TOK, LW)
    return pl.pallas_call(
        act_kernel,
        in_specs=in_smem(1) + in_hbm(2) + in_vmem(4),
        out_specs=in_hbm(2) + in_vmem(1),
        out_shape=[hbm(x), hbm(bc), DONE],
        scratch_shapes=[
            pltpu.VMEM((TOK, GROUPS, GW), BF16),
            pltpu.VMEM((ENDS, GROUPS, GW), BF16),
            pltpu.VMEM((GW // LANE, TOK * GROUPS, LANE), F32),
            pltpu.VMEM(x, BF16),
            pltpu.VMEM(bc, BF16),
            pltpu.SemaphoreType.DMA((2, GROUPS)),
            pltpu.SemaphoreType.DMA((2, GW // LW)),
        ],
        compiler_params=params(18),
        cost_estimate=pl.CostEstimate(flops=20_000_000, bytes_accessed=8_000_000, transcendentals=1_400_000),
        name="activate",
    )(core, from_hbm(conv_input), from_hbm(sib), own_halo, sib_halo, own_weights, sib_weights)


def scan_kernel(chips, in_ref, done_ref, out_hbm, out_ref, sems):
    each = CHUNKS // chips
    parts = 4
    size = CHUNKS // parts
    states = [jnp.zeros((64, LANE), F32) for _ in range(each)]
    stores = []
    for k in range(parts):
        for at in range(k * size, (k + 1) * size):
            i = at % each
            extra = in_ref[at, 64:ROWS].astype(F32)
            state = extra[3:4] * states[i]
            out_ref[at] = state.astype(BF16)
            states[i] = (extra[0:1] + extra[1:2] + extra[2:3]) * state + in_ref[at, 0:64].astype(F32)
        span = pl.ds(k * size, size)
        stores.append(pltpu.make_async_copy(out_ref.at[span], out_hbm.at[span], sems.at[k]))
        stores[-1].start()
    for store in stores:
        store.wait()


def scan(chips, pieces, done):
    return pl.pallas_call(
        functools.partial(scan_kernel, chips),
        in_specs=in_vmem(1) + [pl.BlockSpec(memory_space=pl.ANY)],
        out_specs=in_hbm(1)[0],
        out_shape=hbm((CHUNKS, 64, LANE)),
        scratch_shapes=[pltpu.VMEM((CHUNKS, 64, LANE), BF16), pltpu.SemaphoreType.DMA((4,))],
        compiler_params=params(4),
        name="scan",
    )(pieces, done)


def local_kernel(other, core_ref, len_ref, x_ref, bc_ref, tab_ref, before_ref, dts_ref, gate_ref, skip_ref, p_ref, q_ref, done_ref):
    core = core_ref[0]
    done_ref[...] = jnp.zeros_like(done_ref)
    group = (core + other) % 2 + 2 * pl.program_id(0)
    inner, after, since = (tab_ref[k] for k in range(3))
    since = since * jnp.where(core == 1, dts_ref[TOK : TOK + 1], 1.0)
    rise = jnp.where(core == 1, tab_ref[2, TOK // 2 - 1 : TOK // 2], 0.0)
    rise = jnp.broadcast_to(rise, (8, LANE))
    spread = lambda table, j: jnp.concatenate([widen(table, group * 16 + j * 4 + 2 * k) for k in range(2)], axis=1)
    b = bc_ref[0, :, :LANE]
    c = bc_ref[0, :, LANE:]
    scores = lax.dot_general(c, b, (((1,), (1,)), ((), ())), preferred_element_type=F32)
    causal = iota((TOK, TOK), 0) >= iota((TOK, TOK), 1)
    scores = jnp.where(causal, scores, 0.0).astype(BF16)
    live = iota((TOK, LW), 0) < len_ref[0] - head_place() * TOK
    for j in range(4):
        at = slice(j * LW, (j + 1) * LW)
        x = x_ref[0, :, at].astype(F32)
        scaled = (x * spread(inner, j)).astype(BF16)
        before = jnp.concatenate(
            [jnp.concatenate([before_ref[0, j, tile * 2], before_ref[0, j, tile * 2 + 1]], axis=0) for tile in range(2)],
            axis=1,
        )
        read = jnp.dot(scores, scaled, preferred_element_type=F32)
        read = read + spread(rise, j)[0:1] * jnp.dot(c, before, preferred_element_type=F32)
        y = spread(after, j) * read + skip_ref[:, at] * x
        half = gate_ref[:, at].astype(F32) * 0.5
        silu = half + half * jnp.tanh(half)
        p_ref[0, :, at] = jnp.where(live, y * silu, 0.0).astype(BF16)
        q_ref[0, :, at] = jnp.where(live, spread(since, j) * silu, 0.0).astype(BF16)


def local(other, core, seg_length, x, bc, tables, before, d_sib, gate_input, skip):
    group = lambda i, s: (s[0] + other) % 2 + 2 * i
    out = hbm((4, TOK, XW))
    out_spec = pl.BlockSpec((1, TOK, XW), lambda i, s: (i, 0, 0))
    return pl.pallas_call(
        functools.partial(local_kernel, other),
        grid_spec=pltpu.PrefetchScalarGridSpec(
            num_scalar_prefetch=1,
            grid=(4,),
            in_specs=[
                pl.BlockSpec(memory_space=pltpu.SMEM),
                pl.BlockSpec((1, TOK, XW), lambda i, s: (group(i, s), 0, 0)),
                pl.BlockSpec((1, TOK, LW), lambda i, s: (group(i, s), 0, 0)),
                pl.BlockSpec((3, TOK, LANE), lambda i, s: (0, 0, 0)),
                pl.BlockSpec((1, 4, 4, 64, LANE), lambda i, s: (i, 0, 0, 0, 0)),
                pl.BlockSpec((TOK + 8, LANE), lambda i, s: (0, 0)),
                pl.BlockSpec((TOK, XW), lambda i, s: (0, group(i, s))),
                pl.BlockSpec((1, XW), lambda i, s: (0, group(i, s))),
            ],
            out_specs=[out_spec, out_spec, pl.BlockSpec((8, LANE), lambda i, s: (0, 0))],
        ),
        out_shape=[out, out, DONE],
        compiler_params=params(),
        cost_estimate=pl.CostEstimate(flops=400_000_000, bytes_accessed=8_000_000, transcendentals=600_000),
        name="local",
    )(core, seg_length, from_hbm(x), from_hbm(bc), tables, from_hbm(before), d_sib, from_hbm(gate_input), skip)


def finish_kernel(other, core_ref, p_ref, q_ref, bc_ref, state_ref, gain_ref, *rest):
    first = (core_ref[0] + other) % 2
    copies = []

    def send(half, i, rows_ref, sems):
        group = (core_ref[0] + half) % 2 + 2 * i
        to = out_ref.at[:, pl.ds(pl.multiple_of(group * XW, XW), XW)]
        copies.append(pltpu.make_async_copy(rows_ref.at[i], to, sems.at[half, i]))
        copies[-1].start()

    if other:
        own_rows_ref, out_ref, rows_ref, sems = rest
        for i in range(4):
            send(0, i, own_rows_ref, sems)
    else:
        _, rows_ref, p_to, q_to, state_to, load_sems = rest
        loads = []
        for i in range(4):
            group = pl.ds(i * 16, 16)
            loads.append(pltpu.make_async_copy(state_ref.at[group], state_to.at[group], load_sems.at[0, i]))
            loads.append(pltpu.make_async_copy(p_ref.at[i], p_to.at[i], load_sems.at[1, i]))
            loads.append(pltpu.make_async_copy(q_ref.at[i], q_to.at[i], load_sems.at[2, i]))
        for load in loads:
            load.start()
        p_ref, q_ref, state_ref = p_to, q_to, state_to
    for i in range(4):
        if not other:
            for load in loads[3 * i : 3 * i + 6 if i % 2 == 0 else 3 * i]:
                load.wait()
        c = bc_ref[first + 2 * i, :, LANE:]
        gated = []
        for tile in range(0, 8, 2):
            state = jnp.concatenate(
                [
                    jnp.concatenate([state_ref[i * 16 + (tile + k) * 2], state_ref[i * 16 + (tile + k) * 2 + 1]], axis=0)
                    for k in range(2)
                ],
                axis=1,
            )
            at = slice(tile * LANE, (tile + 2) * LANE)
            read = jnp.dot(c, state, preferred_element_type=F32)
            gated.append(p_ref[i, :, at].astype(F32) + read * q_ref[i, :, at].astype(F32))
        total = sum(jnp.sum(v * v, axis=1, keepdims=True) for v in gated)
        scale = lax.rsqrt(total / XW + EPSILON)
        for j, v in enumerate(gated):
            at = slice(j * LW, (j + 1) * LW)
            rows_ref[i, :, at] = (v * scale * gain_ref[first + 2 * i, :, at]).astype(BF16)
        if other:
            send(1, i, rows_ref, sems)
    for copy in copies:
        copy.wait()


def finish(other, core, p, q, bc, states, gain, out):
    rows = pltpu.VMEM((4, TOK, XW), BF16)
    if other:
        operands = [core, p, q, bc, states, gain, out]
        in_specs = in_smem(1) + in_vmem(5) + [pl.BlockSpec(memory_space=pl.ANY)]
        out_shape = jax.ShapeDtypeStruct((TOK, GROUPS * XW), BF16)
        out_spec = pl.BlockSpec(memory_space=pl.ANY)
        scratch = [rows, pltpu.SemaphoreType.DMA((2, 4))]
    else:
        operands = [core, from_hbm(p), from_hbm(q), bc, from_hbm(states), gain, out]
        in_specs = in_smem(1) + in_hbm(2) + in_vmem(1) + in_hbm(1) + in_vmem(1) + [pl.BlockSpec(memory_space=pl.ANY)]
        out_shape = jax.ShapeDtypeStruct((4, TOK, XW), BF16)
        out_spec = in_vmem(1)[0]
        scratch = [rows, rows, pltpu.VMEM((CHUNKS, 64, LANE), BF16), pltpu.SemaphoreType.DMA((3, 4))]
    return pl.pallas_call(
        functools.partial(finish_kernel, other),
        in_specs=in_specs,
        out_specs=out_spec,
        scratch_shapes=scratch,
        out_shape=out_shape,
        compiler_params=params(),
        cost_estimate=pl.CostEstimate(flops=200_000_000, bytes_accessed=4_000_000, transcendentals=1000),
        name="finish",
    )(*operands)


def body(
    conv_input,
    gate_input,
    step_size,
    decay_log,
    conv_weight,
    conv_bias,
    skip_gain,
    norm_gain,
    seg_length,
    seg_first,
):
    segments = lax.axis_size("seq")
    in_segment = lax.axis_size("y") * lax.axis_size("core")
    chips = segments * in_segment // 2
    core = lax.axis_index("core").astype(jnp.int32).reshape(1)
    swap = [(0, 1), (1, 0)]

    sib = lax.ppermute(conv_input, "core", swap)
    tables, et_own, ends = start(seg_length, decay_log, step_size, conv_input)
    onward, tail = pack(ends, lax.ppermute(ends, "core", swap), conv_weight, conv_bias)
    packs = [
        lax.ppermute(tail if k > 1 else onward, CHIPS, [(c, (c + k) % chips) for c in range(chips)]) for k in range(1, 5)
    ]
    et_sib = lax.ppermute(et_own, "core", swap)

    pieces, before_own, weights, halo = chip_states(
        core, seg_first, conv_input, sib, [tail] + packs, et_sib, et_own
    )
    pieces = lax.all_to_all(pieces, CHIPS, 0, 0, tiled=True)
    before_oth = lax.ppermute(before_own, "core", swap[:1])
    halo_sib = lax.ppermute(halo, "core", swap)
    weights_sib = lax.ppermute(weights, "core", swap)
    x, bc, done = activate(core, conv_input, sib, halo, halo_sib, weights, weights_sib)

    skip = jnp.repeat(skip_gain, HEAD_DIM)[None]
    p_own, q_own, done_own = local(0, core, seg_length, x, bc, tables, before_own, et_sib, gate_input, skip)
    p_oth, q_oth, done_oth = local(1, core, seg_length, x, bc, tables, before_oth, et_sib, gate_input, skip)
    states = lax.all_to_all(scan(chips, pieces, done), CHIPS, 0, 0, tiled=True)
    states, done = lax.optimization_barrier((states, done_own + done_oth))
    states_oth = lax.ppermute(states, "core", swap)
    gain = norm_gain.reshape(GROUPS, 1, XW)
    out = finish(0, core, p_own, q_own, bc, states, gain, done)
    return finish(1, core, p_oth, q_oth, bc, states_oth, gain, out)


def solution(mesh):
    segments, in_segment = mesh.devices.shape
    fine = Mesh(mesh.devices.reshape(segments, in_segment // 2, 2), AXES)
    tokens = P(AXES, None)
    return jax.shard_map(
        body,
        mesh=fine,
        in_specs=(
            P(AXES, None, None),
            tokens,
            tokens,
            tokens,
            P(None, ("y", "core"), None),
            P(("y", "core"), None),
            P(),
            P(),
            P("seq"),
            P("seq"),
        ),
        out_specs=tokens,
        check_vma=False,
    )
```

```python
import functools

import jax
import jax.numpy as jnp
from jax import lax
from jax.experimental import pallas as pl
from jax.experimental.pallas import tpu as pltpu
from jax.sharding import Mesh, PartitionSpec as P

HEAD_DIM = 64
KERNEL = 4
EPSILON = 1e-05
TOK = 128
GROUPS = 8
XW = 1024
GW = 1280
LANE = 128
LW = 256
CHUNKS = 64
ENDS = KERNEL - 1
PACK = 24
ROWS = 72
AXES = ("seq", "y", "core")
CHIPS = ("seq", "y")
F32 = jnp.float32
BF16 = jnp.bfloat16
DONE = jax.ShapeDtypeStruct((8, LANE), F32)


def iota(shape, dim):
    return lax.broadcasted_iota(jnp.int32, shape, dim)


def split3(v):
    hi = v.astype(BF16).astype(F32)
    mid = (v - hi).astype(BF16).astype(F32)
    return hi, mid, v - hi - mid


def widen(table, first):
    lane = iota(table.shape, 1) // HEAD_DIM + first
    return jnp.take_along_axis(table, lane, axis=1, mode="promise_in_bounds")


def head_place():
    return lax.axis_index("y") * 2 + lax.axis_index("core")


def in_vmem(count):
    return [pl.BlockSpec(memory_space=pltpu.VMEM)] * count


def in_hbm(count):
    return [pl.BlockSpec(memory_space=pltpu.HBM)] * count


def in_smem(count):
    return [pl.BlockSpec(memory_space=pltpu.SMEM)] * count


def hbm(shape):
    return pltpu.HBM(shape, BF16)


def from_hbm(value):
    return pltpu.with_memory_space_constraint(value, pltpu.HBM)


def params(mib=16):
    return pltpu.CompilerParams(vmem_limit_bytes=mib * 1024 * 1024)


def start_kernel(
    len_ref, decay_hbm, step_hbm, conv_hbm, tab_ref, et_ref, ends_ref, decay_ref, step_ref, rows_ref, sems
):
    first_row = len_ref[0] - head_place() * TOK
    copies = [
        pltpu.make_async_copy(decay_hbm, decay_ref, sems.at[0]),
        pltpu.make_async_copy(step_hbm, step_ref, sems.at[1]),
    ]
    for k in range(ENDS):
        row = jnp.clip(first_row - ENDS + k, 0, TOK - 1)
        copies.append(pltpu.make_async_copy(conv_hbm.at[pl.ds(row, 1)], rows_ref.at[pl.ds(k, 1)], sems.at[2 + k]))
    copies.append(pltpu.make_async_copy(conv_hbm.at[pl.ds(TOK - ENDS, ENDS)], rows_ref.at[pl.ds(ENDS, ENDS)], sems.at[2 + ENDS]))
    for copy in copies:
        copy.start()
    for copy in copies:
        copy.wait()
    for k in range(ENDS):
        row = first_row - ENDS + k
        inside = jnp.where((row >= 0) & (row < TOK), 1.0, 0.0)
        ends_ref[k] = (rows_ref[k].astype(F32) * inside).astype(BF16)
        ends_ref[ENDS + k] = rows_ref[ENDS + k]
    live = iota((TOK, LANE), 0) < first_row
    log_rate = jnp.where(live, decay_ref[...].astype(F32), 0.0)
    gain = jnp.where(live, step_ref[...].astype(F32), 0.0)
    upto = jnp.where(iota((TOK, TOK), 0) >= iota((TOK, TOK), 1), 1.0, 0.0).astype(BF16)
    running = jnp.dot(upto, log_rate.astype(BF16), preferred_element_type=F32)
    middle = running[TOK // 2 - 1 : TOK // 2]
    total = running[TOK - 1 : TOK]
    tab_ref[0] = jnp.exp(middle - running) * gain
    tab_ref[1] = jnp.exp(running - middle)
    tab_ref[2] = jnp.exp(running)
    et_ref[0:TOK] = jnp.exp(total - running) * gain
    et_ref[TOK:] = jnp.broadcast_to(jnp.exp(total), (8, LANE))


def start(seg_length, decay_log, step_size, conv_input):
    return pl.pallas_call(
        start_kernel,
        in_specs=in_smem(1) + in_hbm(3),
        out_specs=in_vmem(3),
        out_shape=[
            jax.ShapeDtypeStruct((3, TOK, LANE), F32),
            jax.ShapeDtypeStruct((TOK + 8, LANE), F32),
            jax.ShapeDtypeStruct((2 * ENDS, GROUPS, GW), BF16),
        ],
        scratch_shapes=[
            pltpu.VMEM((TOK, LANE), BF16),
            pltpu.VMEM((TOK, LANE), BF16),
            pltpu.VMEM((2 * ENDS, GROUPS, GW), BF16),
            pltpu.SemaphoreType.DMA((3 + ENDS,)),
        ],
        compiler_params=params(),
        name="start",
    )(seg_length, from_hbm(decay_log), from_hbm(step_size), from_hbm(conv_input))


def weight_row(m):
    return m // 4 * 8 + m % 4 * 2 + 1


def pack_kernel(own_ref, sib_ref, weight_ref, bias_ref, on_ref, tail_ref):
    place, core = lax.axis_index("y"), lax.axis_index("core")
    row = iota((GROUPS, LANE), 0)
    even = row % 2 == 0
    for tile in range(GW // LANE):
        at = slice(tile * LANE, (tile + 1) * LANE)
        rows = [weight_ref[k, :, at] for k in range(KERNEL)] + [bias_ref[:, at]]
        rows = rows + [v - v.astype(BF16).astype(F32) for v in rows]
        for k in range(ENDS):
            fill = jnp.zeros((GROUPS, LANE), F32)
            for m in range(4 * k, min(4 * k + 4, len(rows))):
                fill = jnp.where(row == weight_row(m % 4), rows[m], fill)
            tail = own_ref[k, :, at].astype(F32) + sib_ref[k, :, at].astype(F32)
            last = jnp.where(core == 0, sib_ref[ENDS + k, :, at].astype(F32), own_ref[ENDS + k, :, at].astype(F32))
            onward = jnp.where(place == lax.axis_size("y") - 1, tail, last)
            for value, ref in ((onward, on_ref), (tail, tail_ref)):
                value = jnp.where(core == 0, value, pltpu.roll(value, GROUPS - 1, 0))
                ref[k * 8 : k * 8 + 8, at] = jnp.where(even, value, fill).astype(BF16)


def pack(own, sib, weight, bias):
    shape = jax.ShapeDtypeStruct((PACK, GW), BF16)
    return pl.pallas_call(
        pack_kernel,
        in_specs=in_vmem(4),
        out_specs=in_vmem(2),
        out_shape=[shape, shape],
        compiler_params=params(),
        name="pack",
    )(own, sib, weight, bias)


PART = 16


def convolve(window, taps):
    half = taps[KERNEL][None] + taps[0][None] * window[0:PART]
    for k in range(1, KERNEL):
        half = half + taps[k][None] * window[k : k + PART]
    half = half + half * jnp.tanh(half)
    return half.reshape(PART * GROUPS, LANE)


def load_lanes(refs, to_refs, sems):
    loads = []
    for i in range(GW // LW):
        at = pl.ds(i * LW, LW)
        loads.append(
            [pltpu.make_async_copy(ref.at[:, :, at], to.at[:, :, at], sems.at[k, i]) for k, (ref, to) in enumerate(zip(refs, to_refs))]
        )
        for load in loads[-1]:
            load.start()
    return loads


def states_kernel(
    core_ref, first_ref, own_hbm, sib_hbm, p0, p1, p2, p3, p4, ets_ref, eto_ref, out_hbm, before_hbm, w_ref, halo_ref,
    own_ref, sib_ref, packed_ref, act_ref, pieces_ref, before_ref, sems, load_sems,
):
    core = core_ref[0]
    place = lax.axis_index("y")
    loads = load_lanes((own_hbm, sib_hbm), (own_ref, sib_ref), load_sems)
    keep = jnp.where(place == 0, 1 - first_ref[0], 1).astype(F32)
    low = iota((1, GROUPS, LANE), 1) % 2 == 0
    kept = iota((1, GROUPS, LANE), 1) % 2 == core
    swap = lambda v: pltpu.roll(v, 1 + 6 * core, v.ndim - 2)
    for tile in range(GW // LANE):
        at = slice(tile * LANE, (tile + 1) * LANE)
        packs = [ref[:, at].astype(F32) for ref in (p0, p1, p2, p3)]
        for k, pack in enumerate(packs):
            source = lax.rem(place - k + 4, 4)
            for double in range(2):
                packed_ref[pl.ds(pl.multiple_of((source * 2 + double) * PACK, 8), PACK), :] = pack
        halves = [packed_ref[pl.ds(weight_row(m), GROUPS, stride=PACK), :] * 0.5 for m in range(2 * KERNEL + 2)]
        taps = [halves[k] + halves[k + KERNEL + 1] for k in range(KERNEL + 1)]
        for k, v in enumerate(taps):
            w_ref[k, :, at] = v
        before = packs[1] + jnp.where(place == 0, packs[2] + packs[3] + p4[:, at].astype(F32), 0.0)
        before = jnp.where(low, before.reshape(ENDS, GROUPS, LANE) * keep, 0.0)
        halo_ref[:, :, at] = before.astype(BF16)
        if tile % 2 == 0:
            for load in loads[tile // 2]:
                load.wait()

        def merged(rows, at=at):
            return jnp.where(kept, own_ref[rows, :, at].astype(F32), swap(sib_ref[rows, :, at].astype(F32)))

        def tokens(i, carry, tile=tile, taps=taps, merged=merged):
            window = merged(pl.ds(i * PART - (KERNEL - 1), PART + KERNEL - 1))
            act_ref[tile, pl.ds(pl.multiple_of(i * PART * GROUPS, PART * GROUPS), PART * GROUPS), :] = convolve(window, taps)
            return carry

        last = slice(TOK - (KERNEL - 1), TOK)
        between = jnp.where(core == 0, swap(own_ref[last, :, at].astype(F32)), sib_ref[last, :, at].astype(F32))
        window = jnp.concatenate([jnp.where(low, before, between), merged(slice(0, PART))], axis=0)
        act_ref[tile, 0 : PART * GROUPS, :] = convolve(window, taps)
        lax.fori_loop(1, TOK // PART, tokens, 0, unroll=True)

    own, sib = eto_ref[...], ets_ref[...]
    decay = [jnp.where(core == 0, own, sib), jnp.where(core == 0, sib, own)]
    d_last = decay[1][TOK:]
    d_chip = decay[0][TOK:] * d_last
    row = iota((8, LANE), 0)
    copies = []
    for i in range(4):
        of_group = lambda half, tile: act_ref[tile, pl.ds(2 * i + half, TOK, stride=GROUPS), :]
        b_t = [of_group(half, 8).T.astype(BF16) for half in range(2)]
        for j in range(4):
            states = []
            for half in range(2):
                carried = [
                    (of_group(half, tile) * widen(decay[half][:TOK], core * 16 + i * 32 + tile * 2)).astype(BF16)
                    for tile in (2 * j, 2 * j + 1)
                ]
                states.append(jnp.dot(b_t[half], jnp.concatenate(carried, axis=1), preferred_element_type=F32))
            for tile in range(2):
                lanes = slice(tile * LANE, (tile + 1) * LANE)
                head = core * 16 + i * 32 + (2 * j + tile) * 2
                hi, mid, bottom = split3(widen(d_chip, head))
                extra = jnp.where(row == 0, hi, jnp.where(row == 1, mid, jnp.where(row == 2, bottom, keep)))
                first = states[0][:, lanes]
                both = (first * widen(d_last, head)[0:1] + states[1][:, lanes]).astype(BF16)
                first = first.astype(BF16)
                for rows in range(2):
                    piece = (i * 8 + 2 * j + tile) * 2 + rows
                    before_ref[i, j, tile * 2 + rows] = first[rows * 64 : rows * 64 + 64]
                    pieces_ref[piece, 0:64] = both[rows * 64 : rows * 64 + 64]
                    pieces_ref[piece, 64:ROWS] = extra.astype(BF16)
        group = pl.ds(i * 16, 16)
        copies.append(pltpu.make_async_copy(pieces_ref.at[group], out_hbm.at[group], sems.at[0, i]))
        copies.append(pltpu.make_async_copy(before_ref.at[i], before_hbm.at[i], sems.at[1, i]))
        copies[-2].start()
        copies[-1].start()
    for copy in copies:
        copy.wait()


def chip_states(core, seg_first, own, sib, packs, et_sib, et_own):
    pieces = (CHUNKS, ROWS, LANE)
    before = (4, 4, 4, 64, LANE)
    return pl.pallas_call(
        states_kernel,
        in_specs=in_smem(2) + in_hbm(2) + in_vmem(7),
        out_specs=in_hbm(2) + in_vmem(2),
        out_shape=[
            hbm(pieces),
            hbm(before),
            jax.ShapeDtypeStruct((KERNEL + 1, GROUPS, GW), F32),
            jax.ShapeDtypeStruct((ENDS, GROUPS, GW), BF16),
        ],
        scratch_shapes=[
            pltpu.VMEM((TOK, GROUPS, GW), BF16),
            pltpu.VMEM((TOK, GROUPS, GW), BF16),
            pltpu.VMEM((GROUPS * PACK, LANE), F32),
            pltpu.VMEM((GW // LANE, TOK * GROUPS, LANE), F32),
            pltpu.VMEM(pieces, BF16),
            pltpu.VMEM(before, BF16),
            pltpu.SemaphoreType.DMA((2, 4)),
            pltpu.SemaphoreType.DMA((2, GW // LW)),
        ],
        compiler_params=params(20),
        name="chip_states",
    )(core, seg_first, from_hbm(own), from_hbm(sib), *packs, et_sib, et_own)


def act_kernel(
    core_ref, conv_hbm, sib_hbm, own_halo_ref, sib_halo_ref, own_w_ref, sib_w_ref, x_hbm, bc_hbm, done_ref,
    conv_ref, last_ref, act_ref, x_ref, bc_ref, sems, load_sems,
):
    done_ref[...] = jnp.zeros_like(done_ref)
    core = core_ref[0]
    last = pltpu.make_async_copy(sib_hbm.at[pl.ds(TOK - ENDS, ENDS)], last_ref, load_sems.at[1, 0])
    last.start()
    loads = load_lanes((conv_hbm,), (conv_ref,), load_sems)
    last.wait()
    low = iota((1, GROUPS, LANE), 1) % 2 == 0
    kept = iota((GROUPS, LANE), 0) % 2 == core
    for tile in range(GW // LANE):
        at = slice(tile * LANE, (tile + 1) * LANE)
        taps = [jnp.where(kept, own_w_ref[k, :, at], sib_w_ref[k, :, at]) for k in range(KERNEL + 1)]
        if tile % 2 == 0:
            loads[tile // 2][0].wait()

        def tokens(i, carry, at=at, tile=tile, taps=taps):
            window = conv_ref[pl.ds(i * PART - (KERNEL - 1), PART + KERNEL - 1), :, at].astype(F32)
            act_ref[tile, pl.ds(pl.multiple_of(i * PART * GROUPS, PART * GROUPS), PART * GROUPS), :] = convolve(window, taps)
            return carry

        halo = pltpu.roll(sib_halo_ref[:, :, at].astype(F32), 1, 1)
        halo = jnp.where(low, own_halo_ref[:, :, at].astype(F32), halo)
        halo = jnp.where(core == 0, halo, last_ref[:, :, at].astype(F32))
        window = jnp.concatenate([halo, conv_ref[0:PART, :, at].astype(F32)], axis=0)
        act_ref[tile, 0 : PART * GROUPS, :] = convolve(window, taps)
        lax.fori_loop(1, TOK // PART, tokens, 0, unroll=True)
    copies = []
    for g in range(GROUPS):
        for tile in range(GW // LANE):
            values = act_ref[tile, pl.ds(g, TOK, stride=GROUPS), :].astype(BF16)
            if tile < XW // LANE:
                x_ref[g, :, tile * LANE : (tile + 1) * LANE] = values
            else:
                bc_ref[g, :, tile * LANE - XW : (tile + 1) * LANE - XW] = values
        copies.append(pltpu.make_async_copy(x_ref.at[g], x_hbm.at[g], sems.at[0, g]))
        copies.append(pltpu.make_async_copy(bc_ref.at[g], bc_hbm.at[g], sems.at[1, g]))
        copies[-2].start()
        copies[-1].start()
    for copy in copies:
        copy.wait()


def activate(core, conv_input, sib, own_halo, sib_halo, own_weights, sib_weights):
    x, bc = (GROUPS, TOK, XW), (GROUPS, TOK, LW)
    return pl.pallas_call(
        act_kernel,
        in_specs=in_smem(1) + in_hbm(2) + in_vmem(4),
        out_specs=in_hbm(2) + in_vmem(1),
        out_shape=[hbm(x), hbm(bc), DONE],
        scratch_shapes=[
            pltpu.VMEM((TOK, GROUPS, GW), BF16),
            pltpu.VMEM((ENDS, GROUPS, GW), BF16),
            pltpu.VMEM((GW // LANE, TOK * GROUPS, LANE), F32),
            pltpu.VMEM(x, BF16),
            pltpu.VMEM(bc, BF16),
            pltpu.SemaphoreType.DMA((2, GROUPS)),
            pltpu.SemaphoreType.DMA((2, GW // LW)),
        ],
        compiler_params=params(18),
        cost_estimate=pl.CostEstimate(flops=20_000_000, bytes_accessed=8_000_000, transcendentals=1_400_000),
        name="activate",
    )(core, from_hbm(conv_input), from_hbm(sib), own_halo, sib_halo, own_weights, sib_weights)


def scan_kernel(chips, in_ref, done_ref, out_hbm, out_ref, sems):
    each = CHUNKS // chips
    parts = 8
    size = CHUNKS // parts
    states = [jnp.zeros((64, LANE), F32) for _ in range(each)]
    stores = []
    for k in range(parts):
        for at in range(k * size, (k + 1) * size):
            i = at % each
            extra = in_ref[at, 64:ROWS].astype(F32)
            state = extra[3:4] * states[i]
            out_ref[at] = state.astype(BF16)
            states[i] = (extra[0:1] + extra[1:2] + extra[2:3]) * state + in_ref[at, 0:64].astype(F32)
        span = pl.ds(k * size, size)
        stores.append(pltpu.make_async_copy(out_ref.at[span], out_hbm.at[span], sems.at[k]))
        stores[-1].start()
    for store in stores:
        store.wait()


def scan(chips, pieces, done):
    return pl.pallas_call(
        functools.partial(scan_kernel, chips),
        in_specs=in_vmem(1) + [pl.BlockSpec(memory_space=pl.ANY)],
        out_specs=in_hbm(1)[0],
        out_shape=hbm((CHUNKS, 64, LANE)),
        scratch_shapes=[pltpu.VMEM((CHUNKS, 64, LANE), BF16), pltpu.SemaphoreType.DMA((8,))],
        compiler_params=params(4),
        name="scan",
    )(pieces, done)


def local_kernel(other, core_ref, len_ref, x_ref, bc_ref, tab_ref, before_ref, dts_ref, gate_ref, skip_ref, p_ref, q_ref, done_ref):
    core = core_ref[0]
    done_ref[...] = jnp.zeros_like(done_ref)
    group = (core + other) % 2 + 2 * pl.program_id(0)
    inner, after, since = (tab_ref[k] for k in range(3))
    since = since * jnp.where(core == 1, dts_ref[TOK : TOK + 1], 1.0)
    rise = jnp.where(core == 1, tab_ref[2, TOK // 2 - 1 : TOK // 2], 0.0)
    rise = jnp.broadcast_to(rise, (8, LANE))
    spread = lambda table, j: jnp.concatenate([widen(table, group * 16 + j * 4 + 2 * k) for k in range(2)], axis=1)
    b = bc_ref[0, :, :LANE]
    c = bc_ref[0, :, LANE:]
    scores = lax.dot_general(c, b, (((1,), (1,)), ((), ())), preferred_element_type=F32)
    causal = iota((TOK, TOK), 0) >= iota((TOK, TOK), 1)
    scores = jnp.where(causal, scores, 0.0).astype(BF16)
    live = iota((TOK, LW), 0) < len_ref[0] - head_place() * TOK
    for j in range(4):
        at = slice(j * LW, (j + 1) * LW)
        x = x_ref[0, :, at].astype(F32)
        scaled = (x * spread(inner, j)).astype(BF16)
        before = jnp.concatenate(
            [jnp.concatenate([before_ref[0, j, tile * 2], before_ref[0, j, tile * 2 + 1]], axis=0) for tile in range(2)],
            axis=1,
        )
        read = jnp.dot(scores, scaled, preferred_element_type=F32)
        read = read + spread(rise, j)[0:1] * jnp.dot(c, before, preferred_element_type=F32)
        y = spread(after, j) * read + skip_ref[:, at] * x
        half = gate_ref[:, at].astype(F32) * 0.5
        silu = half + half * jnp.tanh(half)
        p_ref[0, :, at] = jnp.where(live, y * silu, 0.0).astype(BF16)
        q_ref[0, :, at] = jnp.where(live, spread(since, j) * silu, 0.0).astype(BF16)


def local(other, core, seg_length, x, bc, tables, before, d_sib, gate_input, skip):
    group = lambda i, s: (s[0] + other) % 2 + 2 * i
    out = hbm((4, TOK, XW))
    out_spec = pl.BlockSpec((1, TOK, XW), lambda i, s: (i, 0, 0))
    return pl.pallas_call(
        functools.partial(local_kernel, other),
        grid_spec=pltpu.PrefetchScalarGridSpec(
            num_scalar_prefetch=1,
            grid=(4,),
            in_specs=[
                pl.BlockSpec(memory_space=pltpu.SMEM),
                pl.BlockSpec((1, TOK, XW), lambda i, s: (group(i, s), 0, 0)),
                pl.BlockSpec((1, TOK, LW), lambda i, s: (group(i, s), 0, 0)),
                pl.BlockSpec((3, TOK, LANE), lambda i, s: (0, 0, 0)),
                pl.BlockSpec((1, 4, 4, 64, LANE), lambda i, s: (i, 0, 0, 0, 0)),
                pl.BlockSpec((TOK + 8, LANE), lambda i, s: (0, 0)),
                pl.BlockSpec((TOK, XW), lambda i, s: (0, group(i, s))),
                pl.BlockSpec((1, XW), lambda i, s: (0, group(i, s))),
            ],
            out_specs=[out_spec, out_spec, pl.BlockSpec((8, LANE), lambda i, s: (0, 0))],
        ),
        out_shape=[out, out, DONE],
        compiler_params=params(),
        cost_estimate=pl.CostEstimate(flops=400_000_000, bytes_accessed=8_000_000, transcendentals=600_000),
        name="local",
    )(core, seg_length, from_hbm(x), from_hbm(bc), tables, from_hbm(before), d_sib, from_hbm(gate_input), skip)


def finish_kernel(other, core_ref, p_ref, q_ref, bc_ref, state_ref, gain_ref, *rest):
    first = (core_ref[0] + other) % 2
    copies = []

    def send(half, i, rows_ref, sems):
        group = (core_ref[0] + half) % 2 + 2 * i
        to = out_ref.at[:, pl.ds(pl.multiple_of(group * XW, XW), XW)]
        copies.append(pltpu.make_async_copy(rows_ref.at[i], to, sems.at[half, i]))
        copies[-1].start()

    if other:
        own_rows_ref, out_ref, rows_ref, sems = rest
        for i in range(4):
            send(0, i, own_rows_ref, sems)
    else:
        _, rows_ref, p_to, q_to, state_to, load_sems = rest
        loads = []
        for i in range(4):
            group = pl.ds(i * 16, 16)
            loads.append(pltpu.make_async_copy(state_ref.at[group], state_to.at[group], load_sems.at[0, i]))
            loads.append(pltpu.make_async_copy(p_ref.at[i], p_to.at[i], load_sems.at[1, i]))
            loads.append(pltpu.make_async_copy(q_ref.at[i], q_to.at[i], load_sems.at[2, i]))
        for load in loads:
            load.start()
        p_ref, q_ref, state_ref = p_to, q_to, state_to
    for i in range(4):
        if not other:
            for load in loads[3 * i : 3 * i + 6 if i % 2 == 0 else 3 * i]:
                load.wait()
        c = bc_ref[first + 2 * i, :, LANE:]
        gated = []
        for tile in range(0, 8, 2):
            state = jnp.concatenate(
                [
                    jnp.concatenate([state_ref[i * 16 + (tile + k) * 2], state_ref[i * 16 + (tile + k) * 2 + 1]], axis=0)
                    for k in range(2)
                ],
                axis=1,
            )
            at = slice(tile * LANE, (tile + 2) * LANE)
            read = jnp.dot(c, state, preferred_element_type=F32)
            gated.append(p_ref[i, :, at].astype(F32) + read * q_ref[i, :, at].astype(F32))
        total = sum(jnp.sum(v * v, axis=1, keepdims=True) for v in gated)
        scale = lax.rsqrt(total / XW + EPSILON)
        for j, v in enumerate(gated):
            at = slice(j * LW, (j + 1) * LW)
            rows_ref[i, :, at] = (v * scale * gain_ref[first + 2 * i, :, at]).astype(BF16)
        if other:
            send(1, i, rows_ref, sems)
    for copy in copies:
        copy.wait()


def finish(other, core, p, q, bc, states, gain, out):
    rows = pltpu.VMEM((4, TOK, XW), BF16)
    if other:
        operands = [core, p, q, bc, states, gain, out]
        in_specs = in_smem(1) + in_vmem(5) + [pl.BlockSpec(memory_space=pl.ANY)]
        out_shape = jax.ShapeDtypeStruct((TOK, GROUPS * XW), BF16)
        out_spec = pl.BlockSpec(memory_space=pl.ANY)
        scratch = [rows, pltpu.SemaphoreType.DMA((2, 4))]
    else:
        operands = [core, from_hbm(p), from_hbm(q), bc, from_hbm(states), gain, out]
        in_specs = in_smem(1) + in_hbm(2) + in_vmem(1) + in_hbm(1) + in_vmem(1) + [pl.BlockSpec(memory_space=pl.ANY)]
        out_shape = jax.ShapeDtypeStruct((4, TOK, XW), BF16)
        out_spec = in_vmem(1)[0]
        scratch = [rows, rows, pltpu.VMEM((CHUNKS, 64, LANE), BF16), pltpu.SemaphoreType.DMA((3, 4))]
    return pl.pallas_call(
        functools.partial(finish_kernel, other),
        in_specs=in_specs,
        out_specs=out_spec,
        scratch_shapes=scratch,
        out_shape=out_shape,
        compiler_params=params(),
        cost_estimate=pl.CostEstimate(flops=200_000_000, bytes_accessed=4_000_000, transcendentals=1000),
        name="finish",
    )(*operands)


def body(
    conv_input,
    gate_input,
    step_size,
    decay_log,
    conv_weight,
    conv_bias,
    skip_gain,
    norm_gain,
    seg_length,
    seg_first,
):
    segments = lax.axis_size("seq")
    in_segment = lax.axis_size("y") * lax.axis_size("core")
    chips = segments * in_segment // 2
    core = lax.axis_index("core").astype(jnp.int32).reshape(1)
    swap = [(0, 1), (1, 0)]

    sib = lax.ppermute(conv_input, "core", swap)
    tables, et_own, ends = start(seg_length, decay_log, step_size, conv_input)
    onward, tail = pack(ends, lax.ppermute(ends, "core", swap), conv_weight, conv_bias)
    packs = [
        lax.ppermute(tail if k > 1 else onward, CHIPS, [(c, (c + k) % chips) for c in range(chips)]) for k in range(1, 5)
    ]
    et_sib = lax.ppermute(et_own, "core", swap)

    pieces, before_own, weights, halo = chip_states(
        core, seg_first, conv_input, sib, [tail] + packs, et_sib, et_own
    )
    pieces = lax.all_to_all(pieces, CHIPS, 0, 0, tiled=True)
    before_oth = lax.ppermute(before_own, "core", swap[:1])
    halo_sib = lax.ppermute(halo, "core", swap)
    weights_sib = lax.ppermute(weights, "core", swap)
    x, bc, done = activate(core, conv_input, sib, halo, halo_sib, weights, weights_sib)

    skip = jnp.repeat(skip_gain, HEAD_DIM)[None]
    p_own, q_own, done_own = local(0, core, seg_length, x, bc, tables, before_own, et_sib, gate_input, skip)
    p_oth, q_oth, done_oth = local(1, core, seg_length, x, bc, tables, before_oth, et_sib, gate_input, skip)
    states = lax.all_to_all(scan(chips, pieces, done), CHIPS, 0, 0, tiled=True)
    states, done = lax.optimization_barrier((states, done_own + done_oth))
    states_oth = lax.ppermute(states, "core", swap)
    gain = norm_gain.reshape(GROUPS, 1, XW)
    out = finish(0, core, p_own, q_own, bc, states, gain, done)
    return finish(1, core, p_oth, q_oth, bc, states_oth, gain, out)


def solution(mesh):
    segments, in_segment = mesh.devices.shape
    fine = Mesh(mesh.devices.reshape(segments, in_segment // 2, 2), AXES)
    tokens = P(AXES, None)
    return jax.shard_map(
        body,
        mesh=fine,
        in_specs=(
            P(AXES, None, None),
            tokens,
            tokens,
            tokens,
            P(None, ("y", "core"), None),
            P(("y", "core"), None),
            P(),
            P(),
            P("seq"),
            P("seq"),
        ),
        out_specs=tokens,
        check_vma=False,
    )
```
